128 devices in a mesh: dp: 16 (over y, z_hi, core), ctx: 8 (over x, z_lo).
Axes of the slice: x: 4, y: 4, z: 4 (z_hi: 2, z_lo: 2; z = z_hi * 2 + z_lo), core: 2. Of those that a mesh axis runs over, the one named last changes fastest.
Arguments:
- hidden_in: bfloat16 [16, 1024, 768], P('dp', 'ctx'), may hold values from -6 to 6
- out_grad: bfloat16 [16, 1024, 768], P('dp', 'ctx'), may hold values from -6 to 6
- sequence_group: int32 [48], replicated, may hold values from 0 to 15, as said below
- sequence_start: int32 [48], replicated, may hold values from 0 to 992
- sequence_length: int32 [48], replicated, may hold values from 1 to 991
- norm_gain: bfloat16 [2, 2, 768], P(None, None, ('dp', 'ctx')), may hold values from 0.5 to 1.5
- norm_bias: bfloat16 [2, 2, 768], P(None, None, ('dp', 'ctx')), may hold values from -1.5 to 1.5
- input_weight: bfloat16 [2, 768, 2304], P(None, ('dp', 'ctx')), may hold values from -0.21875 to 0.21875
- input_bias: bfloat16 [2, 2, 768], P(None, None, ('dp', 'ctx')), may hold values from -1.5 to 1.5
- output_weight: bfloat16 [2, 768, 768], P(None, ('dp', 'ctx')), may hold values from -2.5 to 2.5
- branch_bias: bfloat16 [2, 2, 768], P(None, None, ('dp', 'ctx')), may hold values from -1.5 to 1.5
- up_weight: bfloat16 [2, 768, 3072], P(None, ('dp', 'ctx')), may hold values from -0.21875 to 0.21875
- up_bias: bfloat16 [2, 3072], P(None, ('dp', 'ctx')), may hold values from -1.5 to 1.5
- down_weight: bfloat16 [2, 3072, 768], P(None, ('dp', 'ctx')), may hold values from -0.109375 to 0.109375
Outputs:
- hidden_out: bfloat16 [16, 1024, 768], P('dp', 'ctx')
- grad_in: float32 [16, 1024, 768], P('dp', 'ctx')
- grad_norm_gain: float32 [2, 2, 768], P(None, None, ('dp', 'ctx'))
- grad_norm_bias: float32 [2, 2, 768], P(None, None, ('dp', 'ctx'))
- grad_input_weight: float32 [2, 768, 2304], P(None, ('dp', 'ctx'))
- grad_input_bias: float32 [2, 2, 768], P(None, None, ('dp', 'ctx'))
- grad_output_weight: float32 [2, 768, 768], P(None, ('dp', 'ctx'))
- grad_branch_bias: float32 [2, 2, 768], P(None, None, ('dp', 'ctx'))
- grad_up_weight: float32 [2, 768, 3072], P(None, ('dp', 'ctx'))
- grad_up_bias: float32 [2, 3072], P(None, ('dp', 'ctx'))
- grad_down_weight: float32 [2, 3072, 768], P(None, ('dp', 'ctx'))
The draws below stay inside these ranges and needn't reach their ends.
Inputs may be any that keep to these rules, and one draw needn't show every extreme that they name: `sequence_group`: each group holds three sequences laid end to end from its first token slot; the slots after them are padding.
All inputs are finite; a program needn't handle non-finite values.
Results may differ from the reference program's by a relative error of at most 0.014.
Values may be sent and summed in bfloat16 or wider, within the bound.
No kernel may reach another device: no remote copies, remote signals or barrier semaphores. Data moves between devices by JAX's collectives and lax.ppermute only.
A program may use at most 256 MiB of HBM per device.

```python
from functools import partial
import jax
import jax.numpy as jnp
from jax import lax

D = 768
HEADS = 12
HEAD_DIM = 64
FF = 3072
LAYERS = 2
TOK_DEV = 128
GROUPS = 16
GROUP_TOK = 1024


def sequence_table(key):
    quarter = TOK_DEV // 4
    first_key, second_key, third_key, fourth_key, fifth_key = jax.random.split(key, 5)
    head_end = jax.random.randint(first_key, (GROUPS,), 1, quarter + 1)
    long_end = jax.random.randint(second_key, (GROUPS,), GROUP_TOK - 2 * quarter, GROUP_TOK - quarter + 1)
    chosen = jnp.arange(GROUPS) == jax.random.randint(third_key, (), 0, GROUPS)
    head_end = jnp.where(chosen, 1, head_end)
    long_end = jnp.where(chosen, GROUP_TOK - quarter, long_end)
    tail_end = long_end + 1 + jax.random.randint(fourth_key, (GROUPS,), 0, 1048576) % (GROUP_TOK - long_end)
    starts = jnp.stack([jnp.zeros_like(head_end), head_end, long_end], axis=1).reshape(-1)
    end_points = jnp.stack([head_end, long_end, tail_end], axis=1).reshape(-1)
    owners = jnp.repeat(jnp.arange(GROUPS), 3)
    shuffle = jax.random.permutation(fifth_key, 3 * GROUPS)
    return (owners[shuffle].astype(jnp.int32), starts[shuffle].astype(jnp.int32), (end_points - starts)[shuffle].astype(jnp.int32))


def draw_sequence_group(key, part):
    return sequence_table(key)[0]


def draw_sequence_start(key, part):
    return sequence_table(key)[1]


def draw_sequence_length(key, part):
    return sequence_table(key)[2]


def level_of(stream_key, shape, cuts, low, high):
    def one(dim, shards_of):
        heights = jax.random.uniform(jax.random.fold_in(jax.random.fold_in(stream_key, 6), dim), (shards_of,), jnp.float32, low / len(cuts), high / len(cuts))
        return jnp.repeat(jnp.exp(heights), shape[dim] // shards_of).reshape((-1,) + (1,) * (len(shape) - dim - 1))

    factor_of = one(*cuts[0])
    for cut in cuts[1:]:
        factor_of = factor_of * one(*cut)
    return factor_of


def bell_draw(rng, shape, scale, limit, pieces=(), held_as=jnp.bfloat16):
    drawn = scale * jax.random.normal(rng, shape, jnp.float32)
    if pieces:
        drawn = drawn * level_of(rng, shape, pieces, -0.22, 0.18)
    return jnp.clip(drawn, -limit, limit).astype(held_as)


def setup_inputs(seed: int = 0) -> dict:
    streams_of = jax.random.split(jax.random.key(seed), 15)
    return {
        "hidden_in": bell_draw(streams_of[0], (GROUPS, GROUP_TOK, D), 1.0, 6.0, ((0, 16), (1, 8))),
        "out_grad": bell_draw(streams_of[1], (GROUPS, GROUP_TOK, D), 1.0, 6.0, ((0, 16), (1, 8))),
        "sequence_group": draw_sequence_group(jax.random.fold_in(streams_of[14], 71), 0),
        "sequence_start": draw_sequence_start(jax.random.fold_in(streams_of[14], 71), 0),
        "sequence_length": draw_sequence_length(jax.random.fold_in(streams_of[14], 71), 0),
        "norm_gain": jnp.clip(1.0 + 0.1 * jax.random.normal(streams_of[5], (LAYERS, 2, D), jnp.float32), 0.5, 1.5).astype(jnp.bfloat16),
        "norm_bias": bell_draw(streams_of[6], (LAYERS, 2, D), 0.3, 1.5, ((2, 128),)),
        "input_weight": bell_draw(streams_of[7], (LAYERS, D, 3 * D), D ** -0.5, 0.21875, ((1, 128),)),
        "input_bias": bell_draw(streams_of[8], (LAYERS, 2, D), 0.3, 1.5, ((2, 128),)),
        "output_weight": bell_draw(streams_of[9], (LAYERS, D, D), (D // 128) ** -0.5, 2.5, ((1, 128),)),
        "branch_bias": bell_draw(streams_of[10], (LAYERS, 2, D), 0.3, 1.5, ((2, 128),)),
        "up_weight": bell_draw(streams_of[11], (LAYERS, D, FF), D ** -0.5, 0.21875, ((1, 128),)),
        "up_bias": bell_draw(streams_of[12], (LAYERS, FF), 0.3, 1.5, ((1, 128),)),
        "down_weight": bell_draw(streams_of[13], (LAYERS, FF, D), FF ** -0.5, 0.109375, ((1, 128),)),
    }


@jax.custom_vjp
def low(v):
    return lax.optimization_barrier(v.astype(jnp.bfloat16)).astype(jnp.float32)

@jax.custom_vjp
def low_back(v):
    return v

def low_keep(v):
    return (low(v), None)

def low_pass(kept, grad):
    return (grad,)

def back_keep(v):
    return (v, None)

def back_low(kept, grad):
    return (low(grad),)
low.defvjp(low_keep, low_pass)
low_back.defvjp(back_keep, back_low)
norm_eps = 1e-05
score_scale = 0.125
highest = lax.Precision.HIGHEST

def product(left, right):
    return jnp.dot(left, right, precision=highest, preferred_element_type=jnp.float32)

def layer_norm(values, scales, offset):
    centre = values - lax.optimization_barrier(jnp.mean(values, axis=-1, keepdims=True))
    spread = lax.optimization_barrier(jnp.mean(centre * centre, axis=-1, keepdims=True))
    return centre * lax.rsqrt(spread + norm_eps) * scales + offset

def gelu_tanh(values):
    return 0.5 * values * (1.0 + jnp.tanh(0.7978845608028654 * (values + 0.044715 * values * values * values)))

def token_ids(group_index, positions, sequence_group, sequence_start, sequence_length):
    member = (sequence_group[None, :] == group_index) & (sequence_start[None, :] <= positions[:, None]) & (positions[:, None] < (sequence_start + sequence_length)[None, :])
    numbers = jnp.arange(sequence_group.shape[0], dtype=jnp.int32) + 1
    located = lax.optimization_barrier(jnp.sum(jnp.where(member, numbers[None, :], 0), axis=1)).astype(jnp.int32)
    return jnp.where(located > 0, located - 1, -1 - positions).astype(jnp.int32)

def attention(queries, key_rows, value_rows, visible):
    number = queries.shape[0]
    query_heads = queries.reshape(number, HEADS, HEAD_DIM)
    key_heads = key_rows.reshape(number, HEADS, HEAD_DIM)
    value_heads = value_rows.reshape(number, HEADS, HEAD_DIM)
    scores = jnp.einsum('qhd,khd->hqk', query_heads, key_heads, precision=highest) * score_scale
    scores = low_back(scores)
    scores = jnp.where(visible[None], scores, -1000000000.0)
    row_max = lax.optimization_barrier(jnp.max(scores, axis=-1, keepdims=True))
    raised = jnp.exp(scores - row_max)
    soft_weights = low(raised / lax.optimization_barrier(jnp.sum(raised, axis=-1, keepdims=True)))
    mixture = jnp.einsum('hqk,khd->qhd', soft_weights, value_heads, precision=highest)
    return mixture.reshape(number, D)

def group_layer(hidden, visible, weights):
    scales, offsets, joint_matrix, input_offsets, out_matrix, out_biases, up_matrix, up_offset, down_matrix = weights
    normed = low(layer_norm(hidden, scales[0], offsets[0]))
    joined = product(normed, joint_matrix)
    queries = low(low_back(joined[:, :D] + input_offsets[0]))
    key_rows = low(low_back(joined[:, D:2 * D]))
    value_rows = low(low_back(joined[:, 2 * D:] + input_offsets[1]))
    mixture = low(low_back(attention(queries, key_rows, value_rows, visible)))
    middle = hidden + low_back(product(mixture, out_matrix) + out_biases[0])
    second = low(layer_norm(middle, scales[1], offsets[1]))
    pre_gelu = low_back(product(second, up_matrix) + up_offset)
    activated = low(gelu_tanh(pre_gelu))
    return middle + low_back(product(activated, down_matrix) + out_biases[1])

def forward(hidden, params, visible):
    for layer_index in range(LAYERS):
        current = tuple((entry[layer_index] for entry in params))
        stepper = jax.checkpoint(partial(group_layer, weights=current))
        hidden = lax.map(lambda inputs: stepper(inputs[0], inputs[1]), (hidden, visible))
    return hidden

def reference(hidden_in, out_grad, sequence_group, sequence_start, sequence_length, norm_gain, norm_bias, input_weight, input_bias, output_weight, branch_bias, up_weight, up_bias, down_weight):
    positions = jnp.arange(GROUP_TOK, dtype=jnp.int32)

    def group_mask(group_index):
        sequence_ids = token_ids(group_index, positions, sequence_group, sequence_start, sequence_length)
        same = (sequence_ids[:, None] == sequence_ids[None, :]) & (positions[None, :] <= positions[:, None])
        return same | (positions[None, :] == positions[:, None])
    visible = lax.map(group_mask, jnp.arange(GROUPS, dtype=jnp.int32))
    params = tuple((entry.astype(jnp.float32) for entry in (norm_gain, norm_bias, input_weight, input_bias, output_weight, branch_bias, up_weight, up_bias, down_weight)))
    initial = hidden_in.astype(jnp.float32)
    result, pullback = jax.vjp(lambda hidden, weights: forward(hidden, weights, visible), initial, params)
    grad_hidden, grads = pullback(out_grad.astype(jnp.float32))
    return (result.astype(jnp.bfloat16), grad_hidden, grads[0], grads[1], grads[2], grads[3], grads[4], grads[5], grads[6], grads[7], grads[8])
```

```python
import jax
import jax.numpy as jnp
from jax import lax
from jax.sharding import Mesh, PartitionSpec as P

HEAD_DIM = 64
LAYERS = 2


norm_eps = 1e-05
score_scale = 0.125


def layer_norm(values, scales, offset):
    centre = values - jnp.mean(values, axis=-1, keepdims=True)
    spread = jnp.mean(centre * centre, axis=-1, keepdims=True)
    return centre * lax.rsqrt(spread + norm_eps) * scales + offset


def gelu_tanh(values):
    return (
        0.5
        * values
        * (1.0 + jnp.tanh(0.7978845608028654 * (values + 0.044715 * values * values * values)))
    )


def token_ids(group_index, positions, sequence_group, sequence_start, sequence_length):
    member = (
        (sequence_group[None, :] == group_index)
        & (sequence_start[None, :] <= positions[:, None])
        & (positions[:, None] < (sequence_start + sequence_length)[None, :])
    )
    numbers = jnp.arange(sequence_group.shape[0], dtype=jnp.int32) + 1
    located = jnp.sum(jnp.where(member, numbers[None, :], 0), axis=1)
    return jnp.where(located > 0, located - 1, -1 - positions)


DATA = ("y", "zh", "c")
CTX = ("x", "zl")
ALL = DATA + CTX
bf16 = jnp.bfloat16
f32 = jnp.float32


def outer_sum(left, right):
    return lax.dot_general(left, right, (((0,), (0,)), ((), ())), preferred_element_type=f32)


def back_product(left, matrix):
    return lax.dot_general(left, matrix, (((1,), (1,)), ((), ())), preferred_element_type=f32)


def column_sums(values):
    return jnp.sum(values.astype(f32), axis=0)


def spread(values, axes):
    count = lax.axis_size(axes)
    return lax.all_to_all(jnp.broadcast_to(values[None], (count,) + values.shape), axes, 0, 0)


def scores_of(q, k):
    return lax.dot_general(q, k, (((1,), (1,)), ((), ())), preferred_element_type=f32) * score_scale


def attend(q, k, v, visible):
    scores = jnp.where(visible, scores_of(q, k), -1000000000.0)
    row_max = jnp.max(scores, axis=-1, keepdims=True)
    raised = jnp.exp(scores - row_max)
    totals = jnp.sum(raised, axis=-1, keepdims=True)
    weights = (raised / totals).astype(bf16)
    mixed = jnp.dot(weights, v, preferred_element_type=f32)
    return mixed.astype(bf16), row_max + jnp.log(totals)


def attend_back(q, k, v, visible, log_total, mix_grad):
    weights = jnp.where(visible, jnp.exp(scores_of(q, k) - log_total), 0.0)
    weight_grad = lax.dot_general(mix_grad, v, (((1,), (1,)), ((), ())), preferred_element_type=f32)
    centre = jnp.sum(weights * weight_grad, axis=-1, keepdims=True)
    score_grad = (weights * (weight_grad - centre)).astype(bf16)
    q_grad = jnp.dot(score_grad, k, preferred_element_type=f32) * score_scale
    k_grad = outer_sum(score_grad, q) * score_scale
    v_grad = outer_sum(weights.astype(bf16), mix_grad)
    return q_grad.astype(bf16), k_grad.astype(bf16), v_grad.astype(bf16)


def to_heads(values, parts):
    pieces = []
    for x in range(4):
        for zl in range(2):
            own, shared = 3 * x + 2 * zl, 3 * x + 1
            for head in (own, shared):
                for v in values:
                    pieces.append(v[:, 64 * head : 64 * head + 64])
    width = 128 * len(values)
    return jnp.concatenate(pieces, axis=1).reshape(values[0].shape[0], 8, width).transpose(1, 0, 2)


def body(hidden_in, out_grad, sequence_group, sequence_start, sequence_length, norm_gain, norm_bias,
         input_weight, input_bias, output_weight, branch_bias, up_weight, up_bias, down_weight):
    width = hidden_in.shape[2]
    rows = hidden_in.shape[1]
    group_index = lax.axis_index(DATA)
    parity = lax.axis_index("zl")
    slots = rows * 8
    positions = jnp.arange(slots, dtype=jnp.int32)
    ids = token_ids(group_index, positions, sequence_group, sequence_start, sequence_length)
    visible = (ids[:, None] == ids[None, :]) & (positions[None, :] <= positions[:, None])

    def half_of(values):
        split = values.reshape((4, 2, rows) + values.shape[1:])
        return lax.dynamic_index_in_dim(split, parity, 1, keepdims=False).reshape((4 * rows,) + values.shape[1:])

    def pad_half(values):
        zero = jnp.zeros((4, 2, rows) + values.shape[1:], values.dtype)
        return lax.dynamic_update_index_in_dim(zero, values.reshape((4, rows) + values.shape[1:]), parity, 1).reshape(
            (8 * rows,) + values.shape[1:])

    visible_half = half_of(visible)

    smalls = jnp.concatenate([v.reshape(-1) for v in (norm_gain, norm_bias, input_bias, branch_bias, up_bias)])
    smalls = jnp.pad(smalls, (0, 2048 - smalls.shape[0])).reshape(16, 128)
    full = []
    for l in range(LAYERS):
        flat = [input_weight[l].reshape(-1, 128), output_weight[l].reshape(-1, 128), up_weight[l].reshape(-1, 128),
                down_weight[l].reshape(-1, 128)]
        if l == 0:
            flat.append(smalls)
        got = spread(jnp.concatenate(flat, axis=0), CTX)
        if l == 0:
            few = spread(got[:, 432:434], DATA).reshape(128, 256)
        own = (got[:, 0:108].reshape(48, 2304), got[:, 108:144].reshape(48, 768), got[:, 144:288].reshape(48, 3072),
               got[:, 288:432].reshape(192, 768))
        full.append([lax.all_gather(w, DATA, axis=0, tiled=True) for w in own])
    few = few.astype(f32)

    def vec(first):
        return few[:, first : first + 6].reshape(-1)

    gains = [[vec(12 * l + 6 * i) for i in range(2)] for l in range(2)]
    offsets = [[vec(24 + 12 * l + 6 * i) for i in range(2)] for l in range(2)]
    in_biases = [[vec(48 + 12 * l + 6 * i) for i in range(2)] for l in range(2)]
    out_biases = [[vec(72 + 12 * l + 6 * i) for i in range(2)] for l in range(2)]
    up_biases = [few[:, 96 + 24 * l : 120 + 24 * l].reshape(-1) for l in range(2)]

    hidden = hidden_in[0].astype(f32)
    stored = []
    for l in range(LAYERS):
        w_in, w_out, w_up, w_down = full[l]
        normed = layer_norm(hidden, gains[l][0], offsets[l][0]).astype(bf16)
        joined = jnp.dot(normed, w_in, preferred_element_type=f32)
        q = (joined[:, :width] + in_biases[l][0]).astype(bf16)
        k = joined[:, width : 2 * width].astype(bf16)
        v = (joined[:, 2 * width :] + in_biases[l][1]).astype(bf16)
        heads = lax.all_to_all(to_heads((q, k, v), 3), CTX, 0, 0).reshape(slots, 384)
        own = (heads[:, :64], heads[:, 64:128], heads[:, 128:192])
        shared = (half_of(heads[:, 192:256]), heads[:, 256:320], heads[:, 320:384])
        mix_own, log_own = attend(*own, visible)
        mix_shared, log_shared = attend(*shared, visible_half)
        back = lax.all_to_all(
            jnp.concatenate([mix_own, pad_half(mix_shared)], axis=1).reshape(8, rows, 128), CTX, 0, 0)
        mixed = []
        for x in range(4):
            mixed += [back[2 * x, :, :64], back[2 * x, :, 64:] + back[2 * x + 1, :, 64:], back[2 * x + 1, :, :64]]
        mixed = jnp.concatenate(mixed, axis=1)
        middle = hidden + jnp.dot(mixed, w_out, preferred_element_type=f32) + out_biases[l][0]
        second = layer_norm(middle, gains[l][1], offsets[l][1]).astype(bf16)
        pre_gelu = jnp.dot(second, w_up, preferred_element_type=f32) + up_biases[l]
        activated = gelu_tanh(pre_gelu).astype(bf16)
        stored.append((hidden, normed, own, shared, log_own, log_shared, mixed, middle, second, pre_gelu, activated))
        hidden = middle + jnp.dot(activated, w_down, preferred_element_type=f32) + out_biases[l][1]

    grad_hidden = out_grad[0].astype(f32)
    grads = [None, None]
    small_grads = [None, None]
    for l in reversed(range(LAYERS)):
        w_in, w_out, w_up, w_down = full[l]
        layer_input, normed, own, shared, log_own, log_shared, mixed, middle, second, pre_gelu, activated = stored[l]

        def scatter(grad):
            return lax.psum_scatter(grad.astype(bf16), DATA, scatter_dimension=0, tiled=True)

        down_grad = grad_hidden.astype(bf16)
        grad_down = scatter(outer_sum(activated, down_grad))
        bias_down = column_sums(down_grad)
        gelu_grad = back_product(down_grad, w_down)
        pre_grad = jax.vjp(gelu_tanh, pre_gelu)[1](gelu_grad)[0].astype(bf16)
        grad_up = scatter(outer_sum(second, pre_grad))
        bias_up = column_sums(pre_grad)
        second_grad = back_product(pre_grad, w_up)
        middle_grad, scale_two, offset_two = jax.vjp(layer_norm, middle, gains[l][1], offsets[l][1])[1](second_grad)
        grad_middle = grad_hidden + middle_grad
        branch_grad = grad_middle.astype(bf16)
        grad_output = scatter(outer_sum(mixed, branch_grad))
        bias_out = column_sums(branch_grad)
        mix_grad = back_product(branch_grad, w_out).astype(bf16)
        got = lax.all_to_all(to_heads((mix_grad,), 1), CTX, 0, 0).reshape(slots, 128)
        own_grads = attend_back(*own, visible, log_own, got[:, :64])
        shared_grads = attend_back(*shared, visible_half, log_shared, half_of(got[:, 64:]))
        shared_grads = (pad_half(shared_grads[0]),) + shared_grads[1:]
        back = lax.all_to_all(
            jnp.concatenate(own_grads + shared_grads, axis=1).reshape(8, rows, 384), CTX, 0, 0)
        joined_grad = []
        for part in range(3):
            for x in range(4):
                lo, hi = back[2 * x], back[2 * x + 1]
                a, b = 64 * part, 192 + 64 * part
                both = (lo[:, b : b + 64].astype(f32) + hi[:, b : b + 64].astype(f32)).astype(bf16)
                joined_grad += [lo[:, a : a + 64], both, hi[:, a : a + 64]]
        joined_grad = jnp.concatenate(joined_grad, axis=1)
        grad_joint = scatter(outer_sum(normed, joined_grad))
        bias_query = column_sums(joined_grad[:, :width])
        bias_value = column_sums(joined_grad[:, 2 * width :])
        normed_grad = back_product(joined_grad, w_in)
        input_grad, scale_one, offset_one = jax.vjp(layer_norm, layer_input, gains[l][0], offsets[l][0])[1](normed_grad)
        grad_hidden = grad_middle + input_grad
        flat = jnp.concatenate([grad_joint.reshape(8, 108, 128), grad_output.reshape(8, 36, 128),
                                grad_up.reshape(8, 144, 128), grad_down.reshape(8, 144, 128)], axis=1)
        flat = jnp.sum(lax.all_to_all(flat, CTX, 0, 0).astype(f32), axis=0)
        grads[l] = (flat[0:108].reshape(6, 2304), flat[108:144].reshape(6, 768), flat[144:288].reshape(6, 3072),
                    flat[288:432].reshape(24, 768))
        small_grads[l] = [t.reshape(128, -1) for t in (scale_one, scale_two, offset_one, offset_two, bias_query,
                                                       bias_value, bias_out, bias_down, bias_up)]
    few = jnp.concatenate(small_grads[0] + small_grads[1], axis=1)
    few = jnp.pad(few, ((0, 0), (0, 256 - 144)))
    few = jnp.sum(lax.all_to_all(few, ALL, 0, 0, tiled=True), axis=0)

    def pair(first):
        return jnp.stack([jnp.stack([few[72 * l + first + 6 * i : 72 * l + first + 6 * i + 6] for i in range(2)])
                          for l in range(2)])

    return (
        hidden.astype(bf16)[None],
        grad_hidden[None],
        pair(0),
        pair(12),
        jnp.stack([grads[0][0], grads[1][0]]),
        pair(24),
        jnp.stack([grads[0][1], grads[1][1]]),
        pair(36),
        jnp.stack([grads[0][2], grads[1][2]]),
        jnp.stack([few[48:72], few[120:144]]),
        jnp.stack([grads[0][3], grads[1][3]]),
    )


def solution(mesh):
    mesh = Mesh(mesh.devices.reshape(4, 2, 2, 4, 2), ALL)
    token = P(DATA, CTX, None)
    one = P(None, ALL)
    two = P(None, None, ALL)
    mat = P(None, ALL, None)
    return jax.shard_map(
        body,
        mesh=mesh,
        in_specs=(token, token, P(), P(), P(), two, two, mat, two, mat, two, mat, one, mat),
        out_specs=(token, token, two, two, mat, two, mat, two, mat, one, mat),
        check_vma=False,
    )
```

```python
import functools

import jax
import jax.numpy as jnp
from jax import lax
from jax.experimental import pallas as pl
from jax.experimental.pallas import tpu as pltpu
from jax.sharding import Mesh, PartitionSpec as P

LAYERS = 2
D = 768
TOK = 128
CTX_DEV = 8
SLOTS = TOK * CTX_DEV
DATA = ("y", "zh", "c")
CTX = ("x", "zl")
ALL = DATA + CTX
bf16 = jnp.bfloat16
f32 = jnp.float32
norm_eps = 1e-05
score_scale = 0.125
hidden_value = -1000000000.0


def coord(bit_b, bit_a, core):
    return core * (2 * bit_b + bit_a) + (1 - core) * (3 * bit_a + bit_b * (1 - 2 * bit_a))


def place(n, core):
    y = coord((n >> 5) & 1, (n >> 2) & 1, core)
    z = coord((n >> 4) & 1, (n >> 1) & 1, core)
    x = coord((n >> 3) & 1, n & 1, core)
    return (y * 2 + (z >> 1)) * 2 + core, x * 2 + (z & 1)


SLOT_OF = {(c,) + place(n, c): n for c in range(2) for n in range(64)}


def device_id(y, z, core, x):
    return y * 32 + (z >> 1) * 16 + core * 8 + x * 2 + (z & 1)


def cube_groups(level):
    found = {}
    for core in range(2):
        for n in range(64):
            bits = [(n >> s) & 1 for s in range(6)]
            y, z, x = (coord(bits[3 + s], bits[s], core) for s in (2, 1, 0))
            if level == 1:
                key = (core,) + tuple(coord(bits[3 + s], 0, core) for s in (2, 1, 0))
                slot = n & 7
            else:
                pair = [coord(bits[3 + s], bits[s], core) for s in (2, 1, 0)]
                pair = [(v // 2 if core == 0 else ((v + 1) // 2) % 2) for v in pair]
                key = (core,) + tuple(pair)
                slot = n >> 3
            found.setdefault(key, [None] * 8)[slot] = device_id(y, z, core, x)
    return [found[k] for k in sorted(found)]


GROUPS_A = cube_groups(1)
GROUPS_B = cube_groups(0)


def fetch(core_ref, mine, theirs, w, sem, low, high):
    core = core_ref[0]

    def step(n, carry):
        for src, own in ((mine, core), (theirs, 1 - core)):
            row, triple = place(n, own)

            @pl.when((triple >= low) & (triple < high))
            def _():
                pltpu.make_async_copy(src.at[n], w.at[row, pl.ds((triple - low) * 3, 3)], sem).start()

        return carry

    lax.fori_loop(0, 64, step, 0)


def arrived(w, sem):
    pltpu.make_async_copy(w, w, sem).wait()


def units(w, first, count):
    parts = [w[:, first + i].reshape(D, 128) for i in range(count)]
    return parts[0] if count == 1 else jnp.concatenate(parts, axis=1)


def tall_units(w, cb):
    return w[:, 4 * cb : 4 * cb + 4].reshape(4 * D, 128)


def mul(a, b):
    return jnp.dot(a, b, preferred_element_type=f32)


def mul_t(a, b):
    return lax.dot_general(a, b, (((1,), (1,)), ((), ())), preferred_element_type=f32)


def t_mul(a, b):
    return lax.dot_general(a, b, (((0,), (0,)), ((), ())), preferred_element_type=f32)


def norm_parts(values):
    centre = values - jnp.mean(values, axis=-1, keepdims=True)
    var = jnp.mean(centre * centre, axis=-1, keepdims=True)
    r = lax.rsqrt(var + norm_eps)
    return centre * r, r


def norm_back(cot, gain, xh, r):
    cg = cot * gain
    return r * (cg - jnp.mean(cg, axis=-1, keepdims=True) - xh * jnp.mean(cg * xh, axis=-1, keepdims=True))


def rows_sum(values):
    return jnp.sum(values, axis=0, keepdims=True)


def windows(values):
    out = []
    for x in range(4):
        for zl in range(2):
            own, shared = 3 * x + 2 * zl, 3 * x + 1
            out.append(jnp.concatenate([values[:, 64 * own : 64 * own + 64],
                                        values[:, 64 * shared : 64 * shared + 64]], axis=1))
    return out


def unwindow(get):
    parts = []
    for x in range(4):
        lo, hi = get(2 * x), get(2 * x + 1)
        parts += [lo[:, :64], lo[:, 64:] + hi[:, 64:], hi[:, :64]]
    return jnp.concatenate(parts, axis=1)


def gelu_both(u):
    k = 0.7978845608028654
    t = jnp.tanh(k * (u + 0.044715 * u * u * u))
    half = 0.5 * (1.0 + t)
    return u * half, half + 0.5 * u * (1.0 - t * t) * (k * (1.0 + 3 * 0.044715 * u * u))


def project_kernel(core, h_ref, vec, mine, theirs, a1_ref, pay_ref, w, sem):
    fetch(core, mine, theirs, w, sem, 0, 6)
    xh, _ = norm_parts(h_ref[...].astype(f32))
    a1 = (xh * vec[0:1] + vec[1:2]).astype(bf16)
    a1_ref[...] = a1
    arrived(w, sem)
    for part in range(3):
        cols = [mul(a1, units(w, 6 * part + 2 * j, 2)) for j in range(3)]
        got = jnp.concatenate(cols, axis=1)
        if part != 1:
            got = got + vec[2 + part // 2 : 3 + part // 2]
        got = got.astype(bf16).astype(f32)
        for d, win in enumerate(windows(got)):
            pay_ref[d, :, 128 * part : 128 * part + 128] = win.astype(bf16)


def visible_of(block, count, idc_ref, idr_ref):
    n = count * TOK
    qpos = block * TOK + lax.broadcasted_iota(jnp.int32, (TOK, n), 0)
    kpos = lax.broadcasted_iota(jnp.int32, (TOK, n), 1)
    return (idc_ref[block] == idr_ref[:, 0:n]) & (kpos <= qpos)


def head_blocks(par):
    for i in range(4):
        yield i, ((0, 2 * i, 2 * i + 1), (0, 2 * i + 1, 2 * i + 2), (1, 2 * i + par, 2 * i + 2))


def half(values, head):
    return values[:, 64 * head : 64 * head + 64]


def store_pair(out, lanes, i, par, parts):
    for k in range(2):
        shared = jnp.where(par == k, parts[2], 0.0)
        out[2 * i + k, :, lanes] = jnp.concatenate([parts[k], shared], axis=1).astype(bf16)


def weights_of(q, key, seen):
    s = jnp.where(seen, mul_t(q, key) * score_scale, hidden_value)
    e = jnp.exp(s - jnp.max(s, axis=1, keepdims=True))
    return e / jnp.sum(e, axis=1, keepdims=True)


def attend_kernel(par_ref, heads, idc, idr, out):
    par = par_ref[0]
    key = heads[:, :, 128:256].reshape(SLOTS, 128)
    val = heads[:, :, 256:384].reshape(SLOTS, 128)
    keys, vals = [half(key, h) for h in range(2)], [half(val, h) for h in range(2)]
    for i, blocks in head_blocks(par):
        parts = []
        for head, block, count in blocks:
            n = count * TOK
            q = half(heads[block, :, 0:128], head)
            p = weights_of(q, keys[head][:n], visible_of(block, count, idc, idr)).astype(bf16)
            parts.append(mul(p, vals[head][:n]))
        store_pair(out, slice(0, 128), i, par, parts)


def attend_back_kernel(par_ref, heads, cot, idc, idr, out, dk_acc, dv_acc):
    par = par_ref[0]
    key = heads[:, :, 128:256].reshape(SLOTS, 128)
    val = heads[:, :, 256:384].reshape(SLOTS, 128)
    keys, vals = [half(key, h) for h in range(2)], [half(val, h) for h in range(2)]
    dk_acc[...] = jnp.zeros_like(dk_acc)
    dv_acc[...] = jnp.zeros_like(dv_acc)
    for i, blocks in head_blocks(par):
        parts = []
        for head, block, count in blocks:
            n = count * TOK
            q = half(heads[block, :, 0:128], head)
            g = half(cot[block], head)
            p = weights_of(q, keys[head][:n], visible_of(block, count, idc, idr))
            dp = mul_t(g, vals[head][:n])
            ds = (p * (dp - jnp.sum(p * dp, axis=1, keepdims=True))).astype(bf16)
            parts.append(mul(ds, keys[head][:n]) * score_scale)
            dk_acc[head, 0:n] += t_mul(ds, q)
            dv_acc[head, 0:n] += t_mul(p.astype(bf16), g)
        store_pair(out, slice(0, 128), i, par, parts)
    dk = jnp.concatenate([dk_acc[0], dk_acc[1]], axis=1) * score_scale
    dv = jnp.concatenate([dv_acc[0], dv_acc[1]], axis=1)
    out[:, :, 128:256] = dk.astype(bf16).reshape(8, TOK, 128)
    out[:, :, 256:384] = dv.astype(bf16).reshape(8, TOK, 128)


def forward_kernel(core, h_ref, back, vec, upb, me, te, mu, tu, md, td,
                   o_ref, h1_ref, a2_ref, u_ref, next_ref, wo, wu, wd, sems):
    fetch(core, me, te, wo, sems.at[0], 6, 8)
    fetch(core, mu, tu, wu, sems.at[1], 0, 8)
    fetch(core, md, td, wd, sems.at[2], 0, 8)
    o = unwindow(lambda d: back[d].astype(f32)).astype(bf16)
    o_ref[...] = o
    arrived(wo, sems.at[0])
    got = jnp.concatenate([mul(o, units(wo, 2 * j, 2)) for j in range(3)], axis=1)
    h1 = h_ref[...].astype(f32) + got + vec[2:3]
    h1_ref[...] = h1
    xh, _ = norm_parts(h1)
    a2 = (xh * vec[0:1] + vec[1:2]).astype(bf16)
    a2_ref[...] = a2
    arrived(wu, sems.at[1])
    acts = []
    for j in range(12):
        u = mul(a2, units(wu, 2 * j, 2)) + upb[:, 256 * j : 256 * j + 256]
        u_ref[:, 256 * j : 256 * j + 256] = u
        acts.append(gelu_both(u)[0].astype(bf16))
    f = jnp.concatenate(acts, axis=1)
    arrived(wd, sems.at[2])
    for j in range(3):
        w = jnp.concatenate([tall_units(wd, 2 * j), tall_units(wd, 2 * j + 1)], axis=1)
        c = slice(256 * j, 256 * j + 256)
        next_ref[:, c] = (h1[:, c] + mul(f, w) + vec[3:4, c]).astype(next_ref.dtype)


def backward_kernel(core, e_ref, u_ref, h1_ref, vec, me, te, mu, tu, md, td,
                    f_ref, du_ref, e1_ref, pay_ref, small_ref, upb_ref, wo, wu, wd, sems):
    fetch(core, md, td, wd, sems.at[2], 0, 8)
    fetch(core, mu, tu, wu, sems.at[1], 0, 8)
    fetch(core, me, te, wo, sems.at[0], 6, 8)
    e = e_ref[...].astype(f32)
    e2 = e.astype(bf16)
    arrived(wd, sems.at[2])
    df = jnp.zeros((TOK, 4 * D), f32)
    for j in range(3):
        w = jnp.concatenate([tall_units(wd, 2 * j), tall_units(wd, 2 * j + 1)], axis=1)
        df = df + mul_t(e2[:, 256 * j : 256 * j + 256], w)
    arrived(wu, sems.at[1])
    cot = jnp.zeros((TOK, D), f32)
    for j in range(12):
        c = slice(256 * j, 256 * j + 256)
        f, slope = gelu_both(u_ref[:, c])
        f_ref[:, c] = f.astype(bf16)
        du = (df[:, c] * slope).astype(bf16)
        du_ref[:, c] = du
        upb_ref[:, c] = rows_sum(du.astype(f32))
        cot = cot + mul_t(du, units(wu, 2 * j, 2))
    xh, r = norm_parts(h1_ref[...])
    e1 = e + norm_back(cot, vec[0:1], xh, r)
    e1_ref[...] = e1
    b1 = e1.astype(bf16)
    small_ref[0:1] = rows_sum(cot * xh)
    small_ref[1:2] = rows_sum(cot)
    small_ref[2:3] = rows_sum(b1.astype(f32))
    small_ref[3:4] = rows_sum(e2.astype(f32))
    arrived(wo, sems.at[0])
    do = jnp.zeros((TOK, D), f32)
    for j in range(3):
        do = do + mul_t(b1[:, 256 * j : 256 * j + 256], units(wo, 2 * j, 2))
    do = do.astype(bf16).astype(f32)
    for d, win in enumerate(windows(do)):
        pay_ref[d] = win.astype(bf16)


def back_project_kernel(core, back, e1_ref, h_ref, vec, mine, theirs, g_ref, e_ref, small_ref, w, sem):
    fetch(core, mine, theirs, w, sem, 0, 6)
    for part in range(3):
        got = unwindow(lambda d: back[d, :, 128 * part : 128 * part + 128].astype(f32)).astype(bf16)
        g_ref[:, D * part : D * part + D] = got
        if part != 1:
            small_ref[2 + part // 2 : 3 + part // 2] = rows_sum(got.astype(f32))
    arrived(w, sem)
    cot = jnp.zeros((TOK, D), f32)
    for j in range(9):
        cot = cot + mul_t(g_ref[:, 256 * j : 256 * j + 256], units(w, 2 * j, 2))
    xh, r = norm_parts(h_ref[...].astype(f32))
    small_ref[0:1] = rows_sum(cot * xh)
    small_ref[1:2] = rows_sum(cot)
    e_ref[...] = e1_ref[...] + norm_back(cot, vec[0:1], xh, r)


def store_grad(core, out, wide, first):
    for i in range(wide.shape[1] // 128):
        rows = wide[:, 128 * i : 128 * i + 128].astype(bf16).reshape(16, 48, 128)
        triple, k = divmod(first + i, 3)
        for row in range(16):
            target = row & 1
            out[core ^ target, SLOT_OF[(target, row, triple)], k] = rows[row]


def grad_wide_kernel(core_ref, a_ref, b_ref, out):
    core = core_ref[0]
    at = a_ref[...].T
    for j in range(4):
        store_grad(core, out, mul(at, b_ref[:, D * j : D * j + D]), 6 * j)


def grad_tall_kernel(core_ref, f_ref, e_ref, out):
    core = core_ref[0]
    ft = f_ref[...].T
    e2 = e_ref[...].astype(f32).astype(bf16)
    for j in range(3):
        wide = mul(ft, e2[:, 256 * j : 256 * j + 256]).astype(bf16)
        for half in range(2):
            rows = wide[:, 128 * half : 128 * half + 128].reshape(16, 4, 48, 128)
            for q in range(4):
                triple, k = divmod(4 * (2 * j + half) + q, 3)
                for row in range(16):
                    target = row & 1
                    out[core ^ target, SLOT_OF[(target, row, triple)], k] = rows[row, q]


def grad_joint_kernel(core_ref, a_ref, g_ref, o_ref, e1_ref, out):
    core = core_ref[0]
    at = a_ref[...].T
    for j in range(3):
        store_grad(core, out, mul(at, g_ref[:, D * j : D * j + D]), 6 * j)
    store_grad(core, out, mul(o_ref[...].T, e1_ref[...].astype(bf16)), 18)


def call(kernel, outs, ins, scratch=(), flops=0, bytes_accessed=0):
    spaces = {"s": pltpu.SMEM, "v": pltpu.VMEM, "a": pl.ANY}
    return pl.pallas_call(
        kernel,
        out_shape=[jax.ShapeDtypeStruct(*o) for o in outs],
        in_specs=[pl.BlockSpec(memory_space=spaces[m]) for _, m in ins],
        out_specs=[pl.BlockSpec(memory_space=pltpu.VMEM)] * len(outs),
        scratch_shapes=list(scratch),
        compiler_params=pltpu.CompilerParams(vmem_limit_bytes=56 * 1024 * 1024),
        cost_estimate=pl.CostEstimate(flops=flops, bytes_accessed=bytes_accessed, transcendentals=0),
    )(*[a for a, _ in ins])


def w_scratch(count):
    return pltpu.VMEM((16, count, 48, 128), bf16)


DMA = pltpu.SemaphoreType.DMA


def copies(values, groups):
    many = jnp.broadcast_to(values[None], (8,) + values.shape)
    return lax.all_to_all(many, ALL, 0, 0, axis_index_groups=groups)


def sum_first(values):
    return jnp.sum(values.astype(f32), axis=0)


def swap_core(values):
    return lax.ppermute(values, "c", [(0, 1), (1, 0)])


def spread(shard):
    rows = shard.shape[1]
    mine = copies(shard.reshape(8 * rows, 128), GROUPS_B).reshape(64, rows // 48, 48, 128)
    return mine, swap_core(mine)


def ff_in(values):
    lead = values.shape[:-1]
    return jnp.swapaxes(values.reshape(lead + (16, 8, 4, 6)), -3, -2).reshape(lead + (4 * D,))


def ff_out(values):
    lead = values.shape[:-1]
    return jnp.swapaxes(values.reshape(lead + (16, 4, 8, 6)), -3, -2).reshape(lead + (4 * D,))


def to_units(values):
    return jnp.swapaxes(values.reshape(6, -1, 128), 0, 1)


def from_units(values):
    return jnp.swapaxes(values, 0, 1).reshape(6, -1)


def token_ids(group_index, positions, sequence_group, sequence_start, sequence_length):
    member = (
        (sequence_group[None, :] == group_index)
        & (sequence_start[None, :] <= positions[:, None])
        & (positions[:, None] < (sequence_start + sequence_length)[None, :])
    )
    numbers = jnp.arange(sequence_group.shape[0], dtype=jnp.int32) + 1
    located = jnp.sum(jnp.where(member, numbers[None, :], 0), axis=1)
    return jnp.where(located > 0, located - 1, -1 - positions)


def body(hidden_in, out_grad, sequence_group, sequence_start, sequence_length, norm_gain, norm_bias,
         input_weight, input_bias, output_weight, branch_bias, up_weight, up_bias, down_weight):
    core = lax.axis_index("c").astype(jnp.int32).reshape(1)
    par = lax.axis_index("zl").astype(jnp.int32).reshape(1)
    positions = jnp.arange(SLOTS, dtype=jnp.int32)
    ids = token_ids(lax.axis_index(DATA), positions, sequence_group, sequence_start, sequence_length)
    idc, idr = ids.reshape(CTX_DEV, TOK, 1), ids.reshape(1, SLOTS)

    parts = []
    for l in range(LAYERS):
        parts.append(to_units(input_weight[l]))
        parts.append(to_units(output_weight[l]))
        parts.append(to_units(ff_in(up_weight[l])))
        down = down_weight[l].reshape(4, 6, 6, 128)
        parts.append(down.transpose(2, 0, 1, 3).reshape(24, 6, 128))
    packed = jnp.concatenate(parts, axis=0).reshape(2, 3, 8, 3, 6, 128)
    packed = packed.transpose(2, 0, 1, 3, 4, 5).reshape(8, 18, 6, 128)
    got = lax.all_to_all(packed, CTX, 0, 0)
    got = got.transpose(1, 0, 2, 3).reshape(2, 3, 144, 128)

    smalls = jnp.concatenate([v.reshape(-1) for v in (norm_gain, norm_bias, input_bias, branch_bias, up_bias)])
    smalls = jnp.pad(smalls, (0, 256 - 144)).reshape(1, 2, 128)
    few = lax.all_to_all(jnp.broadcast_to(smalls, (128, 2, 128)), ALL, 0, 0).reshape(128, 256).astype(f32)
    vecs = few[:, :96].reshape(128, 16, 6).transpose(1, 0, 2).reshape(16, D)
    ups = few[:, 96:144].reshape(16, 8, 2, 4, 6).transpose(2, 0, 3, 1, 4).reshape(2, 4 * D)

    first = copies(got[0, 0], GROUPS_A)
    rest = copies(got.reshape(6 * 144, 128)[144:], GROUPS_A).reshape(8, 5, 144, 128)
    weights = [[spread(first), spread(rest[:, 0]), spread(rest[:, 1])],
               [spread(rest[:, 2]), spread(rest[:, 3]), spread(rest[:, 4])]]

    def vec(*index):
        return jnp.concatenate([vecs[i : i + 1] for i in index], axis=0)

    hidden = hidden_in[0]
    stored = []
    for l in range(LAYERS):
        group_e, group_u, group_d = weights[l]
        a1, pay = call(
            project_kernel,
            [((TOK, D), bf16), ((8, TOK, 384), bf16)],
            [(core, "s"), (hidden, "v"), (vec(2 * l, 4 + 2 * l, 8 + 2 * l, 9 + 2 * l), "v"),
             (group_e[0], "a"), (group_e[1], "a")],
            [w_scratch(18), DMA],
            flops=2 * TOK * D * 3 * D, bytes_accessed=4 * 2**20)
        heads = lax.all_to_all(pay, CTX, 0, 0)
        (mix,) = call(
            attend_kernel,
            [((8, TOK, 128), bf16)],
            [(par, "s"), (heads, "v"), (idc, "v"), (idr, "v")],
            flops=2 * 2 * 64 * 56 * 128 * 128, bytes_accessed=2**20)
        back = lax.all_to_all(mix, CTX, 0, 0)
        o, h1, a2, u, following = call(
            forward_kernel,
            [((TOK, D), bf16), ((TOK, D), f32), ((TOK, D), bf16), ((TOK, 4 * D), f32),
             ((TOK, D), f32 if l == 0 else bf16)],
            [(core, "s"), (hidden, "v"), (back, "v"), (vec(2 * l + 1, 5 + 2 * l, 12 + 2 * l, 13 + 2 * l), "v"),
             (ups[l : l + 1], "v")] + [(w, "a") for pair in weights[l] for w in pair],
            [w_scratch(6), w_scratch(24), w_scratch(24), DMA((3,))],
            flops=2 * TOK * D * 9 * D, bytes_accessed=12 * 2**20)
        stored.append((hidden, a1, heads, o, h1, a2, u))
        hidden = following

    grad = out_grad[0]
    sums = []
    few_rows, few_up = [None] * 2, [None] * 2
    for l in reversed(range(LAYERS)):
        layer_in, a1, heads, o, h1, a2, u = stored[l]
        f, du, e1, pay, small_b, small_u = call(
            backward_kernel,
            [((TOK, 4 * D), bf16), ((TOK, 4 * D), bf16), ((TOK, D), f32), ((8, TOK, 128), bf16),
             ((4, D), f32), ((1, 4 * D), f32)],
            [(core, "s"), (grad, "v"), (u, "v"), (h1, "v"), (vec(2 * l + 1), "v")]
            + [(w, "a") for pair in weights[l] for w in pair],
            [w_scratch(6), w_scratch(24), w_scratch(24), DMA((3,))],
            flops=2 * TOK * D * 9 * D, bytes_accessed=12 * 2**20)
        cot = lax.all_to_all(pay, CTX, 0, 0)
        (grad_d,) = call(grad_tall_kernel, [((2, 64, 3, 48, 128), bf16)], [(core, "s"), (f, "v"), (grad, "v")],
                         flops=2 * TOK * D * 4 * D, bytes_accessed=6 * 2**20)
        (grad_u,) = call(grad_wide_kernel, [((2, 64, 3, 48, 128), bf16)], [(core, "s"), (a2, "v"), (du, "v")],
                         flops=2 * TOK * D * 4 * D, bytes_accessed=6 * 2**20)
        (pay2,) = call(
            attend_back_kernel,
            [((8, TOK, 384), bf16)],
            [(par, "s"), (heads, "v"), (cot, "v"), (idc, "v"), (idr, "v")],
            [pltpu.VMEM((2, SLOTS, 64), f32)] * 2,
            flops=5 * 2 * 64 * 56 * 128 * 128, bytes_accessed=2**21)
        back2 = lax.all_to_all(pay2, CTX, 0, 0)
        g, grad, small_a = call(
            back_project_kernel,
            [((TOK, 3 * D), bf16), ((TOK, D), f32), ((4, D), f32)],
            [(core, "s"), (back2, "v"), (e1, "v"), (layer_in, "v"), (vec(2 * l), "v"),
             (weights[l][0][0], "a"), (weights[l][0][1], "a")],
            [w_scratch(18), DMA],
            flops=2 * TOK * D * 3 * D, bytes_accessed=4 * 2**20)
        (grad_e,) = call(grad_joint_kernel, [((2, 64, 3, 48, 128), bf16)],
                         [(core, "s"), (a1, "v"), (g, "v"), (o, "v"), (e1, "v")],
                         flops=2 * TOK * D * 4 * D, bytes_accessed=6 * 2**20)
        layer_sums = []
        for both in (grad_e, grad_u, grad_d):
            part = (both[0].astype(f32) + swap_core(both[1]).astype(f32)).astype(bf16).reshape(8, 8 * 144, 128)
            part = sum_first(lax.all_to_all(part, ALL, 0, 0, axis_index_groups=GROUPS_B)).astype(bf16)
            layer_sums.append(part.reshape(8, 144, 128))
        sums.append(layer_sums)
        few_rows[l] = jnp.concatenate([small_a[0:1], small_b[0:1], small_a[1:2], small_b[1:2], small_a[2:4],
                                       small_b[2:4]], axis=0)
        few_up[l] = small_u

    def finish(values):
        n = values.shape[1] // 144
        part = sum_first(lax.all_to_all(values, ALL, 0, 0, axis_index_groups=GROUPS_A))
        part = part.reshape(n * 3, 8, 6, 128).transpose(1, 0, 2, 3)
        part = lax.all_to_all(part, CTX, 0, 0)
        return part.reshape(8, n, 3, 6, 128).transpose(1, 0, 2, 3, 4).reshape(n, 24, 6, 128)

    (e_hi, u_hi, d_hi), (e_lo, u_lo, d_lo) = sums
    early = finish(jnp.concatenate([e_hi, u_hi, d_hi, u_lo, d_lo], axis=1))
    late = finish(e_lo)
    group_e, group_u, group_d = (late[0], early[0]), (early[3], early[1]), (early[4], early[2])

    few = jnp.concatenate([r.reshape(8, 128, 6).transpose(1, 0, 2).reshape(128, 48) for r in few_rows]
                          + [r.reshape(16, 4, 8, 6).transpose(0, 2, 1, 3).reshape(128, 24) for r in few_up], axis=1)
    few = jnp.pad(few, ((0, 0), (0, 256 - 144))).reshape(128, 2, 128)
    few = jnp.sum(lax.all_to_all(few, ALL, 0, 0), axis=0).reshape(256)
    few_l = [few[48 * l : 48 * l + 48].reshape(4, 2, 6) for l in range(2)]

    def pair(k):
        return jnp.stack([few_l[0][k], few_l[1][k]])

    return (
        hidden[None],
        grad[None],
        pair(0),
        pair(1),
        jnp.stack([from_units(v[:18]) for v in group_e]),
        pair(2),
        jnp.stack([from_units(v[18:]) for v in group_e]),
        pair(3),
        jnp.stack([ff_out(from_units(v)) for v in group_u]),
        few[96:144].reshape(2, 24),
        jnp.stack([v.reshape(6, 4, 6, 128).transpose(1, 2, 0, 3).reshape(24, D) for v in group_d]),
    )


def solution(mesh):
    mesh = Mesh(mesh.devices.reshape(4, 2, 2, 4, 2), ALL)
    token = P(DATA, CTX, None)
    one = P(None, ALL)
    two = P(None, None, ALL)
    mat = P(None, ALL, None)
    return jax.shard_map(
        body,
        mesh=mesh,
        in_specs=(token, token, P(), P(), P(), two, two, mat, two, mat, two, mat, one, mat),
        out_specs=(token, token, two, two, mat, two, mat, two, mat, one, mat),
        check_vma=False,
    )
```

```python
import functools

import jax
import jax.numpy as jnp
import numpy as np
from jax import lax
from jax.experimental import pallas as pl
from jax.experimental.pallas import tpu as pltpu
from jax.sharding import Mesh, PartitionSpec as P

LAYERS = 2
D = 768
TOK = 128
CTX_DEV = 8
SLOTS = TOK * CTX_DEV
DATA = ("y", "zh", "c")
CTX = ("x", "zl")
ALL = DATA + CTX
bf16 = jnp.bfloat16
f32 = jnp.float32
norm_eps = 1e-05
score_scale = 0.125
hidden_value = -1000000000.0


def coord(bit_b, bit_a, core):
    return core * (2 * bit_b + bit_a) + (1 - core) * (3 * bit_a + bit_b * (1 - 2 * bit_a))


def place(n, core):
    y = coord((n >> 5) & 1, (n >> 2) & 1, core)
    z = coord((n >> 4) & 1, (n >> 1) & 1, core)
    x = coord((n >> 3) & 1, n & 1, core)
    return (y * 2 + (z >> 1)) * 2 + core, x * 2 + (z & 1)


SLOT_OF = {(c,) + place(n, c): n for c in range(2) for n in range(64)}


def tail_order():
    table = np.zeros((128, 128), np.float32)
    for (c, row, triple), n in SLOT_OF.items():
        table[row * 8 + triple, 64 * c + n] = 1.0
    return table


TAIL_ORDER = tail_order()


def device_id(y, z, core, x):
    return y * 32 + (z >> 1) * 16 + core * 8 + x * 2 + (z & 1)


def cube_groups(level):
    found = {}
    for core in range(2):
        for n in range(64):
            bits = [(n >> s) & 1 for s in range(6)]
            y, z, x = (coord(bits[3 + s], bits[s], core) for s in (2, 1, 0))
            if level == 1:
                key = (core,) + tuple(coord(bits[3 + s], 0, core) for s in (2, 1, 0))
                slot = n & 7
            else:
                pair = [coord(bits[3 + s], bits[s], core) for s in (2, 1, 0)]
                pair = [(v // 2 if core == 0 else ((v + 1) // 2) % 2) for v in pair]
                key = (core,) + tuple(pair)
                slot = n >> 3
            found.setdefault(key, [None] * 8)[slot] = device_id(y, z, core, x)
    return [found[k] for k in sorted(found)]


GROUPS_A = cube_groups(1)
GROUPS_B = cube_groups(0)


def ff_order():
    used = np.arange(384)
    block, q, ctx, r = used // 192, used // 48 % 4, used // 6 % 8, used % 6
    table = np.zeros((384, 384), np.float32)
    table[block * 192 + ctx * 24 + q * 6 + r, used] = 1.0
    return table


FF_ORDER = ff_order()


def fetch_cube(core_ref, mine, theirs, offset, w, sem, low, high):
    core = core_ref[0]

    def step(n, carry):
        for src, own in ((mine, core), (theirs, 1 - core)):
            row, triple = place(n, own)

            @pl.when((triple >= low) & (triple < high))
            def _():
                pltpu.make_async_copy(
                    src.at[n, pl.ds(offset, 9)], w.at[row, pl.ds((triple - low) * 9, 9)], sem).start()

        return carry

    lax.fori_loop(0, 64, step, 0)


COMES = {(0, 0): ("cube", 0), (0, 1): ("cube", 0), (0, 2): ("plain", 0),
         (1, 0): ("cube", 9), (1, 1): ("plain", 0), (1, 2): ("plain", 72)}


def fetch(layer, group, core_ref, sources, w, sem, low, high):
    kind, first = COMES[layer, group]
    if kind == "cube":
        fetch_cube(core_ref, sources[0], sources[1], first, w, sem, low, high)
    else:
        tiles = pl.ds(first + 9 * low, 9 * (high - low))
        pltpu.make_async_copy(sources[0].at[:, tiles], w, sem).start()


def sources_of(layer, groups, refs):
    out, at = {}, 0
    for group in groups:
        n = 2 if COMES[layer, group][0] == "cube" else 1
        out[group] = refs[at : at + n]
        at += n
    return out, refs[at:]


def arrived(w, sem):
    pltpu.make_async_copy(w, w, sem).wait()


def units(w, first, count):
    parts = [w[:, 3 * (first + i) : 3 * (first + i) + 3].reshape(D, 128) for i in range(count)]
    return parts[0] if count == 1 else jnp.concatenate(parts, axis=1)


def tall_units(w, cb):
    return w[:, 12 * cb : 12 * cb + 12].reshape(4 * D, 128)


def mul(a, b):
    return jnp.dot(a, b, preferred_element_type=f32)


def mul_t(a, b):
    return lax.dot_general(a, b, (((1,), (1,)), ((), ())), preferred_element_type=f32)


def t_mul(a, b):
    return lax.dot_general(a, b, (((0,), (0,)), ((), ())), preferred_element_type=f32)


def norm_parts(values):
    centre = values - jnp.mean(values, axis=-1, keepdims=True)
    var = jnp.mean(centre * centre, axis=-1, keepdims=True)
    r = lax.rsqrt(var + norm_eps)
    return centre * r, r


def norm_back(cot, gain, xh, r):
    cg = cot * gain
    return r * (cg - jnp.mean(cg, axis=-1, keepdims=True) - xh * jnp.mean(cg * xh, axis=-1, keepdims=True))


def rows_sum(values):
    return jnp.sum(values, axis=0, keepdims=True)


def windows(values):
    out = []
    for x in range(4):
        for zl in range(2):
            own, shared = 3 * x + 2 * zl, 3 * x + 1
            out.append(jnp.concatenate([values[:, 64 * own : 64 * own + 64],
                                        values[:, 64 * shared : 64 * shared + 64]], axis=1))
    return out


def unwindow(get):
    parts = []
    for x in range(4):
        lo, hi = get(2 * x), get(2 * x + 1)
        parts += [lo[:, :64], lo[:, 64:] + hi[:, 64:], hi[:, :64]]
    return jnp.concatenate(parts, axis=1)


def gelu_both(u):
    k = 0.7978845608028654
    t = jnp.tanh(k * (u + 0.044715 * u * u * u))
    half = 0.5 * (1.0 + t)
    return u * half, half + 0.5 * u * (1.0 - t * t) * (k * (1.0 + 3 * 0.044715 * u * u))


def project_kernel(layer, core, h_ref, vec, *refs):
    src, (a1_ref, pay_ref, w, sem) = sources_of(layer, (0,), refs)
    fetch(layer, 0, core, src[0], w, sem, 0, 6)
    xh, _ = norm_parts(h_ref[...].astype(f32))
    a1 = (xh * vec[0:1] + vec[1:2]).astype(bf16)
    a1_ref[...] = a1
    arrived(w, sem)
    for part in range(3):
        cols = [mul(a1, units(w, 6 * part + 2 * j, 2)) for j in range(3)]
        got = jnp.concatenate(cols, axis=1)
        if part != 1:
            got = got + vec[2 + part // 2 : 3 + part // 2]
        got = got.astype(bf16).astype(f32)
        for d, win in enumerate(windows(got)):
            pay_ref[d, :, 128 * part : 128 * part + 128] = win.astype(bf16)


def visible_of(block, count, idc_ref, idr_ref):
    n = count * TOK
    qpos = block * TOK + lax.broadcasted_iota(jnp.int32, (TOK, n), 0)
    kpos = lax.broadcasted_iota(jnp.int32, (TOK, n), 1)
    return (idc_ref[block] == idr_ref[:, 0:n]) & (kpos <= qpos)


def head_blocks(par):
    for i in range(4):
        yield i, ((0, 2 * i, 2 * i + 1), (0, 2 * i + 1, 2 * i + 2), (1, 2 * i + par, 2 * i + 2))


def half(values, head):
    return values[:, 64 * head : 64 * head + 64]


def store_pair(out, lanes, i, par, parts):
    for k in range(2):
        shared = jnp.where(par == k, parts[2], 0.0)
        out[2 * i + k, :, lanes] = jnp.concatenate([parts[k], shared], axis=1).astype(bf16)


def weights_of(q, key, seen):
    s = jnp.where(seen, mul_t(q, key) * score_scale, hidden_value)
    e = jnp.exp(s - jnp.max(s, axis=1, keepdims=True))
    return e / jnp.sum(e, axis=1, keepdims=True)


def attend_kernel(par_ref, heads, idc, idr, out):
    par = par_ref[0]
    key = heads[:, :, 128:256].reshape(SLOTS, 128)
    val = heads[:, :, 256:384].reshape(SLOTS, 128)
    keys, vals = [half(key, h) for h in range(2)], [half(val, h) for h in range(2)]
    for i, blocks in head_blocks(par):
        parts = []
        for head, block, count in blocks:
            n = count * TOK
            q = half(heads[block, :, 0:128], head)
            p = weights_of(q, keys[head][:n], visible_of(block, count, idc, idr)).astype(bf16)
            parts.append(mul(p, vals[head][:n]))
        store_pair(out, slice(0, 128), i, par, parts)


def attend_back_kernel(par_ref, heads, cot, idc, idr, out, dk_acc, dv_acc):
    par = par_ref[0]
    key = heads[:, :, 128:256].reshape(SLOTS, 128)
    val = heads[:, :, 256:384].reshape(SLOTS, 128)
    keys, vals = [half(key, h) for h in range(2)], [half(val, h) for h in range(2)]
    dk_acc[...] = jnp.zeros_like(dk_acc)
    dv_acc[...] = jnp.zeros_like(dv_acc)
    for i, blocks in head_blocks(par):
        parts = []
        for head, block, count in blocks:
            n = count * TOK
            q = half(heads[block, :, 0:128], head)
            g = half(cot[block], head)
            p = weights_of(q, keys[head][:n], visible_of(block, count, idc, idr))
            dp = mul_t(g, vals[head][:n])
            ds = (p * (dp - jnp.sum(p * dp, axis=1, keepdims=True))).astype(bf16)
            parts.append(mul(ds, keys[head][:n]) * score_scale)
            dk_acc[head, 0:n] += t_mul(ds, q)
            dv_acc[head, 0:n] += t_mul(p.astype(bf16), g)
        store_pair(out, slice(0, 128), i, par, parts)
    dk = jnp.concatenate([dk_acc[0], dk_acc[1]], axis=1) * score_scale
    dv = jnp.concatenate([dv_acc[0], dv_acc[1]], axis=1)
    out[:, :, 128:256] = dk.astype(bf16).reshape(8, TOK, 128)
    out[:, :, 256:384] = dv.astype(bf16).reshape(8, TOK, 128)


def forward_kernel(layer, core, h_ref, back, vec, upb, *refs):
    src, (o_ref, h1_ref, a2_ref, u_ref, next_ref, wo, wu, wd, sems) = sources_of(layer, (0, 1, 2), refs)
    fetch(layer, 0, core, src[0], wo, sems.at[0], 6, 8)
    fetch(layer, 1, core, src[1], wu, sems.at[1], 0, 8)
    fetch(layer, 2, core, src[2], wd, sems.at[2], 0, 8)
    o = unwindow(lambda d: back[d].astype(f32)).astype(bf16)
    o_ref[...] = o
    arrived(wo, sems.at[0])
    got = jnp.concatenate([mul(o, units(wo, 2 * j, 2)) for j in range(3)], axis=1)
    h1 = h_ref[...].astype(f32) + got + vec[2:3]
    h1_ref[...] = h1
    xh, _ = norm_parts(h1)
    a2 = (xh * vec[0:1] + vec[1:2]).astype(bf16)
    a2_ref[...] = a2
    arrived(wu, sems.at[1])
    acts = []
    for j in range(12):
        u = mul(a2, units(wu, 2 * j, 2)) + upb[:, 256 * j : 256 * j + 256]
        u_ref[:, 256 * j : 256 * j + 256] = u
        acts.append(gelu_both(u)[0].astype(bf16))
    f = jnp.concatenate(acts, axis=1)
    arrived(wd, sems.at[2])
    for j in range(3):
        w = jnp.concatenate([tall_units(wd, 2 * j), tall_units(wd, 2 * j + 1)], axis=1)
        c = slice(256 * j, 256 * j + 256)
        next_ref[:, c] = (h1[:, c] + mul(f, w) + vec[3:4, c]).astype(next_ref.dtype)


def backward_kernel(layer, core, e_ref, u_ref, h1_ref, vec, *refs):
    src, (f_ref, du_ref, e1_ref, pay_ref, small_ref, upb_ref, wo, wu, wd, sems) = sources_of(layer, (0, 1, 2), refs)
    fetch(layer, 2, core, src[2], wd, sems.at[2], 0, 8)
    fetch(layer, 1, core, src[1], wu, sems.at[1], 0, 8)
    fetch(layer, 0, core, src[0], wo, sems.at[0], 6, 8)
    e = e_ref[...].astype(f32)
    e2 = e.astype(bf16)
    arrived(wd, sems.at[2])
    df = jnp.zeros((TOK, 4 * D), f32)
    for j in range(3):
        w = jnp.concatenate([tall_units(wd, 2 * j), tall_units(wd, 2 * j + 1)], axis=1)
        df = df + mul_t(e2[:, 256 * j : 256 * j + 256], w)
    arrived(wu, sems.at[1])
    cot = jnp.zeros((TOK, D), f32)
    for j in range(12):
        c = slice(256 * j, 256 * j + 256)
        f, slope = gelu_both(u_ref[:, c])
        f_ref[:, c] = f.astype(bf16)
        du = (df[:, c] * slope).astype(bf16)
        du_ref[:, c] = du
        upb_ref[:, c] = rows_sum(du.astype(f32))
        cot = cot + mul_t(du, units(wu, 2 * j, 2))
    xh, r = norm_parts(h1_ref[...])
    e1 = e + norm_back(cot, vec[0:1], xh, r)
    e1_ref[...] = e1
    b1 = e1.astype(bf16)
    small_ref[0:1] = rows_sum(cot * xh)
    small_ref[1:2] = rows_sum(cot)
    small_ref[2:3] = rows_sum(b1.astype(f32))
    small_ref[3:4] = rows_sum(e2.astype(f32))
    arrived(wo, sems.at[0])
    do = jnp.zeros((TOK, D), f32)
    for j in range(3):
        do = do + mul_t(b1[:, 256 * j : 256 * j + 256], units(wo, 2 * j, 2))
    do = do.astype(bf16).astype(f32)
    for d, win in enumerate(windows(do)):
        pay_ref[d] = win.astype(bf16)


def back_project_kernel(layer, core, back, e1_ref, h_ref, vec, *refs):
    src, (g_ref, e_ref, small_ref, w, sem) = sources_of(layer, (0,), refs)
    fetch(layer, 0, core, src[0], w, sem, 0, 6)
    for part in range(3):
        got = unwindow(lambda d: back[d, :, 128 * part : 128 * part + 128].astype(f32)).astype(bf16)
        g_ref[:, D * part : D * part + D] = got
        if part != 1:
            small_ref[2 + part // 2 : 3 + part // 2] = rows_sum(got.astype(f32))
    arrived(w, sem)
    cot = jnp.zeros((TOK, D), f32)
    for j in range(9):
        cot = cot + mul_t(g_ref[:, 256 * j : 256 * j + 256], units(w, 2 * j, 2))
    xh, r = norm_parts(h_ref[...].astype(f32))
    small_ref[0:1] = rows_sum(cot * xh)
    small_ref[1:2] = rows_sum(cot)
    e_ref[...] = e1_ref[...] + norm_back(cot, vec[0:1], xh, r)


def cube_store(core, stage, first_tile, triple, k, rows):
    for row in range(16):
        target = row & 1
        tile = first_tile + 3 * k
        stage[core ^ target, SLOT_OF[(target, row, triple)], tile : tile + 3] = rows[row].reshape(3, 16, 128)


def plain_store(stage, unit, rows):
    stage[:, 3 * unit : 3 * unit + 3] = rows.reshape(16, 3, 16, 128)


def wide_grad(at, b, first, store):
    for j in range(b.shape[1] // D):
        wide = mul(at, b[:, D * j : D * j + D])
        for i in range(6):
            store(first + 6 * j + i, wide[:, 128 * i : 128 * i + 128].astype(bf16).reshape(16, 48, 128))


def tall_grad(ft, b, store):
    for j in range(3):
        wide = mul(ft, b[:, 256 * j : 256 * j + 256])
        for i in range(2):
            rows = wide[:, 128 * i : 128 * i + 128].astype(bf16).reshape(16, 4, 48, 128)
            for q in range(4):
                store(4 * (2 * j + i) + q, rows[:, q])


def low(ref):
    return ref[...].astype(f32).astype(bf16)


def ship(pairs, sem):
    copies = [pltpu.make_async_copy(src, dst, sem.at[k]) for k, (src, dst) in enumerate(pairs)]
    for copy in copies:
        copy.start()
    for copy in copies:
        copy.wait()


def grad_mlp_cube(core_ref, f_ref, e_ref, a2_ref, du_ref, keep, send, stage, sem):
    core = core_ref[0]
    tall_grad(f_ref[...].T, low(e_ref), lambda u, rows: cube_store(core, stage, 9, u // 3, u % 3, rows))
    wide_grad(a2_ref[...].T, du_ref[...], 0, lambda u, rows: cube_store(core, stage, 0, u // 3, u % 3, rows))
    ship(((stage.at[0], keep), (stage.at[1], send)), sem)


def grad_joint_cube(core_ref, a_ref, g_ref, o_ref, e1_ref, keep, send, stage, sem):
    core = core_ref[0]
    put = lambda u, rows: cube_store(core, stage, 0, u // 3, u % 3, rows)
    wide_grad(a_ref[...].T, g_ref[...], 0, put)
    wide_grad(o_ref[...].T, low(e1_ref), 18, put)
    ship(((stage.at[0], keep), (stage.at[1], send)), sem)


def grad_down_plain(f_ref, e_ref, out, stage, sem):
    tall_grad(f_ref[...].T, low(e_ref), lambda u, rows: plain_store(stage, u, rows))
    ship(((stage, out),), sem)


def grad_up_cube(core_ref, a2_ref, du_ref, keep, send, stage, sem):
    core = core_ref[0]
    wide_grad(a2_ref[...].T, du_ref[...], 0, lambda u, rows: cube_store(core, stage, 0, u // 3, u % 3, rows))
    ship(((stage.at[0], keep), (stage.at[1], send)), sem)


CUBE_IN, PLAIN_IN = ((0, 0), (0, 1), (1, 0)), ((0, 2), (1, 1), (1, 2))
CUBE_OUT = ((0, 0), (0, 1), (0, 2), (1, 0), (1, 1))


def pack_kernel(win, wout, wup, wdown, order, pay):
    ups = []
    for l in range(LAYERS):
        up = [mul(wup[l, :, 384 * m : 384 * m + 384], order[...]) for m in range(8)]
        ups.append(jnp.concatenate(up, axis=1).astype(bf16))

    def get(l, group, u):
        if group == 0:
            return win[l, :, 128 * u : 128 * u + 128] if u < 18 else wout[l, :, 128 * (u - 18) : 128 * (u - 17)]
        if group == 1:
            return ups[l][:, 128 * u : 128 * u + 128]
        cb, q = divmod(u, 4)
        return wdown[l, 6 * q : 6 * q + 6, 128 * cb : 128 * cb + 128]

    for u in range(24):
        for k, key in enumerate(CUBE_IN):
            pay[u // 3, 3 * k + u % 3, 0:6] = get(*key, u)
        for k, key in enumerate(PLAIN_IN):
            rows = get(*key, u)
            for d in range(8):
                pay[d, 9 + 24 * k + u, 0:6] = rows


def join_rows(got, u):
    rows = jnp.concatenate([got[d, u].astype(f32)[0:6] for d in range(8)], axis=0)
    return rows.astype(bf16).reshape(3, 16, 128)


def regroup_kernel(got, smalls, first, third, fourth):
    for u in range(3):
        first[3 * u : 3 * u + 3] = join_rows(got, u)
    first[9] = smalls[...]
    for u in range(3, 9):
        first[3 * u + 1 : 3 * u + 4] = join_rows(got, u)
    for u in range(24):
        third[3 * u : 3 * u + 3] = join_rows(got, 9 + u)
    for u in range(48):
        fourth[3 * u : 3 * u + 3] = join_rows(got, 33 + u)


def smalls_kernel(core_ref, mine, theirs, vecs, few, buf, sem):
    core = core_ref[0]

    def step(n, carry):
        for src, own in ((mine, core), (theirs, 1 - core)):
            row, triple = place(n, own)
            pltpu.make_async_copy(src.at[n, 9], buf.at[row * 8 + triple], sem).start()
        return carry

    lax.fori_loop(0, 64, step, 0)
    pltpu.make_async_copy(buf, buf, sem).wait()
    rows = buf[...].astype(f32)
    low_part, high_part = rows[:, 0], rows[:, 1]
    few[:, 0:128] = low_part
    few[:, 128:256] = high_part
    low_part = low_part.astype(bf16)
    value = lax.broadcasted_iota(jnp.int32, (128, 16), 0) - 6 * lax.broadcasted_iota(jnp.int32, (128, 16), 1)
    place_in = lax.broadcasted_iota(jnp.int32, (128, D), 1) - 6 * lax.broadcasted_iota(jnp.int32, (128, D), 0)
    total = jnp.zeros((16, D), f32)
    for i in range(6):
        picked = mul(low_part, (value == i).astype(f32).astype(bf16)).astype(bf16)
        total = total + t_mul(picked, (place_in == i).astype(f32).astype(bf16))
    vecs[...] = total


def split_rows(out, u, rows):
    for d in range(8):
        part = jnp.concatenate([rows[6 * d : 6 * d + 6], jnp.zeros((2, 128), f32)], axis=0)
        out[d, u] = part.astype(bf16)


def finish_kernel(parts, total, out, few):
    small = jnp.zeros((2, 128), f32)
    for k in range(8):
        small = small + parts[k, 9].astype(f32)[0:2]
    few[...] = small
    for u in range(24):
        split_rows(out, 15 + u, total[3 * u : 3 * u + 3].reshape(48, 128).astype(f32))
    for u in range(15):
        tile = 3 * u if u < 3 else 3 * u + 1
        rows = jnp.zeros((48, 128), f32)
        for k in range(8):
            rows = rows + parts[k, tile : tile + 3].reshape(48, 128).astype(f32)
        split_rows(out, u, rows)


def unpack_kernel(got, order, g_in, g_out, g_up, g_down):
    for l in range(LAYERS):
        for group in range(3):
            ups = []
            for u in range(24):
                if (l, group) in CUBE_OUT:
                    rows = got[u // 3, 3 * CUBE_OUT.index((l, group)) + u % 3].astype(f32)
                else:
                    rows = got[0, 15 + u].astype(f32)
                    for d in range(1, 8):
                        rows = rows + got[d, 15 + u].astype(f32)
                rows = rows[0:6]
                if group == 0 and u < 18:
                    g_in[l, :, 128 * u : 128 * u + 128] = rows
                elif group == 0:
                    g_out[l, :, 128 * (u - 18) : 128 * (u - 17)] = rows
                elif group == 1:
                    ups.append(rows)
                else:
                    cb, q = divmod(u, 4)
                    g_down[l, 6 * q : 6 * q + 6, 128 * cb : 128 * cb + 128] = rows
            for m in range(len(ups) // 3):
                left = jnp.concatenate(ups[3 * m : 3 * m + 3], axis=1)
                wide = jnp.zeros((6, 384), f32)
                for _ in range(3):
                    term = left.astype(bf16)
                    left = left - term.astype(f32)
                    wide = wide + mul_t(term, order[...])
                g_up[l, :, 384 * m : 384 * m + 384] = wide


def call(kernel, outs, ins, scratch=(), us=3, out_spaces=None, aliases=None):
    spaces = {"s": pltpu.SMEM, "v": pltpu.VMEM, "a": pl.ANY}
    return pl.pallas_call(
        kernel,
        out_shape=[jax.ShapeDtypeStruct(*o) for o in outs],
        in_specs=[pl.BlockSpec(memory_space=spaces[m]) for _, m in ins],
        out_specs=[pl.BlockSpec(memory_space=spaces[m]) for m in (out_spaces or "v" * len(outs))],
        scratch_shapes=list(scratch),
        input_output_aliases=aliases or {},
        compiler_params=pltpu.CompilerParams(vmem_limit_bytes=56 * 1024 * 1024),
        cost_estimate=pl.CostEstimate(flops=0, bytes_accessed=us * 3690000, transcendentals=0),
    )(*[a for a, _ in ins])


def w_scratch(count):
    return pltpu.VMEM((16, 3 * count, 16, 128), bf16)


DMA = pltpu.SemaphoreType.DMA


def after(values, *others):
    return lax.optimization_barrier((values,) + others)[0]


def copies(values, groups):
    many = jnp.broadcast_to(values[None], (8,) + values.shape)
    return lax.all_to_all(many, ALL, 0, 0, axis_index_groups=groups)


def sum_first(values):
    return jnp.sum(values.astype(f32), axis=0)


def swap_core(values):
    return lax.ppermute(values, "c", [(0, 1), (1, 0)])


def cube_copies(shards):
    return copies(shards, GROUPS_B).reshape((64,) + shards.shape[1:])


def spread(shards):
    mine = cube_copies(shards)
    return mine, swap_core(mine)


def add_kernel(*refs):
    out, first = refs[-1], 0
    for keep, got in zip(refs[0:-1:2], refs[1:-1:2]):
        n = keep.shape[1]
        out[:, first : first + n] = (keep[...].astype(f32) + got[...].astype(f32)).astype(bf16)
        first += n


def add_pairs(pairs):
    total = sum(a.shape[1] for a, _ in pairs)
    flat = [v for pair in pairs for v in pair]

    def spec(t):
        return pl.BlockSpec((8, t, 16, 128), lambda i: (i, 0, 0, 0))

    return pl.pallas_call(
        add_kernel,
        grid=(8,),
        out_shape=jax.ShapeDtypeStruct((64, total, 16, 128), bf16),
        in_specs=[spec(v.shape[1]) for v in flat],
        out_specs=spec(total),
        compiler_params=pltpu.CompilerParams(vmem_limit_bytes=56 * 1024 * 1024),
        cost_estimate=pl.CostEstimate(flops=2**22, bytes_accessed=3 * 64 * total * 4096, transcendentals=0),
    )(*flat)


def core_sums(pairs):
    return add_pairs([(keep, swap_core(send)) for keep, send in pairs])


def gather_sums(part):
    part = part.reshape((8, 8) + part.shape[1:])
    return sum_first(lax.all_to_all(part, ALL, 0, 0, axis_index_groups=GROUPS_B)).astype(bf16)


def token_ids(group_index, positions, sequence_group, sequence_start, sequence_length):
    member = (
        (sequence_group[None, :] == group_index)
        & (sequence_start[None, :] <= positions[:, None])
        & (positions[:, None] < (sequence_start + sequence_length)[None, :])
    )
    numbers = jnp.arange(sequence_group.shape[0], dtype=jnp.int32) + 1
    located = jnp.sum(jnp.where(member, numbers[None, :], 0), axis=1)
    return jnp.where(located > 0, located - 1, -1 - positions)


def body(hidden_in, out_grad, sequence_group, sequence_start, sequence_length, norm_gain, norm_bias,
         input_weight, input_bias, output_weight, branch_bias, up_weight, up_bias, down_weight):
    core = lax.axis_index("c").astype(jnp.int32).reshape(1)
    par = lax.axis_index("zl").astype(jnp.int32).reshape(1)
    positions = jnp.arange(SLOTS, dtype=jnp.int32)
    ids = token_ids(lax.axis_index(DATA), positions, sequence_group, sequence_start, sequence_length)
    idc, idr = ids.reshape(CTX_DEV, TOK, 1), ids.reshape(1, SLOTS)

    order = jnp.asarray(FF_ORDER, bf16)
    smalls = jnp.concatenate([v.reshape(-1) for v in (norm_gain, norm_bias, input_bias, branch_bias, up_bias)])
    smalls = jnp.pad(smalls, (0, 2048 - 144)).reshape(16, 128)
    (pay,) = call(pack_kernel, [((8, 81, 8, 128), bf16)],
                  [(input_weight, "v"), (output_weight, "v"), (up_weight, "v"), (down_weight, "v"), (order, "v")])
    got = lax.all_to_all(pay, CTX, 0, 0)
    first, third, fourth = call(
        regroup_kernel,
        [((28, 16, 128), bf16), ((72, 16, 128), bf16), ((144, 16, 128), bf16)],
        [(got, "v"), (smalls, "v")])
    down_0 = lax.all_gather(third, DATA, axis=0, tiled=False)
    shards = copies(first, GROUPS_A)
    group_e, shards = spread(shards[:, :10]), shards[:, 10:]
    sources = {(0, 0): group_e, (0, 2): (down_0,)}

    vecs, few = call(
        smalls_kernel, [((16, D), f32), ((128, 256), f32)],
        [(core, "s"), (group_e[0], "a"), (group_e[1], "a")],
        [pltpu.VMEM((128, 16, 128), bf16), DMA], us=2)
    ups = few[:, 96:144].reshape(16, 8, 2, 4, 6).transpose(2, 0, 3, 1, 4).reshape(2, 4 * D)

    def vec(*index):
        return jnp.concatenate([vecs[i : i + 1] for i in index], axis=0)

    def weights(l, all_groups):
        return [(w, "a") for group in range(3 if all_groups else 1) for w in sources[l, group]]

    hidden = hidden_in[0]
    stored = []
    for l in range(LAYERS):
        a1, pay = call(
            functools.partial(project_kernel, l),
            [((TOK, D), bf16), ((8, TOK, 384), bf16)],
            [(core, "s"), (hidden, "v"), (vec(2 * l, 4 + 2 * l, 8 + 2 * l, 9 + 2 * l), "v")] + weights(l, False),
            [w_scratch(18), DMA],
            us=5)
        if l == 0:
            both_1 = lax.all_gather(after(fourth, a1), DATA, axis=0, tiled=False)
            sources[1, 1] = sources[1, 2] = (both_1,)
        heads = lax.all_to_all(pay, CTX, 0, 0)
        if l == 0:
            mine = cube_copies(after(shards, heads, down_0))
        (mix,) = call(
            attend_kernel,
            [((8, TOK, 128), bf16)],
            [(par, "s"), (heads, "v"), (idc, "v"), (idr, "v")],
            us=7)
        if l == 0:
            theirs = swap_core(after(mine, mix))
            for key in CUBE_IN[1:]:
                sources[key] = (mine, theirs)
        mix = after(mix, mine if l == 0 else both_1)
        back = lax.all_to_all(mix, CTX, 0, 0)
        o, h1, a2, u, following = call(
            functools.partial(forward_kernel, l),
            [((TOK, D), bf16), ((TOK, D), f32), ((TOK, D), bf16), ((TOK, 4 * D), f32),
             ((TOK, D), f32 if l == 0 else bf16)],
            [(core, "s"), (hidden, "v"), (back, "v"), (vec(2 * l + 1, 5 + 2 * l, 12 + 2 * l, 13 + 2 * l), "v"),
             (ups[l : l + 1], "v")] + weights(l, True),
            [w_scratch(6), w_scratch(24), w_scratch(24), DMA((3,))],
            us=8)
        stored.append((hidden, a1, heads, o, h1, a2, u))
        hidden = following

    def grad_joint(g, a1, o, e1):
        return call(
            grad_joint_cube, [((64, 9, 16, 128), bf16)] * 2,
            [(core, "s"), (a1, "v"), (g, "v"), (o, "v"), (e1, "v")],
            [pltpu.VMEM((2, 64, 9, 16, 128), bf16), DMA((2,))], us=5, out_spaces="aa")

    grad = out_grad[0]
    few_rows, few_up = [None] * 2, [None] * 2
    for l in reversed(range(LAYERS)):
        layer_in, a1, heads, o, h1, a2, u = stored[l]
        f, du, e1, pay, small_b, small_u = call(
            functools.partial(backward_kernel, l),
            [((TOK, 4 * D), bf16), ((TOK, 4 * D), bf16), ((TOK, D), f32), ((8, TOK, 128), bf16),
             ((4, D), f32), ((1, 4 * D), f32)],
            [(core, "s"), (grad, "v"), (u, "v"), (h1, "v"), (vec(2 * l + 1), "v")] + weights(l, True),
            [w_scratch(6), w_scratch(24), w_scratch(24), DMA((3,))],
            us=10)
        if l == 0:
            sums_up = gather_sums(after(up_1, back2))
            pay = after(pay, sums_up)
            f = after(f, sums_up)
        cot = lax.all_to_all(pay, CTX, 0, 0)
        if l == 1:
            (down_1,) = call(
                grad_down_plain, [((16, 72, 16, 128), bf16)], [(f, "v"), (grad, "v")],
                [w_scratch(24), DMA((1,))], us=5, out_spaces="a")
            up_1 = call(
                grad_up_cube, [((64, 9, 16, 128), bf16)] * 2, [(core, "s"), (a2, "v"), (du, "v")],
                [pltpu.VMEM((2, 64, 9, 16, 128), bf16), DMA((2,))], us=5, out_spaces="aa")
        else:
            keep_ud, send_ud = call(
                grad_mlp_cube, [((64, 18, 16, 128), bf16)] * 2,
                [(core, "s"), (f, "v"), (grad, "v"), (a2, "v"), (du, "v")],
                [pltpu.VMEM((2, 64, 18, 16, 128), bf16), DMA((2,))],
                us=9, out_spaces="aa")
        if l == 0:
            send_ud = after(send_ud, cot)
            joint_1 = grad_joint(after(saved[0], cot), *saved[1:])
        else:
            scattered = lax.psum_scatter(after(down_1, cot), DATA, scatter_dimension=0, tiled=False)
        cot = after(cot, down_1 if l == 1 else keep_ud)
        (pay2,) = call(
            attend_back_kernel,
            [((8, TOK, 384), bf16)],
            [(par, "s"), (heads, "v"), (cot, "v"), (idc, "v"), (idr, "v")],
            [pltpu.VMEM((2, SLOTS, 64), f32)] * 2,
            us=10)
        if l == 0:
            pay2 = after(pay2, scattered)
        back2 = lax.all_to_all(pay2, CTX, 0, 0)
        if l == 1:
            up_1 = core_sums([up_1])
            back2 = after(back2, up_1)
        else:
            middle = core_sums([(keep_ud, send_ud), joint_1])
            back2 = after(back2, middle)
        g, grad, small_a = call(
            functools.partial(back_project_kernel, l),
            [((TOK, 3 * D), bf16), ((TOK, D), f32), ((4, D), f32)],
            [(core, "s"), (back2, "v"), (e1, "v"), (layer_in, "v"), (vec(2 * l), "v")] + weights(l, False),
            [w_scratch(18), DMA],
            us=6)
        if l == 1:
            saved = (g, a1, o, e1)
        else:
            joint_0 = grad_joint(g, a1, o, e1)
        few_rows[l] = jnp.concatenate([small_a[0:1], small_b[0:1], small_a[1:2], small_b[1:2], small_a[2:4],
                                       small_b[2:4]], axis=0)
        few_up[l] = small_u

    few = jnp.concatenate([r.reshape(8, 128, 6).transpose(1, 0, 2).reshape(128, 48) for r in few_rows]
                          + [r.reshape(16, 4, 8, 6).transpose(0, 2, 1, 3).reshape(128, 24) for r in few_up], axis=1)
    few = jnp.pad(few, ((0, 0), (0, 256 - 144))).astype(bf16)
    few = jnp.dot(jnp.asarray(TAIL_ORDER.T, bf16), few, preferred_element_type=f32).astype(bf16)
    few = jnp.pad(few.reshape(2, 64, 1, 2, 128), ((0, 0),) * 3 + ((0, 14), (0, 0)))
    few = [jnp.where(core[0] == k, few[0], few[1]) for k in range(2)]

    middle = gather_sums(middle)
    last = gather_sums(after(core_sums([joint_0, few]), middle))
    sums = jnp.concatenate([last, middle, sums_up], axis=1)
    sums = lax.all_to_all(sums, ALL, 0, 0, axis_index_groups=GROUPS_A)
    sums, few = call(finish_kernel, [((8, 39, 8, 128), bf16), ((2, 128), f32)],
                     [(sums, "v"), (scattered, "v")])
    got = lax.all_to_all(sums, CTX, 0, 0)
    grad_in, grad_out, grad_up, grad_down = call(
        unpack_kernel,
        [((2, 6, 3 * D), f32), ((2, 6, D), f32), ((2, 6, 4 * D), f32), ((2, 24, D), f32)],
        [(got, "v"), (order, "v")])
    few = few.reshape(256)
    few_l = [few[48 * l : 48 * l + 48].reshape(4, 2, 6) for l in range(2)]

    def pair(k):
        return jnp.stack([few_l[0][k], few_l[1][k]])

    return (
        hidden[None],
        grad[None],
        pair(0),
        pair(1),
        grad_in,
        pair(2),
        grad_out,
        pair(3),
        grad_up,
        few[96:144].reshape(2, 24),
        grad_down,
    )


def solution(mesh):
    mesh = Mesh(mesh.devices.reshape(4, 2, 2, 4, 2), ALL)
    token = P(DATA, CTX, None)
    one = P(None, ALL)
    two = P(None, None, ALL)
    mat = P(None, ALL, None)
    return jax.shard_map(
        body,
        mesh=mesh,
        in_specs=(token, token, P(), P(), P(), two, two, mat, two, mat, two, mat, one, mat),
        out_specs=(token, token, two, two, mat, two, mat, two, mat, one, mat),
        check_vma=False,
    )
```

```python
import functools

import jax
import jax.numpy as jnp
import numpy as np
from jax import lax
from jax.experimental import pallas as pl
from jax.experimental.pallas import tpu as pltpu
from jax.sharding import Mesh, PartitionSpec as P

LAYERS = 2
D = 768
TOK = 128
CTX_DEV = 8
SLOTS = TOK * CTX_DEV
DATA = ("y", "zh", "c")
CTX = ("x", "zl")
ALL = DATA + CTX
bf16 = jnp.bfloat16
f32 = jnp.float32
norm_eps = 1e-05
score_scale = 0.125
hidden_value = -1000000000.0


def coord(bit_b, bit_a, core):
    return core * (2 * bit_b + bit_a) + (1 - core) * (3 * bit_a + bit_b * (1 - 2 * bit_a))


def place(n, core):
    y = coord((n >> 5) & 1, (n >> 2) & 1, core)
    z = coord((n >> 4) & 1, (n >> 1) & 1, core)
    x = coord((n >> 3) & 1, n & 1, core)
    return (y * 2 + (z >> 1)) * 2 + core, x * 2 + (z & 1)


SLOT_OF = {(c,) + place(n, c): n for c in range(2) for n in range(64)}


def tail_order():
    table = np.zeros((128, 128), np.float32)
    for (c, row, triple), n in SLOT_OF.items():
        table[row * 8 + triple, 64 * c + n] = 1.0
    return table


TAIL_ORDER = tail_order()


def device_id(y, z, core, x):
    return y * 32 + (z >> 1) * 16 + core * 8 + x * 2 + (z & 1)


def cube_groups(level):
    found = {}
    for core in range(2):
        for n in range(64):
            bits = [(n >> s) & 1 for s in range(6)]
            y, z, x = (coord(bits[3 + s], bits[s], core) for s in (2, 1, 0))
            if level == 1:
                key = (core,) + tuple(coord(bits[3 + s], 0, core) for s in (2, 1, 0))
                slot = n & 7
            else:
                pair = [coord(bits[3 + s], bits[s], core) for s in (2, 1, 0)]
                pair = [(v // 2 if core == 0 else ((v + 1) // 2) % 2) for v in pair]
                key = (core,) + tuple(pair)
                slot = n >> 3
            found.setdefault(key, [None] * 8)[slot] = device_id(y, z, core, x)
    return [found[k] for k in sorted(found)]


GROUPS_A = cube_groups(1)
GROUPS_B = cube_groups(0)


def ff_order():
    used = np.arange(384)
    block, q, ctx, r = used // 192, used // 48 % 4, used // 6 % 8, used % 6
    table = np.zeros((384, 384), np.float32)
    table[block * 192 + ctx * 24 + q * 6 + r, used] = 1.0
    return table


FF_ORDER = ff_order()


def fetch_cube(core_ref, mine, theirs, offset, w, sem, low, high):
    core = core_ref[0]

    def step(n, carry):
        for src, own in ((mine, core), (theirs, 1 - core)):
            row, triple = place(n, own)

            @pl.when((triple >= low) & (triple < high))
            def _():
                pltpu.make_async_copy(
                    src.at[n, pl.ds(offset, 9)], w.at[row, pl.ds((triple - low) * 9, 9)], sem).start()

        return carry

    lax.fori_loop(0, 64, step, 0)


COMES = {(0, 0): ("cube", 0), (0, 1): ("cube", 0), (0, 2): ("plain", 0),
         (1, 0): ("cube", 9), (1, 1): ("plain", 0), (1, 2): ("plain", 72)}


def fetch(layer, group, core_ref, sources, w, sem, low, high):
    kind, first = COMES[layer, group]
    if kind == "cube":
        fetch_cube(core_ref, sources[0], sources[1], first, w, sem, low, high)
    else:
        tiles = pl.ds(first + 9 * low, 9 * (high - low))
        pltpu.make_async_copy(sources[0].at[:, tiles], w, sem).start()


def sources_of(layer, groups, refs):
    out, at = {}, 0
    for group in groups:
        n = 2 if COMES[layer, group][0] == "cube" else 1
        out[group] = refs[at : at + n]
        at += n
    return out, refs[at:]


def arrived(w, sem):
    pltpu.make_async_copy(w, w, sem).wait()


def units(w, first, count):
    parts = [w[:, 3 * (first + i) : 3 * (first + i) + 3].reshape(D, 128) for i in range(count)]
    return parts[0] if count == 1 else jnp.concatenate(parts, axis=1)


def tall_units(w, cb):
    return w[:, 12 * cb : 12 * cb + 12].reshape(4 * D, 128)


def mul(a, b):
    return jnp.dot(a, b, preferred_element_type=f32)


def mul_t(a, b):
    return lax.dot_general(a, b, (((1,), (1,)), ((), ())), preferred_element_type=f32)


def t_mul(a, b):
    return lax.dot_general(a, b, (((0,), (0,)), ((), ())), preferred_element_type=f32)


def norm_parts(values):
    centre = values - jnp.mean(values, axis=-1, keepdims=True)
    var = jnp.mean(centre * centre, axis=-1, keepdims=True)
    r = lax.rsqrt(var + norm_eps)
    return centre * r, r


def norm_back(cot, gain, xh, r):
    cg = cot * gain
    return r * (cg - jnp.mean(cg, axis=-1, keepdims=True) - xh * jnp.mean(cg * xh, axis=-1, keepdims=True))


def rows_sum(values):
    return jnp.sum(values, axis=0, keepdims=True)


def windows(values):
    out = []
    for x in range(4):
        for zl in range(2):
            own, shared = 3 * x + 2 * zl, 3 * x + 1
            out.append(jnp.concatenate([values[:, 64 * own : 64 * own + 64],
                                        values[:, 64 * shared : 64 * shared + 64]], axis=1))
    return out


def unwindow(get):
    parts = []
    for x in range(4):
        lo, hi = get(2 * x), get(2 * x + 1)
        parts += [lo[:, :64], lo[:, 64:] + hi[:, 64:], hi[:, :64]]
    return jnp.concatenate(parts, axis=1)


def gelu_both(u):
    k = 0.7978845608028654
    t = jnp.tanh(k * (u + 0.044715 * u * u * u))
    half = 0.5 * (1.0 + t)
    return u * half, half + 0.5 * u * (1.0 - t * t) * (k * (1.0 + 3 * 0.044715 * u * u))


def project_kernel(layer, core, h_ref, vec, *refs):
    src, (a1_ref, pay_ref, w, sem) = sources_of(layer, (0,), refs)
    fetch(layer, 0, core, src[0], w, sem, 0, 6)
    xh, _ = norm_parts(h_ref[...].astype(f32))
    a1 = (xh * vec[0:1] + vec[1:2]).astype(bf16)
    a1_ref[...] = a1
    arrived(w, sem)
    for part in range(3):
        cols = [mul(a1, units(w, 6 * part + 2 * j, 2)) for j in range(3)]
        got = jnp.concatenate(cols, axis=1)
        if part != 1:
            got = got + vec[2 + part // 2 : 3 + part // 2]
        got = got.astype(bf16).astype(f32)
        for d, win in enumerate(windows(got)):
            pay_ref[d, :, 128 * part : 128 * part + 128] = win.astype(bf16)


def visible_of(block, count, idc_ref, idr_ref):
    n = count * TOK
    qpos = block * TOK + lax.broadcasted_iota(jnp.int32, (TOK, n), 0)
    kpos = lax.broadcasted_iota(jnp.int32, (TOK, n), 1)
    return (idc_ref[block] == idr_ref[:, 0:n]) & (kpos <= qpos)


def head_blocks(par):
    for i in range(4):
        yield i, ((0, 2 * i, 2 * i + 1), (0, 2 * i + 1, 2 * i + 2), (1, 2 * i + par, 2 * i + 2))


def half(values, head):
    return values[:, 64 * head : 64 * head + 64]


def store_pair(out, lanes, i, par, parts):
    for k in range(2):
        shared = jnp.where(par == k, parts[2], 0.0)
        out[2 * i + k, :, lanes] = jnp.concatenate([parts[k], shared], axis=1).astype(bf16)


def weights_of(q, key, seen):
    s = jnp.where(seen, mul_t(q, key) * score_scale, hidden_value)
    e = jnp.exp(s - jnp.max(s, axis=1, keepdims=True))
    return e / jnp.sum(e, axis=1, keepdims=True)


def attend_kernel(par_ref, heads, idc, idr, out):
    par = par_ref[0]
    key = heads[:, :, 128:256].reshape(SLOTS, 128)
    val = heads[:, :, 256:384].reshape(SLOTS, 128)
    keys, vals = [half(key, h) for h in range(2)], [half(val, h) for h in range(2)]
    for i, blocks in head_blocks(par):
        parts = []
        for head, block, count in blocks:
            n = count * TOK
            q = half(heads[block, :, 0:128], head)
            p = weights_of(q, keys[head][:n], visible_of(block, count, idc, idr)).astype(bf16)
            parts.append(mul(p, vals[head][:n]))
        store_pair(out, slice(0, 128), i, par, parts)


def attend_back_kernel(par_ref, heads, cot, idc, idr, out, dk_acc, dv_acc):
    par = par_ref[0]
    key = heads[:, :, 128:256].reshape(SLOTS, 128)
    val = heads[:, :, 256:384].reshape(SLOTS, 128)
    keys, vals = [half(key, h) for h in range(2)], [half(val, h) for h in range(2)]
    dk_acc[...] = jnp.zeros_like(dk_acc)
    dv_acc[...] = jnp.zeros_like(dv_acc)
    for i, blocks in head_blocks(par):
        parts = []
        for head, block, count in blocks:
            n = count * TOK
            q = half(heads[block, :, 0:128], head)
            g = half(cot[block], head)
            p = weights_of(q, keys[head][:n], visible_of(block, count, idc, idr))
            dp = mul_t(g, vals[head][:n])
            ds = (p * (dp - jnp.sum(p * dp, axis=1, keepdims=True))).astype(bf16)
            parts.append(mul(ds, keys[head][:n]) * score_scale)
            dk_acc[head, 0:n] += t_mul(ds, q)
            dv_acc[head, 0:n] += t_mul(p.astype(bf16), g)
        store_pair(out, slice(0, 128), i, par, parts)
    dk = jnp.concatenate([dk_acc[0], dk_acc[1]], axis=1) * score_scale
    dv = jnp.concatenate([dv_acc[0], dv_acc[1]], axis=1)
    out[:, :, 128:256] = dk.astype(bf16).reshape(8, TOK, 128)
    out[:, :, 256:384] = dv.astype(bf16).reshape(8, TOK, 128)


def forward_kernel(layer, core, h_ref, back, vec, upb, *refs):
    src, (o_ref, h1_ref, a2_ref, u_ref, next_ref, wo, wu, wd, sems) = sources_of(layer, (0, 1, 2), refs)
    fetch(layer, 0, core, src[0], wo, sems.at[0], 6, 8)
    fetch(layer, 1, core, src[1], wu, sems.at[1], 0, 8)
    fetch(layer, 2, core, src[2], wd, sems.at[2], 0, 8)
    o = unwindow(lambda d: back[d].astype(f32)).astype(bf16)
    o_ref[...] = o
    arrived(wo, sems.at[0])
    got = jnp.concatenate([mul(o, units(wo, 2 * j, 2)) for j in range(3)], axis=1)
    h1 = h_ref[...].astype(f32) + got + vec[2:3]
    h1_ref[...] = h1
    xh, _ = norm_parts(h1)
    a2 = (xh * vec[0:1] + vec[1:2]).astype(bf16)
    a2_ref[...] = a2
    arrived(wu, sems.at[1])
    acts = []
    for j in range(12):
        u = mul(a2, units(wu, 2 * j, 2)) + upb[:, 256 * j : 256 * j + 256]
        u_ref[:, 256 * j : 256 * j + 256] = u
        acts.append(gelu_both(u)[0].astype(bf16))
    f = jnp.concatenate(acts, axis=1)
    arrived(wd, sems.at[2])
    for j in range(3):
        w = jnp.concatenate([tall_units(wd, 2 * j), tall_units(wd, 2 * j + 1)], axis=1)
        c = slice(256 * j, 256 * j + 256)
        next_ref[:, c] = (h1[:, c] + mul(f, w) + vec[3:4, c]).astype(next_ref.dtype)


def backward_kernel(layer, core, e_ref, u_ref, h1_ref, vec, *refs):
    src, (f_ref, du_ref, e1_ref, pay_ref, small_ref, upb_ref, wo, wu, wd, sems) = sources_of(layer, (0, 1, 2), refs)
    fetch(layer, 2, core, src[2], wd, sems.at[2], 0, 8)
    fetch(layer, 1, core, src[1], wu, sems.at[1], 0, 8)
    fetch(layer, 0, core, src[0], wo, sems.at[0], 6, 8)
    e = e_ref[...].astype(f32)
    e2 = e.astype(bf16)
    arrived(wd, sems.at[2])
    df = jnp.zeros((TOK, 4 * D), f32)
    for j in range(3):
        w = jnp.concatenate([tall_units(wd, 2 * j), tall_units(wd, 2 * j + 1)], axis=1)
        df = df + mul_t(e2[:, 256 * j : 256 * j + 256], w)
    arrived(wu, sems.at[1])
    cot = jnp.zeros((TOK, D), f32)
    for j in range(12):
        c = slice(256 * j, 256 * j + 256)
        f, slope = gelu_both(u_ref[:, c])
        f_ref[:, c] = f.astype(bf16)
        du = (df[:, c] * slope).astype(bf16)
        du_ref[:, c] = du
        upb_ref[:, c] = rows_sum(du.astype(f32))
        cot = cot + mul_t(du, units(wu, 2 * j, 2))
    xh, r = norm_parts(h1_ref[...])
    e1 = e + norm_back(cot, vec[0:1], xh, r)
    e1_ref[...] = e1
    b1 = e1.astype(bf16)
    small_ref[0:1] = rows_sum(cot * xh)
    small_ref[1:2] = rows_sum(cot)
    small_ref[2:3] = rows_sum(b1.astype(f32))
    small_ref[3:4] = rows_sum(e2.astype(f32))
    arrived(wo, sems.at[0])
    do = jnp.zeros((TOK, D), f32)
    for j in range(3):
        do = do + mul_t(b1[:, 256 * j : 256 * j + 256], units(wo, 2 * j, 2))
    do = do.astype(bf16).astype(f32)
    for d, win in enumerate(windows(do)):
        pay_ref[d] = win.astype(bf16)


def back_project_kernel(layer, core, back, e1_ref, h_ref, vec, *refs):
    src, (g_ref, e_ref, small_ref, w, sem) = sources_of(layer, (0,), refs)
    fetch(layer, 0, core, src[0], w, sem, 0, 6)
    for part in range(3):
        got = unwindow(lambda d: back[d, :, 128 * part : 128 * part + 128].astype(f32)).astype(bf16)
        g_ref[:, D * part : D * part + D] = got
        if part != 1:
            small_ref[2 + part // 2 : 3 + part // 2] = rows_sum(got.astype(f32))
    arrived(w, sem)
    cot = jnp.zeros((TOK, D), f32)
    for j in range(9):
        cot = cot + mul_t(g_ref[:, 256 * j : 256 * j + 256], units(w, 2 * j, 2))
    xh, r = norm_parts(h_ref[...].astype(f32))
    small_ref[0:1] = rows_sum(cot * xh)
    small_ref[1:2] = rows_sum(cot)
    e_ref[...] = e1_ref[...] + norm_back(cot, vec[0:1], xh, r)


def cube_store(core, stage, first_tile, triple, k, rows):
    for row in range(16):
        target = row & 1
        tile = first_tile + 3 * k
        stage[core ^ target, SLOT_OF[(target, row, triple)], tile : tile + 3] = rows[row].reshape(3, 16, 128)


def plain_store(stage, unit, rows):
    stage[:, 3 * unit : 3 * unit + 3] = rows.reshape(16, 3, 16, 128)


def wide_grad(at, b, first, store):
    for j in range(b.shape[1] // D):
        wide = mul(at, b[:, D * j : D * j + D])
        for i in range(6):
            store(first + 6 * j + i, wide[:, 128 * i : 128 * i + 128].astype(bf16).reshape(16, 48, 128))


def tall_grad(ft, b, store):
    for j in range(3):
        wide = mul(ft, b[:, 256 * j : 256 * j + 256])
        for i in range(2):
            rows = wide[:, 128 * i : 128 * i + 128].astype(bf16).reshape(16, 4, 48, 128)
            for q in range(4):
                store(4 * (2 * j + i) + q, rows[:, q])


def low(ref):
    return ref[...].astype(f32).astype(bf16)


def ship(pairs, sem):
    copies = [pltpu.make_async_copy(src, dst, sem.at[k]) for k, (src, dst) in enumerate(pairs)]
    for copy in copies:
        copy.start()
    for copy in copies:
        copy.wait()


def grad_mlp_cube(core_ref, f_ref, e_ref, a2_ref, du_ref, keep, send, stage, sem):
    core = core_ref[0]
    tall_grad(f_ref[...].T, low(e_ref), lambda u, rows: cube_store(core, stage, 9, u // 3, u % 3, rows))
    wide_grad(a2_ref[...].T, du_ref[...], 0, lambda u, rows: cube_store(core, stage, 0, u // 3, u % 3, rows))
    ship(((stage.at[0], keep), (stage.at[1], send)), sem)


def grad_joint_cube(core_ref, a_ref, g_ref, o_ref, e1_ref, keep, send, stage, sem):
    core = core_ref[0]
    put = lambda u, rows: cube_store(core, stage, 0, u // 3, u % 3, rows)
    wide_grad(a_ref[...].T, g_ref[...], 0, put)
    wide_grad(o_ref[...].T, low(e1_ref), 18, put)
    ship(((stage.at[0], keep), (stage.at[1], send)), sem)


def grad_mlp_plain(f_ref, e_ref, a2_ref, du_ref, out, stage, sem):
    wide_grad(a2_ref[...].T, du_ref[...], 0, lambda u, rows: plain_store(stage, u, rows))
    tall_grad(f_ref[...].T, low(e_ref), lambda u, rows: plain_store(stage, 24 + u, rows))
    ship(((stage, out),), sem)


CUBE_IN, PLAIN_IN = ((0, 0), (0, 1), (1, 0)), ((0, 2), (1, 1), (1, 2))
CUBE_OUT, PLAIN_OUT = ((0, 0), (1, 0), (0, 1), (0, 2)), ((1, 1), (1, 2))


def dense(pieces, tiles):
    left = 16 * tiles - 6 * len(pieces)
    rows = jnp.concatenate(pieces + ([jnp.zeros((left, 128), f32)] if left else []), axis=0)
    return rows.astype(bf16).reshape(tiles, 16, 128)


def pack_kernel(win, wout, wup, wdown, order, pay):
    ins = [win[...].astype(f32), wout[...].astype(f32)]
    wide = wup[...].astype(f32)
    ups = []
    for l in range(LAYERS):
        rows = wide[:, l].astype(bf16)
        ups.append([mul(rows[:, 384 * m : 384 * m + 384], order[...]) for m in range(8)])
    firsts = [[v[:, l] for v in ins] for l in range(LAYERS)]
    downs = [wdown[l].astype(f32) for l in range(LAYERS)]

    def get(l, group, u):
        if group == 0:
            wide, at = (firsts[l][0], u) if u < 18 else (firsts[l][1], u - 18)
            return wide[:, 128 * at : 128 * at + 128]
        if group == 1:
            return ups[l][u // 3][:, 128 * (u % 3) : 128 * (u % 3) + 128]
        cb, q = divmod(u, 4)
        return downs[l][6 * q : 6 * q + 6, 128 * cb : 128 * cb + 128]

    plain = dense([get(*key, u) for key in PLAIN_IN for u in range(24)], 27)
    for d in range(8):
        pay[d, 0:27] = plain
        pay[d, 27:31] = dense([get(*key, 3 * d + i) for key in CUBE_IN for i in range(3)], 4)


def regroup_kernel(got, smalls, first, third, fourth):
    plain = [got[d, 0:27].astype(f32).reshape(432, 128) for d in range(8)]
    cube = [got[d, 27:31].astype(f32).reshape(64, 128) for d in range(8)]

    def join(rows, u):
        return jnp.concatenate([v[6 * u : 6 * u + 6] for v in rows], axis=0).astype(bf16).reshape(3, 16, 128)

    first[9] = smalls[...]
    for u in range(9):
        tile = 3 * u if u < 3 else 3 * u + 1
        first[tile : tile + 3] = join(cube, u)
    for u in range(24):
        third[3 * u : 3 * u + 3] = join(plain, u)
    for u in range(48):
        fourth[3 * u : 3 * u + 3] = join(plain, 24 + u)


def smalls_kernel(core_ref, mine, theirs, *refs):
    vecs, (few, buf, sem) = refs[:4], refs[4:]
    core = core_ref[0]

    def step(n, carry):
        for src, own in ((mine, core), (theirs, 1 - core)):
            row, triple = place(n, own)
            pltpu.make_async_copy(src.at[n, 9], buf.at[row * 8 + triple], sem).start()
        return carry

    lax.fori_loop(0, 64, step, 0)
    pltpu.make_async_copy(buf, buf, sem).wait()
    rows = buf[...].astype(f32)
    low_part, high_part = rows[:, 0], rows[:, 1]
    few[:, 0:128] = low_part
    few[:, 128:256] = high_part
    low_part = low_part.astype(bf16)
    value = lax.broadcasted_iota(jnp.int32, (128, 16), 0) - 6 * lax.broadcasted_iota(jnp.int32, (128, 16), 1)
    place_in = lax.broadcasted_iota(jnp.int32, (128, D), 1) - 6 * lax.broadcasted_iota(jnp.int32, (128, D), 0)
    total = jnp.zeros((16, D), f32)
    for i in range(6):
        picked = mul(low_part, (value == i).astype(f32).astype(bf16)).astype(bf16)
        total = total + t_mul(picked, (place_in == i).astype(f32).astype(bf16))
    for l in range(LAYERS):
        for k, i in enumerate((2 * l, 4 + 2 * l, 8 + 2 * l, 9 + 2 * l)):
            vecs[2 * l][k : k + 1] = total[i : i + 1]
        for k, i in enumerate((2 * l + 1, 5 + 2 * l, 12 + 2 * l, 13 + 2 * l)):
            vecs[2 * l + 1][k : k + 1] = total[i : i + 1]


def finish_kernel(parts, total, out, few):
    small = jnp.zeros((2, 128), f32)
    for k in range(8):
        small = small + parts[k, 9].astype(f32)[0:2]
    few[...] = small
    units_of = []
    for u in range(12):
        tile = 3 * u if u < 3 else 3 * u + 1
        rows = jnp.zeros((48, 128), f32)
        for k in range(8):
            rows = rows + parts[k, tile : tile + 3].reshape(48, 128).astype(f32)
        units_of.append(rows)
    for u in range(48):
        units_of.append(total[3 * u : 3 * u + 3].reshape(48, 128).astype(f32))
    for d in range(8):
        out[d] = dense([rows[6 * d : 6 * d + 6] for rows in units_of], 23)


def unpack_kernel(got, order, g_in, g_out, g_up, g_down):
    cube = [got[d, 0:5].reshape(80, 128).astype(f32) for d in range(8)]
    plain = got[0].reshape(368, 128).astype(f32)
    for d in range(1, 8):
        plain = plain + got[d].reshape(368, 128).astype(f32)
    for l in range(LAYERS):
        for group in range(3):
            rows = []
            for u in range(24):
                if (l, group) in CUBE_OUT:
                    k = 6 * (3 * CUBE_OUT.index((l, group)) + u % 3)
                    rows.append(cube[u // 3][k : k + 6])
                else:
                    k = 6 * (12 + 24 * PLAIN_OUT.index((l, group)) + u)
                    rows.append(plain[k : k + 6])
            if group == 0:
                g_in[:, l] = jnp.concatenate(rows[:18], axis=1)
                g_out[:, l] = jnp.concatenate(rows[18:], axis=1)
            elif group == 1:
                for m in range(8):
                    left = jnp.concatenate(rows[3 * m : 3 * m + 3], axis=1)
                    wide = jnp.zeros((6, 384), f32)
                    for _ in range(3):
                        term = left.astype(bf16)
                        left = left - term.astype(f32)
                        wide = wide + mul_t(term, order[...])
                    g_up[:, l, 384 * m : 384 * m + 384] = wide
            else:
                for u in range(24):
                    cb, q = divmod(u, 4)
                    g_down[l, 6 * q : 6 * q + 6, 128 * cb : 128 * cb + 128] = rows[u]


def call(kernel, outs, ins, scratch=(), us=3, out_spaces=None, aliases=None):
    spaces = {"s": pltpu.SMEM, "v": pltpu.VMEM, "a": pl.ANY}
    return pl.pallas_call(
        kernel,
        out_shape=[jax.ShapeDtypeStruct(*o) for o in outs],
        in_specs=[pl.BlockSpec(memory_space=spaces[m]) for _, m in ins],
        out_specs=[pl.BlockSpec(memory_space=spaces[m]) for m in (out_spaces or "v" * len(outs))],
        scratch_shapes=list(scratch),
        input_output_aliases=aliases or {},
        compiler_params=pltpu.CompilerParams(vmem_limit_bytes=56 * 1024 * 1024),
        cost_estimate=pl.CostEstimate(flops=0, bytes_accessed=us * 3690000, transcendentals=0),
    )(*[a for a, _ in ins])


def w_scratch(count):
    return pltpu.VMEM((16, 3 * count, 16, 128), bf16)


DMA = pltpu.SemaphoreType.DMA


def after(values, *others):
    return lax.optimization_barrier((values,) + others)[0]


def copies(values, groups):
    many = jnp.broadcast_to(values[None], (8,) + values.shape)
    return lax.all_to_all(many, ALL, 0, 0, axis_index_groups=groups)


def sum_first(values):
    return jnp.sum(values.astype(f32), axis=0)


def swap_core(values):
    return lax.ppermute(values, "c", [(0, 1), (1, 0)])


def cube_copies(shards):
    return copies(shards, GROUPS_B).reshape((64,) + shards.shape[1:])


def spread(shards):
    mine = cube_copies(shards)
    return mine, swap_core(mine)


def add_kernel(*refs):
    out, first = refs[-1], 0
    for keep, got in zip(refs[0:-1:2], refs[1:-1:2]):
        n = keep.shape[1]
        out[:, first : first + n] = (keep[...].astype(f32) + got[...].astype(f32)).astype(bf16)
        first += n


def add_pairs(pairs):
    total = sum(a.shape[1] for a, _ in pairs)
    flat = [v for pair in pairs for v in pair]

    def spec(t):
        return pl.BlockSpec((8, t, 16, 128), lambda i: (i, 0, 0, 0))

    return pl.pallas_call(
        add_kernel,
        grid=(8,),
        out_shape=jax.ShapeDtypeStruct((64, total, 16, 128), bf16),
        in_specs=[spec(v.shape[1]) for v in flat],
        out_specs=spec(total),
        compiler_params=pltpu.CompilerParams(vmem_limit_bytes=56 * 1024 * 1024),
        cost_estimate=pl.CostEstimate(flops=2**22, bytes_accessed=3 * 64 * total * 4096, transcendentals=0),
    )(*flat)


def core_sums(pairs):
    return add_pairs([(keep, swap_core(send)) for keep, send in pairs])


def gather_sums(part):
    part = part.reshape((8, 8) + part.shape[1:])
    return sum_first(lax.all_to_all(part, ALL, 0, 0, axis_index_groups=GROUPS_B)).astype(bf16)


def token_ids(group_index, positions, sequence_group, sequence_start, sequence_length):
    member = (
        (sequence_group[None, :] == group_index)
        & (sequence_start[None, :] <= positions[:, None])
        & (positions[:, None] < (sequence_start + sequence_length)[None, :])
    )
    numbers = jnp.arange(sequence_group.shape[0], dtype=jnp.int32) + 1
    located = jnp.sum(jnp.where(member, numbers[None, :], 0), axis=1)
    return jnp.where(located > 0, located - 1, -1 - positions)


def body(hidden_in, out_grad, sequence_group, sequence_start, sequence_length, norm_gain, norm_bias,
         input_weight, input_bias, output_weight, branch_bias, up_weight, up_bias, down_weight):
    core = lax.axis_index("c").astype(jnp.int32).reshape(1)
    par = lax.axis_index("zl").astype(jnp.int32).reshape(1)
    positions = jnp.arange(SLOTS, dtype=jnp.int32)
    ids = token_ids(lax.axis_index(DATA), positions, sequence_group, sequence_start, sequence_length)
    idc, idr = ids.reshape(CTX_DEV, TOK, 1), ids.reshape(1, SLOTS)

    order = jnp.asarray(FF_ORDER, bf16)
    smalls = jnp.concatenate([v.reshape(-1) for v in (norm_gain, norm_bias, input_bias, branch_bias, up_bias)])
    smalls = jnp.pad(smalls, (0, 2048 - 144)).reshape(16, 128)
    (pay,) = call(pack_kernel, [((8, 31, 16, 128), bf16)],
                  [(jnp.swapaxes(v, 0, 1), "v") for v in (input_weight, output_weight, up_weight)]
                  + [(down_weight, "v"), (order, "v")])
    got = lax.all_to_all(pay, CTX, 0, 0)
    first, third, fourth = call(
        regroup_kernel,
        [((28, 16, 128), bf16), ((72, 16, 128), bf16), ((144, 16, 128), bf16)],
        [(got, "v"), (smalls, "v")])
    down_0 = lax.all_gather(third, DATA, axis=0, tiled=False)
    shards = copies(first, GROUPS_A)
    group_e, shards = spread(shards[:, :10]), shards[:, 10:]
    sources = {(0, 0): group_e, (0, 2): (down_0,)}

    *vecs, few = call(
        smalls_kernel, [((4, D), f32)] * 4 + [((128, 256), f32)],
        [(core, "s"), (group_e[0], "a"), (group_e[1], "a")],
        [pltpu.VMEM((128, 16, 128), bf16), DMA], us=2)
    ups = few[:, 96:144].reshape(16, 8, 2, 4, 6).transpose(2, 0, 3, 1, 4).reshape(2, 4 * D)

    def weights(l, all_groups):
        return [(w, "a") for group in range(3 if all_groups else 1) for w in sources[l, group]]

    hidden = hidden_in[0]
    stored = []
    for l in range(LAYERS):
        a1, pay = call(
            functools.partial(project_kernel, l),
            [((TOK, D), bf16), ((8, TOK, 384), bf16)],
            [(core, "s"), (hidden, "v"), (vecs[2 * l], "v")] + weights(l, False),
            [w_scratch(18), DMA],
            us=5)
        if l == 0:
            both_1 = lax.all_gather(after(fourth, a1), DATA, axis=0, tiled=False)
            sources[1, 1] = sources[1, 2] = (both_1,)
        heads = lax.all_to_all(pay, CTX, 0, 0)
        if l == 0:
            mine = cube_copies(after(shards, heads, down_0))
        (mix,) = call(
            attend_kernel,
            [((8, TOK, 128), bf16)],
            [(par, "s"), (heads, "v"), (idc, "v"), (idr, "v")],
            us=7)
        if l == 0:
            theirs = swap_core(after(mine, mix))
            for key in CUBE_IN[1:]:
                sources[key] = (mine, theirs)
        mix = after(mix, mine if l == 0 else both_1)
        back = lax.all_to_all(mix, CTX, 0, 0)
        o, h1, a2, u, following = call(
            functools.partial(forward_kernel, l),
            [((TOK, D), bf16), ((TOK, D), f32), ((TOK, D), bf16), ((TOK, 4 * D), f32),
             ((TOK, D), f32 if l == 0 else bf16)],
            [(core, "s"), (hidden, "v"), (back, "v"), (vecs[2 * l + 1], "v"),
             (ups[l : l + 1], "v")] + weights(l, True),
            [w_scratch(6), w_scratch(24), w_scratch(24), DMA((3,))],
            us=8)
        stored.append((hidden, a1, heads, o, h1, a2, u))
        hidden = following

    def grad_joint(g, a1, o, e1):
        return call(
            grad_joint_cube, [((64, 9, 16, 128), bf16)] * 2,
            [(core, "s"), (a1, "v"), (g, "v"), (o, "v"), (e1, "v")],
            [pltpu.VMEM((2, 64, 9, 16, 128), bf16), DMA((2,))], us=5, out_spaces="aa")

    grad = out_grad[0]
    few_rows, few_up, joint = [None] * 2, [None] * 2, [None] * 2
    for l in reversed(range(LAYERS)):
        layer_in, a1, heads, o, h1, a2, u = stored[l]
        f, du, e1, pay, small_b, small_u = call(
            functools.partial(backward_kernel, l),
            [((TOK, 4 * D), bf16), ((TOK, 4 * D), bf16), ((TOK, D), f32), ((8, TOK, 128), bf16),
             ((4, D), f32), ((1, 4 * D), f32)],
            [(core, "s"), (grad, "v"), (u, "v"), (h1, "v"), (vecs[2 * l + 1], "v")] + weights(l, True),
            [w_scratch(6), w_scratch(24), w_scratch(24), DMA((3,))],
            us=10)
        cot = lax.all_to_all(pay, CTX, 0, 0)
        if l == 1:
            (mlp_1,) = call(
                grad_mlp_plain, [((16, 144, 16, 128), bf16)], [(f, "v"), (grad, "v"), (a2, "v"), (du, "v")],
                [w_scratch(48), DMA((1,))], us=9, out_spaces="a")
            scattered = lax.psum_scatter(after(mlp_1, cot), DATA, scatter_dimension=0, tiled=False)
        else:
            keep_ud, send_ud = call(
                grad_mlp_cube, [((64, 18, 16, 128), bf16)] * 2,
                [(core, "s"), (f, "v"), (grad, "v"), (a2, "v"), (du, "v")],
                [pltpu.VMEM((2, 64, 18, 16, 128), bf16), DMA((2,))],
                us=9, out_spaces="aa")
        if l == 0:
            send_ud = after(send_ud, cot)
        cot = after(cot, mlp_1 if l == 1 else keep_ud)
        (pay2,) = call(
            attend_back_kernel,
            [((8, TOK, 384), bf16)],
            [(par, "s"), (heads, "v"), (cot, "v"), (idc, "v"), (idr, "v")],
            [pltpu.VMEM((2, SLOTS, 64), f32)] * 2,
            us=10)
        back2 = lax.all_to_all(pay2, CTX, 0, 0)
        if l == 0:
            middle = core_sums([(keep_ud, send_ud)])
            back2 = after(back2, middle)
        g, grad, small_a = call(
            functools.partial(back_project_kernel, l),
            [((TOK, 3 * D), bf16), ((TOK, D), f32), ((4, D), f32)],
            [(core, "s"), (back2, "v"), (e1, "v"), (layer_in, "v"), (vecs[2 * l], "v")] + weights(l, False),
            [w_scratch(18), DMA],
            us=6)
        joint[l] = call(
            grad_joint_cube, [((64, 9, 16, 128), bf16)] * 2,
            [(core, "s"), (a1, "v"), (g, "v"), (o, "v"), (e1, "v")],
            [pltpu.VMEM((2, 64, 9, 16, 128), bf16), DMA((2,))], us=5, out_spaces="aa")
        few_rows[l] = jnp.concatenate([small_a[0:1], small_b[0:1], small_a[1:2], small_b[1:2], small_a[2:4],
                                       small_b[2:4]], axis=0)
        few_up[l] = small_u

    few = jnp.concatenate([r.reshape(8, 128, 6).transpose(1, 0, 2).reshape(128, 48) for r in few_rows]
                          + [r.reshape(16, 4, 8, 6).transpose(0, 2, 1, 3).reshape(128, 24) for r in few_up], axis=1)
    few = jnp.pad(few, ((0, 0), (0, 256 - 144))).astype(bf16)
    few = jnp.dot(jnp.asarray(TAIL_ORDER.T, bf16), few, preferred_element_type=f32).astype(bf16)
    few = jnp.pad(few.reshape(2, 64, 1, 2, 128), ((0, 0),) * 3 + ((0, 14), (0, 0)))
    few = [jnp.where(core[0] == k, few[0], few[1]) for k in range(2)]

    middle = gather_sums(middle)
    last = gather_sums(after(core_sums([joint[0], few, joint[1]]), middle, scattered))
    sums = jnp.concatenate([last, middle], axis=1)
    sums = lax.all_to_all(sums, ALL, 0, 0, axis_index_groups=GROUPS_A)
    sums, few = call(finish_kernel, [((8, 23, 16, 128), bf16), ((2, 128), f32)],
                     [(sums, "v"), (scattered, "v")])
    got = lax.all_to_all(sums, CTX, 0, 0)
    grad_in, grad_out, grad_up, grad_down = call(
        unpack_kernel,
        [((6, 2, 3 * D), f32), ((6, 2, D), f32), ((6, 2, 4 * D), f32), ((2, 24, D), f32)],
        [(got, "v"), (order, "v")])
    few = few.reshape(256)
    few_l = [few[48 * l : 48 * l + 48].reshape(4, 2, 6) for l in range(2)]

    def pair(k):
        return jnp.stack([few_l[0][k], few_l[1][k]])

    return (
        hidden[None],
        grad[None],
        pair(0),
        pair(1),
        jnp.swapaxes(grad_in, 0, 1),
        pair(2),
        jnp.swapaxes(grad_out, 0, 1),
        pair(3),
        jnp.swapaxes(grad_up, 0, 1),
        few[96:144].reshape(2, 24),
        grad_down,
    )


def solution(mesh):
    mesh = Mesh(mesh.devices.reshape(4, 2, 2, 4, 2), ALL)
    token = P(DATA, CTX, None)
    one = P(None, ALL)
    two = P(None, None, ALL)
    mat = P(None, ALL, None)
    return jax.shard_map(
        body,
        mesh=mesh,
        in_specs=(token, token, P(), P(), P(), two, two, mat, two, mat, two, mat, one, mat),
        out_specs=(token, token, two, two, mat, two, mat, two, mat, one, mat),
        check_vma=False,
    )
```

```python
import functools

import jax
import jax.numpy as jnp
import numpy as np
from jax import lax
from jax.experimental import pallas as pl
from jax.experimental.pallas import tpu as pltpu
from jax.sharding import Mesh, PartitionSpec as P

LAYERS = 2
D = 768
TOK = 128
CTX_DEV = 8
SLOTS = TOK * CTX_DEV
DATA = ("y", "zh", "c")
CTX = ("x", "zl")
ALL = DATA + CTX
bf16 = jnp.bfloat16
f32 = jnp.float32
norm_eps = 1e-05
score_scale = 0.125
hidden_value = -1000000000.0


def coord(bit_b, bit_a, core):
    return core * (2 * bit_b + bit_a) + (1 - core) * (3 * bit_a + bit_b * (1 - 2 * bit_a))


def place(n, core):
    y = coord((n >> 5) & 1, (n >> 2) & 1, core)
    z = coord((n >> 4) & 1, (n >> 1) & 1, core)
    x = coord((n >> 3) & 1, n & 1, core)
    return (y * 2 + (z >> 1)) * 2 + core, x * 2 + (z & 1)


SLOT_OF = {(c,) + place(n, c): n for c in range(2) for n in range(64)}


def tail_order():
    table = np.zeros((128, 128), np.float32)
    for (c, row, triple), n in SLOT_OF.items():
        table[row * 8 + triple, 64 * c + n] = 1.0
    return table


TAIL_ORDER = tail_order()


def device_id(y, z, core, x):
    return y * 32 + (z >> 1) * 16 + core * 8 + x * 2 + (z & 1)


def cube_groups(level):
    found = {}
    for core in range(2):
        for n in range(64):
            bits = [(n >> s) & 1 for s in range(6)]
            y, z, x = (coord(bits[3 + s], bits[s], core) for s in (2, 1, 0))
            if level == 1:
                key = (core,) + tuple(coord(bits[3 + s], 0, core) for s in (2, 1, 0))
                slot = n & 7
            else:
                pair = [coord(bits[3 + s], bits[s], core) for s in (2, 1, 0)]
                pair = [(v // 2 if core == 0 else ((v + 1) // 2) % 2) for v in pair]
                key = (core,) + tuple(pair)
                slot = n >> 3
            found.setdefault(key, [None] * 8)[slot] = device_id(y, z, core, x)
    return [found[k] for k in sorted(found)]


GROUPS_A = cube_groups(1)
GROUPS_B = cube_groups(0)


def ff_order():
    used = np.arange(384)
    block, q, ctx, r = used // 192, used // 48 % 4, used // 6 % 8, used % 6
    table = np.zeros((384, 384), np.float32)
    table[block * 192 + ctx * 24 + q * 6 + r, used] = 1.0
    return table


FF_ORDER = ff_order()


def fetch_cube(core_ref, mine, theirs, offset, w, sem, low, high):
    core = core_ref[0]

    def step(n, carry):
        for src, own in ((mine, core), (theirs, 1 - core)):
            row, triple = place(n, own)

            @pl.when((triple >= low) & (triple < high))
            def _():
                pltpu.make_async_copy(
                    src.at[n, pl.ds(offset, 9)], w.at[row, pl.ds((triple - low) * 9, 9)], sem).start()

        return carry

    lax.fori_loop(0, 64, step, 0)


COMES = {(0, 0): ("cube", 0), (0, 1): ("cube", 0), (0, 2): ("plain", 0),
         (1, 0): ("cube", 9), (1, 1): ("plain", 0), (1, 2): ("plain", 72)}


def fetch(layer, group, core_ref, sources, w, sem, low, high):
    kind, first = COMES[layer, group]
    if kind == "cube":
        fetch_cube(core_ref, sources[0], sources[1], first, w, sem, low, high)
    else:
        tiles = pl.ds(first + 9 * low, 9 * (high - low))
        pltpu.make_async_copy(sources[0].at[:, tiles], w, sem).start()


def sources_of(layer, groups, refs):
    out, at = {}, 0
    for group in groups:
        n = 2 if COMES[layer, group][0] == "cube" else 1
        out[group] = refs[at : at + n]
        at += n
    return out, refs[at:]


def arrived(w, sem):
    pltpu.make_async_copy(w, w, sem).wait()


def units(w, first, count):
    parts = [w[:, 3 * (first + i) : 3 * (first + i) + 3].reshape(D, 128) for i in range(count)]
    return parts[0] if count == 1 else jnp.concatenate(parts, axis=1)


def tall_units(w, cb):
    return w[:, 12 * cb : 12 * cb + 12].reshape(4 * D, 128)


def mul(a, b):
    return jnp.dot(a, b, preferred_element_type=f32)


def mul_t(a, b):
    return lax.dot_general(a, b, (((1,), (1,)), ((), ())), preferred_element_type=f32)


def t_mul(a, b):
    return lax.dot_general(a, b, (((0,), (0,)), ((), ())), preferred_element_type=f32)


def norm_parts(values):
    centre = values - jnp.mean(values, axis=-1, keepdims=True)
    var = jnp.mean(centre * centre, axis=-1, keepdims=True)
    r = lax.rsqrt(var + norm_eps)
    return centre * r, r


def norm_back(cot, gain, xh, r):
    cg = cot * gain
    return r * (cg - jnp.mean(cg, axis=-1, keepdims=True) - xh * jnp.mean(cg * xh, axis=-1, keepdims=True))


def rows_sum(values):
    return jnp.sum(values, axis=0, keepdims=True)


def windows(values):
    out = []
    for x in range(4):
        for zl in range(2):
            own, shared = 3 * x + 2 * zl, 3 * x + 1
            out.append(jnp.concatenate([values[:, 64 * own : 64 * own + 64],
                                        values[:, 64 * shared : 64 * shared + 64]], axis=1))
    return out


def unwindow(get):
    parts = []
    for x in range(4):
        lo, hi = get(2 * x), get(2 * x + 1)
        parts += [lo[:, :64], lo[:, 64:] + hi[:, 64:], hi[:, :64]]
    return jnp.concatenate(parts, axis=1)


def gelu_both(u):
    k = 0.7978845608028654
    t = jnp.tanh(k * (u + 0.044715 * u * u * u))
    half = 0.5 * (1.0 + t)
    return u * half, half + 0.5 * u * (1.0 - t * t) * (k * (1.0 + 3 * 0.044715 * u * u))


def project_kernel(layer, core, h_ref, vec, *refs):
    src, (a1_ref, pay_ref, w, sem) = sources_of(layer, (0,), refs)
    fetch(layer, 0, core, src[0], w, sem, 0, 6)
    xh, _ = norm_parts(h_ref[...].astype(f32))
    a1 = (xh * vec[0:1] + vec[1:2]).astype(bf16)
    a1_ref[...] = a1
    arrived(w, sem)
    for part in range(3):
        cols = [mul(a1, units(w, 6 * part + 2 * j, 2)) for j in range(3)]
        got = jnp.concatenate(cols, axis=1)
        if part != 1:
            got = got + vec[2 + part // 2 : 3 + part // 2]
        got = got.astype(bf16).astype(f32)
        for d, win in enumerate(windows(got)):
            pay_ref[d, :, 128 * part : 128 * part + 128] = win.astype(bf16)


def masked(scores, first_block, second_block, idc_ref, idr_ref):
    n = scores.shape[1]
    ids = jnp.concatenate([idc_ref[first_block], idc_ref[second_block]], axis=0)
    row = lax.broadcasted_iota(jnp.int32, (2 * TOK, n), 0)
    qpos = row + jnp.where(row < TOK, first_block * TOK, (second_block - 1) * TOK)
    seen = (ids == idr_ref[:, 0:n]) & (lax.broadcasted_iota(jnp.int32, (2 * TOK, n), 1) <= qpos)
    return jnp.where(seen, scores, hidden_value)


def head_pairs(par):
    return ([(0, 2 * i, 2 * i + 1, 2 * i + 2) for i in range(4)]
            + [(1, 4 * i + par, 4 * i + 2 + par, 4 * i + 4) for i in range(2)])


def half(values, head):
    return values[:, 64 * head : 64 * head + 64]


def two_blocks(ref, first, second, lanes, head):
    return jnp.concatenate([half(ref[first, :, lanes], head), half(ref[second, :, lanes], head)], axis=0)


def store_blocks(out, par, results):
    for b in range(8):
        own = results[b // 2][TOK * (b % 2) : TOK * (b % 2) + TOK]
        shared = results[4 + b // 4][TOK * (b // 2 % 2) : TOK * (b // 2 % 2) + TOK]
        shared = jnp.where(par == b % 2, shared, 0.0)
        out[b, :, 0:128] = jnp.concatenate([own, shared], axis=1).astype(bf16)


def weights_of(q, key, *where):
    s = masked(mul_t(q, key), *where)
    e = jnp.exp(s - jnp.max(s, axis=1, keepdims=True))
    return e * (1.0 / jnp.sum(e, axis=1, keepdims=True))


def attend_kernel(par_ref, heads, idc, idr, out):
    par = par_ref[0]
    key = heads[:, :, 128:256].reshape(SLOTS, 128)
    val = heads[:, :, 256:384].reshape(SLOTS, 128)
    keys, vals = [half(key, h) for h in range(2)], [half(val, h) for h in range(2)]
    results = []
    for head, first, second, count in head_pairs(par):
        n = count * TOK
        q = two_blocks(heads, first, second, slice(0, 128), head) * score_scale
        p = weights_of(q, keys[head][:n], first, second, idc, idr).astype(bf16)
        results.append(mul(p, vals[head][:n]))
    store_blocks(out, par, results)


def attend_back_kernel(par_ref, heads, cot, idc, idr, out, dk_acc, dv_acc):
    par = par_ref[0]
    key = heads[:, :, 128:256].reshape(SLOTS, 128)
    val = heads[:, :, 256:384].reshape(SLOTS, 128)
    keys, vals = [half(key, h) for h in range(2)], [half(val, h) for h in range(2)]
    dk_acc[...] = jnp.zeros_like(dk_acc)
    dv_acc[...] = jnp.zeros_like(dv_acc)
    results = []
    for head, first, second, count in head_pairs(par):
        n = count * TOK
        q = two_blocks(heads, first, second, slice(0, 128), head) * score_scale
        g = two_blocks(cot, first, second, slice(0, 128), head)
        p = weights_of(q, keys[head][:n], first, second, idc, idr)
        dp = mul_t(g, vals[head][:n])
        ds = (p * (dp - jnp.sum(p * dp, axis=1, keepdims=True))).astype(bf16)
        results.append(mul(ds, keys[head][:n]) * score_scale)
        dk_acc[head, 0:n] += t_mul(ds, q)
        dv_acc[head, 0:n] += t_mul(p.astype(bf16), g)
    store_blocks(out, par, results)
    dk = jnp.concatenate([dk_acc[0], dk_acc[1]], axis=1)
    dv = jnp.concatenate([dv_acc[0], dv_acc[1]], axis=1)
    out[:, :, 128:256] = dk.astype(bf16).reshape(8, TOK, 128)
    out[:, :, 256:384] = dv.astype(bf16).reshape(8, TOK, 128)


def forward_kernel(layer, core, h_ref, back, vec, upb, *refs):
    src, (o_ref, h1_ref, a2_ref, u_ref, next_ref, wo, wu, wd, sems) = sources_of(layer, (0, 1, 2), refs)
    fetch(layer, 0, core, src[0], wo, sems.at[0], 6, 8)
    fetch(layer, 1, core, src[1], wu, sems.at[1], 0, 8)
    fetch(layer, 2, core, src[2], wd, sems.at[2], 0, 8)
    o = unwindow(lambda d: back[d].astype(f32)).astype(bf16)
    o_ref[...] = o
    arrived(wo, sems.at[0])
    got = jnp.concatenate([mul(o, units(wo, 2 * j, 2)) for j in range(3)], axis=1)
    h1 = h_ref[...].astype(f32) + got + vec[2:3]
    h1_ref[...] = h1
    xh, _ = norm_parts(h1)
    a2 = (xh * vec[0:1] + vec[1:2]).astype(bf16)
    a2_ref[...] = a2
    arrived(wu, sems.at[1])
    acts = []
    for j in range(12):
        u = mul(a2, units(wu, 2 * j, 2)) + upb[:, 256 * j : 256 * j + 256]
        u_ref[:, 256 * j : 256 * j + 256] = u
        acts.append(gelu_both(u)[0].astype(bf16))
    f = jnp.concatenate(acts, axis=1)
    arrived(wd, sems.at[2])
    for j in range(3):
        w = jnp.concatenate([tall_units(wd, 2 * j), tall_units(wd, 2 * j + 1)], axis=1)
        c = slice(256 * j, 256 * j + 256)
        next_ref[:, c] = (h1[:, c] + mul(f, w) + vec[3:4, c]).astype(next_ref.dtype)


def backward_kernel(layer, core, e_ref, u_ref, h1_ref, vec, *refs):
    src, (f_ref, du_ref, e1_ref, pay_ref, small_ref, upb_ref, wo, wu, wd, sems) = sources_of(layer, (0, 1, 2), refs)
    fetch(layer, 2, core, src[2], wd, sems.at[2], 0, 8)
    fetch(layer, 1, core, src[1], wu, sems.at[1], 0, 8)
    fetch(layer, 0, core, src[0], wo, sems.at[0], 6, 8)
    e = e_ref[...].astype(f32)
    e2 = e.astype(bf16)
    arrived(wd, sems.at[2])
    df = jnp.zeros((TOK, 4 * D), f32)
    for j in range(3):
        w = jnp.concatenate([tall_units(wd, 2 * j), tall_units(wd, 2 * j + 1)], axis=1)
        df = df + mul_t(e2[:, 256 * j : 256 * j + 256], w)
    arrived(wu, sems.at[1])
    cot = jnp.zeros((TOK, D), f32)
    for j in range(12):
        c = slice(256 * j, 256 * j + 256)
        f, slope = gelu_both(u_ref[:, c])
        f_ref[:, c] = f.astype(bf16)
        du = (df[:, c] * slope).astype(bf16)
        du_ref[:, c] = du
        upb_ref[:, c] = rows_sum(du.astype(f32))
        cot = cot + mul_t(du, units(wu, 2 * j, 2))
    xh, r = norm_parts(h1_ref[...])
    e1 = e + norm_back(cot, vec[0:1], xh, r)
    e1_ref[...] = e1
    b1 = e1.astype(bf16)
    small_ref[0:1] = rows_sum(cot * xh)
    small_ref[1:2] = rows_sum(cot)
    small_ref[2:3] = rows_sum(b1.astype(f32))
    small_ref[3:4] = rows_sum(e2.astype(f32))
    arrived(wo, sems.at[0])
    do = jnp.zeros((TOK, D), f32)
    for j in range(3):
        do = do + mul_t(b1[:, 256 * j : 256 * j + 256], units(wo, 2 * j, 2))
    do = do.astype(bf16).astype(f32)
    for d, win in enumerate(windows(do)):
        pay_ref[d] = win.astype(bf16)


def back_project_kernel(layer, core, back, e1_ref, h_ref, vec, *refs):
    src, (g_ref, e_ref, small_ref, w, sem) = sources_of(layer, (0,), refs)
    fetch(layer, 0, core, src[0], w, sem, 0, 6)
    for part in range(3):
        got = unwindow(lambda d: back[d, :, 128 * part : 128 * part + 128].astype(f32)).astype(bf16)
        g_ref[:, D * part : D * part + D] = got
        if part != 1:
            small_ref[2 + part // 2 : 3 + part // 2] = rows_sum(got.astype(f32))
    arrived(w, sem)
    cot = jnp.zeros((TOK, D), f32)
    for j in range(9):
        cot = cot + mul_t(g_ref[:, 256 * j : 256 * j + 256], units(w, 2 * j, 2))
    xh, r = norm_parts(h_ref[...].astype(f32))
    small_ref[0:1] = rows_sum(cot * xh)
    small_ref[1:2] = rows_sum(cot)
    e_ref[...] = e1_ref[...] + norm_back(cot, vec[0:1], xh, r)


def cube_store(core, stage, first_tile, triple, k, rows):
    for row in range(16):
        target = row & 1
        tile = first_tile + 3 * k
        stage[core ^ target, SLOT_OF[(target, row, triple)], tile : tile + 3] = rows[row].reshape(3, 16, 128)


def plain_store(stage, unit, rows):
    stage[:, 3 * unit : 3 * unit + 3] = rows.reshape(16, 3, 16, 128)


def wide_grad(at, b, first, store):
    for j in range(b.shape[1] // D):
        wide = mul(at, b[:, D * j : D * j + D])
        for i in range(6):
            store(first + 6 * j + i, wide[:, 128 * i : 128 * i + 128].astype(bf16).reshape(16, 48, 128))


def tall_grad(ft, b, store):
    for j in range(3):
        wide = mul(ft, b[:, 256 * j : 256 * j + 256])
        for i in range(2):
            rows = wide[:, 128 * i : 128 * i + 128].astype(bf16).reshape(16, 4, 48, 128)
            for q in range(4):
                store(4 * (2 * j + i) + q, rows[:, q])


def low(ref):
    return ref[...].astype(f32).astype(bf16)


def ship(pairs, sem):
    copies = [pltpu.make_async_copy(src, dst, sem.at[k]) for k, (src, dst) in enumerate(pairs)]
    for copy in copies:
        copy.start()
    for copy in copies:
        copy.wait()


def grad_mlp_cube(core_ref, f_ref, e_ref, a2_ref, du_ref, keep, send, stage, sem):
    core = core_ref[0]
    tall_grad(f_ref[...].T, low(e_ref), lambda u, rows: cube_store(core, stage, 9, u // 3, u % 3, rows))
    wide_grad(a2_ref[...].T, du_ref[...], 0, lambda u, rows: cube_store(core, stage, 0, u // 3, u % 3, rows))
    ship(((stage.at[0], keep), (stage.at[1], send)), sem)


def grad_joint_cube(core_ref, a_ref, g_ref, o_ref, e1_ref, keep, send, stage, sem):
    core = core_ref[0]
    put = lambda u, rows: cube_store(core, stage, 0, u // 3, u % 3, rows)
    wide_grad(a_ref[...].T, g_ref[...], 0, put)
    wide_grad(o_ref[...].T, low(e1_ref), 18, put)
    ship(((stage.at[0], keep), (stage.at[1], send)), sem)


def grad_mlp_plain(f_ref, e_ref, a2_ref, du_ref, out, stage, sem):
    wide_grad(a2_ref[...].T, du_ref[...], 0, lambda u, rows: plain_store(stage, u, rows))
    tall_grad(f_ref[...].T, low(e_ref), lambda u, rows: plain_store(stage, 24 + u, rows))
    ship(((stage, out),), sem)


CUBE_IN, PLAIN_IN = ((0, 0), (0, 1), (1, 0)), ((0, 2), (1, 1), (1, 2))
CUBE_OUT, PLAIN_OUT = ((0, 0), (1, 0), (0, 1), (0, 2)), ((1, 1), (1, 2))


def dense(pieces, tiles):
    left = 16 * tiles - 6 * len(pieces)
    rows = jnp.concatenate(pieces + ([jnp.zeros((left, 128), f32)] if left else []), axis=0)
    return rows.astype(bf16).reshape(tiles, 16, 128)


def pack_kernel(win, wout, wup, wdown, order, pay):
    ins = [win[...].astype(f32), wout[...].astype(f32)]
    wide = wup[...].astype(f32)
    stack = [wide[:, l, 384 * m : 384 * m + 384] for l in range(LAYERS) for m in range(8)]
    stack = mul(jnp.concatenate(stack, axis=0).astype(bf16), order[...])
    ups = [[stack[48 * l + 6 * m : 48 * l + 6 * m + 6] for m in range(8)] for l in range(LAYERS)]
    firsts = [[v[:, l] for v in ins] for l in range(LAYERS)]
    downs = [wdown[l].astype(f32) for l in range(LAYERS)]

    def get(l, group, u):
        if group == 0:
            wide, at = (firsts[l][0], u) if u < 18 else (firsts[l][1], u - 18)
            return wide[:, 128 * at : 128 * at + 128]
        if group == 1:
            return ups[l][u // 3][:, 128 * (u % 3) : 128 * (u % 3) + 128]
        cb, q = divmod(u, 4)
        return downs[l][6 * q : 6 * q + 6, 128 * cb : 128 * cb + 128]

    plain = dense([get(*key, u) for key in PLAIN_IN for u in range(24)], 27)
    for d in range(8):
        pay[d, 0:27] = plain
        pay[d, 27:31] = dense([get(*key, 3 * d + i) for key in CUBE_IN for i in range(3)], 4)


def regroup_kernel(got, smalls, first, third, fourth):
    plain = [got[d, 0:27].astype(f32).reshape(432, 128) for d in range(8)]
    cube = [got[d, 27:31].astype(f32).reshape(64, 128) for d in range(8)]

    def join(rows, u):
        return jnp.concatenate([v[6 * u : 6 * u + 6] for v in rows], axis=0).astype(bf16).reshape(3, 16, 128)

    first[9] = smalls[...]
    for u in range(9):
        tile = 3 * u if u < 3 else 3 * u + 1
        first[tile : tile + 3] = join(cube, u)
    for u in range(24):
        third[3 * u : 3 * u + 3] = join(plain, u)
    for u in range(48):
        fourth[3 * u : 3 * u + 3] = join(plain, 24 + u)


def smalls_kernel(core_ref, mine, theirs, *refs):
    vecs, (few, buf, sem) = refs[:4], refs[4:]
    core = core_ref[0]

    def step(n, carry):
        for src, own in ((mine, core), (theirs, 1 - core)):
            row, triple = place(n, own)
            pltpu.make_async_copy(src.at[n, 9], buf.at[row * 8 + triple], sem).start()
        return carry

    lax.fori_loop(0, 64, step, 0)
    pltpu.make_async_copy(buf, buf, sem).wait()
    rows = buf[...].astype(f32)
    low_part, high_part = rows[:, 0], rows[:, 1]
    few[:, 0:128] = low_part
    few[:, 128:256] = high_part
    low_part = low_part.astype(bf16)
    value = lax.broadcasted_iota(jnp.int32, (128, 16), 0) - 6 * lax.broadcasted_iota(jnp.int32, (128, 16), 1)
    place_in = lax.broadcasted_iota(jnp.int32, (128, D), 1) - 6 * lax.broadcasted_iota(jnp.int32, (128, D), 0)
    total = jnp.zeros((16, D), f32)
    for i in range(6):
        picked = mul(low_part, (value == i).astype(f32).astype(bf16)).astype(bf16)
        total = total + t_mul(picked, (place_in == i).astype(f32).astype(bf16))
    for l in range(LAYERS):
        for k, i in enumerate((2 * l, 4 + 2 * l, 8 + 2 * l, 9 + 2 * l)):
            vecs[2 * l][k : k + 1] = total[i : i + 1]
        for k, i in enumerate((2 * l + 1, 5 + 2 * l, 12 + 2 * l, 13 + 2 * l)):
            vecs[2 * l + 1][k : k + 1] = total[i : i + 1]


def finish_kernel(parts, total, out, few):
    small = jnp.zeros((2, 128), f32)
    for k in range(8):
        small = small + parts[k, 9].astype(f32)[0:2]
    few[...] = small
    units_of = []
    for u in range(12):
        tile = 3 * u if u < 3 else 3 * u + 1
        rows = jnp.zeros((48, 128), f32)
        for k in range(8):
            rows = rows + parts[k, tile : tile + 3].reshape(48, 128).astype(f32)
        units_of.append(rows)
    for u in range(48):
        units_of.append(total[3 * u : 3 * u + 3].reshape(48, 128).astype(f32))
    for d in range(8):
        out[d] = dense([rows[6 * d : 6 * d + 6] for rows in units_of], 23)


def unpack_kernel(got, order, g_in, g_out, g_up, g_down):
    cube = [got[d, 0:5].reshape(80, 128).astype(f32) for d in range(8)]
    plain = got[0].reshape(368, 128).astype(f32)
    for d in range(1, 8):
        plain = plain + got[d].reshape(368, 128).astype(f32)
    stack = []
    for l in range(LAYERS):
        for group in range(3):
            rows = []
            for u in range(24):
                if (l, group) in CUBE_OUT:
                    k = 6 * (3 * CUBE_OUT.index((l, group)) + u % 3)
                    rows.append(cube[u // 3][k : k + 6])
                else:
                    k = 6 * (12 + 24 * PLAIN_OUT.index((l, group)) + u)
                    rows.append(plain[k : k + 6])
            if group == 0:
                g_in[:, l] = jnp.concatenate(rows[:18], axis=1)
                g_out[:, l] = jnp.concatenate(rows[18:], axis=1)
            elif group == 1:
                stack += [jnp.concatenate(rows[3 * m : 3 * m + 3], axis=1) for m in range(8)]
            else:
                for u in range(24):
                    cb, q = divmod(u, 4)
                    g_down[l, 6 * q : 6 * q + 6, 128 * cb : 128 * cb + 128] = rows[u]
    left = jnp.concatenate(stack, axis=0)
    terms = []
    for _ in range(3):
        terms.append(left.astype(bf16))
        left = left - terms[-1].astype(f32)
    wide = mul_t(jnp.concatenate(terms, axis=0), order[...])
    wide = wide[0:96] + wide[96:192] + wide[192:288]
    for l in range(LAYERS):
        for m in range(8):
            g_up[:, l, 384 * m : 384 * m + 384] = wide[48 * l + 6 * m : 48 * l + 6 * m + 6]


def call(kernel, outs, ins, scratch=(), us=3, out_spaces=None, aliases=None):
    spaces = {"s": pltpu.SMEM, "v": pltpu.VMEM, "a": pl.ANY}
    return pl.pallas_call(
        kernel,
        out_shape=[jax.ShapeDtypeStruct(*o) for o in outs],
        in_specs=[pl.BlockSpec(memory_space=spaces[m]) for _, m in ins],
        out_specs=[pl.BlockSpec(memory_space=spaces[m]) for m in (out_spaces or "v" * len(outs))],
        scratch_shapes=list(scratch),
        input_output_aliases=aliases or {},
        compiler_params=pltpu.CompilerParams(vmem_limit_bytes=56 * 1024 * 1024),
        cost_estimate=pl.CostEstimate(flops=0, bytes_accessed=us * 3690000, transcendentals=0),
    )(*[a for a, _ in ins])


def w_scratch(count):
    return pltpu.VMEM((16, 3 * count, 16, 128), bf16)


DMA = pltpu.SemaphoreType.DMA


def after(values, *others):
    return lax.optimization_barrier((values,) + others)[0]


def copies(values, groups):
    many = jnp.broadcast_to(values[None], (8,) + values.shape)
    return lax.all_to_all(many, ALL, 0, 0, axis_index_groups=groups)


def sum_first(values):
    return jnp.sum(values.astype(f32), axis=0)


def swap_core(values):
    return lax.ppermute(values, "c", [(0, 1), (1, 0)])


def cube_copies(shards):
    return copies(shards, GROUPS_B).reshape((64,) + shards.shape[1:])


def spread(shards):
    mine = cube_copies(shards)
    return mine, swap_core(mine)


def add_kernel(*refs):
    out, first = refs[-1], 0
    for keep, got in zip(refs[0:-1:2], refs[1:-1:2]):
        n = keep.shape[1]
        out[:, first : first + n] = (keep[...].astype(f32) + got[...].astype(f32)).astype(bf16)
        first += n


def add_pairs(pairs):
    total = sum(a.shape[1] for a, _ in pairs)
    flat = [v for pair in pairs for v in pair]

    def spec(t):
        return pl.BlockSpec((8, t, 16, 128), lambda i: (i, 0, 0, 0))

    return pl.pallas_call(
        add_kernel,
        grid=(8,),
        out_shape=jax.ShapeDtypeStruct((64, total, 16, 128), bf16),
        in_specs=[spec(v.shape[1]) for v in flat],
        out_specs=spec(total),
        compiler_params=pltpu.CompilerParams(vmem_limit_bytes=56 * 1024 * 1024),
        cost_estimate=pl.CostEstimate(flops=2**22, bytes_accessed=3 * 64 * total * 4096, transcendentals=0),
    )(*flat)


def core_sums(pairs):
    return add_pairs([(keep, swap_core(send)) for keep, send in pairs])


def gather_sums(part):
    part = part.reshape((8, 8) + part.shape[1:])
    return sum_first(lax.all_to_all(part, ALL, 0, 0, axis_index_groups=GROUPS_B)).astype(bf16)


def token_ids(group_index, positions, sequence_group, sequence_start, sequence_length):
    member = (
        (sequence_group[None, :] == group_index)
        & (sequence_start[None, :] <= positions[:, None])
        & (positions[:, None] < (sequence_start + sequence_length)[None, :])
    )
    numbers = jnp.arange(sequence_group.shape[0], dtype=jnp.int32) + 1
    located = jnp.sum(jnp.where(member, numbers[None, :], 0), axis=1)
    return jnp.where(located > 0, located - 1, -1 - positions)


def body(hidden_in, out_grad, sequence_group, sequence_start, sequence_length, norm_gain, norm_bias,
         input_weight, input_bias, output_weight, branch_bias, up_weight, up_bias, down_weight):
    core = lax.axis_index("c").astype(jnp.int32).reshape(1)
    par = lax.axis_index("zl").astype(jnp.int32).reshape(1)
    positions = jnp.arange(SLOTS, dtype=jnp.int32)
    ids = token_ids(lax.axis_index(DATA), positions, sequence_group, sequence_start, sequence_length)
    idc, idr = ids.reshape(CTX_DEV, TOK, 1), ids.reshape(1, SLOTS)

    order = jnp.asarray(FF_ORDER, bf16)
    smalls = jnp.concatenate([v.reshape(-1) for v in (norm_gain, norm_bias, input_bias, branch_bias, up_bias)])
    smalls = jnp.pad(smalls, (0, 2048 - 144)).reshape(16, 128)
    (pay,) = call(pack_kernel, [((8, 31, 16, 128), bf16)],
                  [(jnp.swapaxes(v, 0, 1), "v") for v in (input_weight, output_weight, up_weight)]
                  + [(down_weight, "v"), (order, "v")])
    got = lax.all_to_all(pay, CTX, 0, 0)
    first, third, fourth = call(
        regroup_kernel,
        [((28, 16, 128), bf16), ((72, 16, 128), bf16), ((144, 16, 128), bf16)],
        [(got, "v"), (smalls, "v")])
    down_0 = lax.all_gather(third, DATA, axis=0, tiled=False)
    shards = copies(first, GROUPS_A)
    group_e, shards = spread(shards[:, :10]), shards[:, 10:]
    sources = {(0, 0): group_e, (0, 2): (down_0,)}

    *vecs, few = call(
        smalls_kernel, [((4, D), f32)] * 4 + [((128, 256), f32)],
        [(core, "s"), (group_e[0], "a"), (group_e[1], "a")],
        [pltpu.VMEM((128, 16, 128), bf16), DMA], us=2)
    ups = few[:, 96:144].reshape(16, 8, 2, 4, 6).transpose(2, 0, 3, 1, 4).reshape(2, 4 * D)

    def weights(l, all_groups):
        return [(w, "a") for group in range(3 if all_groups else 1) for w in sources[l, group]]

    hidden = hidden_in[0]
    stored = []
    for l in range(LAYERS):
        a1, pay = call(
            functools.partial(project_kernel, l),
            [((TOK, D), bf16), ((8, TOK, 384), bf16)],
            [(core, "s"), (hidden, "v"), (vecs[2 * l], "v")] + weights(l, False),
            [w_scratch(18), DMA],
            us=5)
        if l == 0:
            both_1 = lax.all_gather(after(fourth, a1), DATA, axis=0, tiled=False)
            sources[1, 1] = sources[1, 2] = (both_1,)
        heads = lax.all_to_all(pay, CTX, 0, 0)
        if l == 0:
            mine = cube_copies(after(shards, heads, down_0))
        (mix,) = call(
            attend_kernel,
            [((8, TOK, 128), bf16)],
            [(par, "s"), (heads, "v"), (idc, "v"), (idr, "v")],
            us=7)
        if l == 0:
            theirs = swap_core(after(mine, mix))
            for key in CUBE_IN[1:]:
                sources[key] = (mine, theirs)
        if l == 0:
            mix = after(mix, mine)
        back = lax.all_to_all(mix, CTX, 0, 0)
        o, h1, a2, u, following = call(
            functools.partial(forward_kernel, l),
            [((TOK, D), bf16), ((TOK, D), f32), ((TOK, D), bf16), ((TOK, 4 * D), f32),
             ((TOK, D), f32 if l == 0 else bf16)],
            [(core, "s"), (hidden, "v"), (back, "v"), (vecs[2 * l + 1], "v"),
             (ups[l : l + 1], "v")] + weights(l, True),
            [w_scratch(6), w_scratch(24), w_scratch(24), DMA((3,))],
            us=8)
        stored.append((hidden, a1, heads, o, h1, a2, u))
        hidden = following

    def grad_joint(g, a1, o, e1):
        return call(
            grad_joint_cube, [((64, 9, 16, 128), bf16)] * 2,
            [(core, "s"), (a1, "v"), (g, "v"), (o, "v"), (e1, "v")],
            [pltpu.VMEM((2, 64, 9, 16, 128), bf16), DMA((2,))], us=5, out_spaces="aa")

    grad = out_grad[0]
    few_rows, few_up, joint = [None] * 2, [None] * 2, [None] * 2
    for l in reversed(range(LAYERS)):
        layer_in, a1, heads, o, h1, a2, u = stored[l]
        f, du, e1, pay, small_b, small_u = call(
            functools.partial(backward_kernel, l),
            [((TOK, 4 * D), bf16), ((TOK, 4 * D), bf16), ((TOK, D), f32), ((8, TOK, 128), bf16),
             ((4, D), f32), ((1, 4 * D), f32)],
            [(core, "s"), (grad, "v"), (u, "v"), (h1, "v"), (vecs[2 * l + 1], "v")] + weights(l, True),
            [w_scratch(6), w_scratch(24), w_scratch(24), DMA((3,))],
            us=10)
        cot = lax.all_to_all(pay, CTX, 0, 0)
        if l == 1:
            (mlp_1,) = call(
                grad_mlp_plain, [((16, 144, 16, 128), bf16)], [(f, "v"), (grad, "v"), (a2, "v"), (du, "v")],
                [w_scratch(48), DMA((1,))], us=9, out_spaces="a")
            scattered = lax.psum_scatter(after(mlp_1, cot), DATA, scatter_dimension=0, tiled=False)
        else:
            keep_ud, send_ud = call(
                grad_mlp_cube, [((64, 18, 16, 128), bf16)] * 2,
                [(core, "s"), (f, "v"), (grad, "v"), (a2, "v"), (du, "v")],
                [pltpu.VMEM((2, 64, 18, 16, 128), bf16), DMA((2,))],
                us=9, out_spaces="aa")
        if l == 0:
            send_ud = after(send_ud, cot)
        cot = after(cot, mlp_1 if l == 1 else keep_ud)
        (pay2,) = call(
            attend_back_kernel,
            [((8, TOK, 384), bf16)],
            [(par, "s"), (heads, "v"), (cot, "v"), (idc, "v"), (idr, "v")],
            [pltpu.VMEM((2, SLOTS, 64), f32)] * 2,
            us=10)
        back2 = lax.all_to_all(pay2, CTX, 0, 0)
        if l == 0:
            middle = core_sums([(keep_ud, send_ud)])
            back2 = after(back2, middle)
        g, grad, small_a = call(
            functools.partial(back_project_kernel, l),
            [((TOK, 3 * D), bf16), ((TOK, D), f32), ((4, D), f32)],
            [(core, "s"), (back2, "v"), (e1, "v"), (layer_in, "v"), (vecs[2 * l], "v")] + weights(l, False),
            [w_scratch(18), DMA],
            us=6)
        joint[l] = call(
            grad_joint_cube, [((64, 9, 16, 128), bf16)] * 2,
            [(core, "s"), (a1, "v"), (g, "v"), (o, "v"), (e1, "v")],
            [pltpu.VMEM((2, 64, 9, 16, 128), bf16), DMA((2,))], us=5, out_spaces="aa")
        few_rows[l] = jnp.concatenate([small_a[0:1], small_b[0:1], small_a[1:2], small_b[1:2], small_a[2:4],
                                       small_b[2:4]], axis=0)
        few_up[l] = small_u

    few = jnp.concatenate([r.reshape(8, 128, 6).transpose(1, 0, 2).reshape(128, 48) for r in few_rows]
                          + [r.reshape(16, 4, 8, 6).transpose(0, 2, 1, 3).reshape(128, 24) for r in few_up], axis=1)
    few = jnp.pad(few, ((0, 0), (0, 256 - 144))).astype(bf16)
    few = jnp.dot(jnp.asarray(TAIL_ORDER.T, bf16), few, preferred_element_type=f32).astype(bf16)
    few = jnp.pad(few.reshape(2, 64, 1, 2, 128), ((0, 0),) * 3 + ((0, 14), (0, 0)))
    few = [jnp.where(core[0] == k, few[0], few[1]) for k in range(2)]

    middle = gather_sums(middle)
    last = gather_sums(after(core_sums([joint[0], few, joint[1]]), middle, scattered))
    sums = jnp.concatenate([last, middle], axis=1)
    sums = lax.all_to_all(sums, ALL, 0, 0, axis_index_groups=GROUPS_A)
    sums, few = call(finish_kernel, [((8, 23, 16, 128), bf16), ((2, 128), f32)],
                     [(sums, "v"), (scattered, "v")])
    got = lax.all_to_all(sums, CTX, 0, 0)
    grad_in, grad_out, grad_up, grad_down = call(
        unpack_kernel,
        [((6, 2, 3 * D), f32), ((6, 2, D), f32), ((6, 2, 4 * D), f32), ((2, 24, D), f32)],
        [(got, "v"), (order, "v")])
    few = few.reshape(256)
    few_l = [few[48 * l : 48 * l + 48].reshape(4, 2, 6) for l in range(2)]

    def pair(k):
        return jnp.stack([few_l[0][k], few_l[1][k]])

    return (
        hidden[None],
        grad[None],
        pair(0),
        pair(1),
        jnp.swapaxes(grad_in, 0, 1),
        pair(2),
        jnp.swapaxes(grad_out, 0, 1),
        pair(3),
        jnp.swapaxes(grad_up, 0, 1),
        few[96:144].reshape(2, 24),
        grad_down,
    )


def solution(mesh):
    mesh = Mesh(mesh.devices.reshape(4, 2, 2, 4, 2), ALL)
    token = P(DATA, CTX, None)
    one = P(None, ALL)
    two = P(None, None, ALL)
    mat = P(None, ALL, None)
    return jax.shard_map(
        body,
        mesh=mesh,
        in_specs=(token, token, P(), P(), P(), two, two, mat, two, mat, two, mat, one, mat),
        out_specs=(token, token, two, two, mat, two, mat, two, mat, one, mat),
        check_vma=False,
    )
```

```python
import functools

import jax
import jax.numpy as jnp
import numpy as np
from jax import lax
from jax.experimental import pallas as pl
from jax.experimental.pallas import tpu as pltpu
from jax.sharding import Mesh, PartitionSpec as P

LAYERS = 2
D = 768
TOK = 128
CTX_DEV = 8
SLOTS = TOK * CTX_DEV
DATA = ("y", "zh", "c")
CTX = ("x", "zl")
ALL = DATA + CTX
bf16 = jnp.bfloat16
f32 = jnp.float32
norm_eps = 1e-05
score_scale = 0.125
hidden_value = -1000000000.0


def coord(bit_b, bit_a, core):
    return core * (2 * bit_b + bit_a) + (1 - core) * (3 * bit_a + bit_b * (1 - 2 * bit_a))


def place(n, core):
    y = coord((n >> 5) & 1, (n >> 2) & 1, core)
    z = coord((n >> 4) & 1, (n >> 1) & 1, core)
    x = coord((n >> 3) & 1, n & 1, core)
    return (y * 2 + (z >> 1)) * 2 + core, x * 2 + (z & 1)


SLOT_OF = {(c,) + place(n, c): n for c in range(2) for n in range(64)}


def tail_order():
    table = np.zeros((128, 128), np.float32)
    for (c, row, triple), n in SLOT_OF.items():
        table[row * 8 + triple, 64 * c + n] = 1.0
    return table


TAIL_ORDER = tail_order()


def device_id(y, z, core, x):
    return y * 32 + (z >> 1) * 16 + core * 8 + x * 2 + (z & 1)


def cube_groups(level):
    found = {}
    for core in range(2):
        for n in range(64):
            bits = [(n >> s) & 1 for s in range(6)]
            y, z, x = (coord(bits[3 + s], bits[s], core) for s in (2, 1, 0))
            if level == 1:
                key = (core,) + tuple(coord(bits[3 + s], 0, core) for s in (2, 1, 0))
                slot = n & 7
            else:
                pair = [coord(bits[3 + s], bits[s], core) for s in (2, 1, 0)]
                pair = [(v // 2 if core == 0 else ((v + 1) // 2) % 2) for v in pair]
                key = (core,) + tuple(pair)
                slot = n >> 3
            found.setdefault(key, [None] * 8)[slot] = device_id(y, z, core, x)
    return [found[k] for k in sorted(found)]


GROUPS_A = cube_groups(1)
GROUPS_B = cube_groups(0)


def ff_order():
    used = np.arange(384)
    block, q, ctx, r = used // 192, used // 48 % 4, used // 6 % 8, used % 6
    table = np.zeros((384, 384), np.float32)
    table[block * 192 + ctx * 24 + q * 6 + r, used] = 1.0
    return table


FF_ORDER = ff_order()


def slot_at(y, z, x, core):
    n = 0
    for v, m in ((y, 4), (z, 2), (x, 1)):
        bit_a = core * (v & 1) + (1 - core) * (v >> 1)
        bit_b = core * (v >> 1) + (1 - core) * ((v ^ (v >> 1)) & 1)
        n = n + m * (8 * bit_b + bit_a)
    return n


def fetch_cube(core_ref, mine, theirs, offset, w, sem, low, high):
    core = core_ref[0]

    def step(k, carry):
        y, z, x = (k >> 2) & 3, k & 3, (low >> 1) + (k >> 4)
        for src, own in ((mine, core), (theirs, 1 - core)):
            row = (y * 2 + (z >> 1)) * 2 + own
            first = ((k >> 4) * 2 + (z & 1)) * 9
            pltpu.make_async_copy(
                src.at[slot_at(y, z, x, own), pl.ds(offset, 9)], w.at[row, pl.ds(first, 9)], sem).start()
        return carry

    lax.fori_loop(0, 8 * (high - low), step, 0, unroll=4)


COMES = {(0, 0): ("cube", 0), (0, 1): ("cube", 0), (0, 2): ("plain", 0),
         (1, 0): ("cube", 9), (1, 1): ("plain", 0), (1, 2): ("plain", 72)}


def fetch(layer, group, core_ref, sources, w, sem, low, high):
    kind, first = COMES[layer, group]
    if kind == "cube":
        fetch_cube(core_ref, sources[0], sources[1], first, w, sem, low, high)
    else:
        tiles = pl.ds(first + 9 * low, 9 * (high - low))
        pltpu.make_async_copy(sources[0].at[:, tiles], w, sem).start()


def sources_of(layer, groups, refs):
    out, at = {}, 0
    for group in groups:
        n = 2 if COMES[layer, group][0] == "cube" else 1
        out[group] = refs[at : at + n]
        at += n
    return out, refs[at:]


def arrived(w, sem):
    pltpu.make_async_copy(w, w, sem).wait()


def units(w, first, count):
    parts = [w[:, 3 * (first + i) : 3 * (first + i) + 3].reshape(D, 128) for i in range(count)]
    return parts[0] if count == 1 else jnp.concatenate(parts, axis=1)


def tall_units(w, cb):
    return w[:, 12 * cb : 12 * cb + 12].reshape(4 * D, 128)


def mul(a, b):
    return jnp.dot(a, b, preferred_element_type=f32)


def mul_t(a, b):
    return lax.dot_general(a, b, (((1,), (1,)), ((), ())), preferred_element_type=f32)


def t_mul(a, b):
    return lax.dot_general(a, b, (((0,), (0,)), ((), ())), preferred_element_type=f32)


def norm_parts(values):
    centre = values - jnp.mean(values, axis=-1, keepdims=True)
    var = jnp.mean(centre * centre, axis=-1, keepdims=True)
    r = lax.rsqrt(var + norm_eps)
    return centre * r, r


def norm_back(cot, gain, xh, r):
    cg = cot * gain
    return r * (cg - jnp.mean(cg, axis=-1, keepdims=True) - xh * jnp.mean(cg * xh, axis=-1, keepdims=True))


def rows_sum(values):
    return jnp.sum(values, axis=0, keepdims=True)


def windows(values):
    out = []
    for x in range(4):
        for zl in range(2):
            own, shared = 3 * x + 2 * zl, 3 * x + 1
            out.append(jnp.concatenate([values[:, 64 * own : 64 * own + 64],
                                        values[:, 64 * shared : 64 * shared + 64]], axis=1))
    return out


def unwindow(get):
    parts = []
    for x in range(4):
        lo, hi = get(2 * x), get(2 * x + 1)
        parts += [lo[:, :64], lo[:, 64:] + hi[:, 64:], hi[:, :64]]
    return jnp.concatenate(parts, axis=1)


def gelu_both(u):
    k = 0.7978845608028654
    t = jnp.tanh(k * (u + 0.044715 * u * u * u))
    half = 0.5 * (1.0 + t)
    return u * half, half + 0.5 * u * (1.0 - t * t) * (k * (1.0 + 3 * 0.044715 * u * u))


def project_kernel(layer, core, h_ref, vec, *refs):
    src, (a1_ref, pay_ref, w, sem) = sources_of(layer, (0,), refs)
    fetch(layer, 0, core, src[0], w, sem, 0, 6)
    project(h_ref, vec, a1_ref, pay_ref, w, sem)


def project(h_ref, vec, a1_ref, pay_ref, w, sem):
    xh, _ = norm_parts(h_ref[...].astype(f32))
    a1 = (xh * vec[0:1] + vec[1:2]).astype(bf16)
    a1_ref[...] = a1
    arrived(w, sem)
    for part in range(3):
        cols = [mul(a1, units(w, 6 * part + 2 * j, 2)) for j in range(3)]
        got = jnp.concatenate(cols, axis=1)
        if part != 1:
            got = got + vec[2 + part // 2 : 3 + part // 2]
        got = got.astype(bf16).astype(f32)
        for d, win in enumerate(windows(got)):
            pay_ref[d, :, 128 * part : 128 * part + 128] = win.astype(bf16)


def masked(scores, first_block, second_block, idc_ref, idr_ref):
    n = scores.shape[1]
    ids = jnp.concatenate([idc_ref[first_block], idc_ref[second_block]], axis=0)
    row = lax.broadcasted_iota(jnp.int32, (2 * TOK, n), 0)
    qpos = row + jnp.where(row < TOK, first_block * TOK, (second_block - 1) * TOK)
    seen = (ids == idr_ref[:, 0:n]) & (lax.broadcasted_iota(jnp.int32, (2 * TOK, n), 1) <= qpos)
    return jnp.where(seen, scores, hidden_value)


def head_pairs(par):
    return ([(0, 2 * i, 2 * i + 1, 2 * i + 2) for i in range(4)]
            + [(1, 4 * i + par, 4 * i + 2 + par, 4 * i + 4) for i in range(2)])


def half(values, head):
    return values[:, 64 * head : 64 * head + 64]


def two_blocks(ref, first, second, lanes, head):
    return jnp.concatenate([half(ref[first, :, lanes], head), half(ref[second, :, lanes], head)], axis=0)


def store_blocks(out, par, results):
    for b in range(8):
        own = results[b // 2][TOK * (b % 2) : TOK * (b % 2) + TOK]
        shared = results[4 + b // 4][TOK * (b // 2 % 2) : TOK * (b // 2 % 2) + TOK]
        shared = jnp.where(par == b % 2, shared, 0.0)
        out[b, :, 0:128] = jnp.concatenate([own, shared], axis=1).astype(bf16)


def weights_of(q, key, *where):
    s = masked(mul_t(q, key), *where)
    e = jnp.exp(s - jnp.max(s, axis=1, keepdims=True))
    return e * (1.0 / jnp.sum(e, axis=1, keepdims=True))


def attend_kernel(par_ref, heads, idc, idr, out):
    par = par_ref[0]
    key = heads[:, :, 128:256].reshape(SLOTS, 128)
    val = heads[:, :, 256:384].reshape(SLOTS, 128)
    keys, vals = [half(key, h) for h in range(2)], [half(val, h) for h in range(2)]
    results = []
    for head, first, second, count in head_pairs(par):
        n = count * TOK
        q = two_blocks(heads, first, second, slice(0, 128), head) * score_scale
        p = weights_of(q, keys[head][:n], first, second, idc, idr).astype(bf16)
        results.append(mul(p, vals[head][:n]))
    store_blocks(out, par, results)


def attend_back_kernel(par_ref, heads, cot, idc, idr, out, dk_acc, dv_acc):
    par = par_ref[0]
    key = heads[:, :, 128:256].reshape(SLOTS, 128)
    val = heads[:, :, 256:384].reshape(SLOTS, 128)
    keys, vals = [half(key, h) for h in range(2)], [half(val, h) for h in range(2)]
    dk_acc[...] = jnp.zeros_like(dk_acc)
    dv_acc[...] = jnp.zeros_like(dv_acc)
    results = []
    for head, first, second, count in head_pairs(par):
        n = count * TOK
        q = two_blocks(heads, first, second, slice(0, 128), head) * score_scale
        g = two_blocks(cot, first, second, slice(0, 128), head)
        p = weights_of(q, keys[head][:n], first, second, idc, idr)
        dp = mul_t(g, vals[head][:n])
        ds = (p * (dp - jnp.sum(p * dp, axis=1, keepdims=True))).astype(bf16)
        results.append(mul(ds, keys[head][:n]) * score_scale)
        dk_acc[head, 0:n] += t_mul(ds, q)
        dv_acc[head, 0:n] += t_mul(p.astype(bf16), g)
    store_blocks(out, par, results)
    dk = jnp.concatenate([dk_acc[0], dk_acc[1]], axis=1)
    dv = jnp.concatenate([dv_acc[0], dv_acc[1]], axis=1)
    out[:, :, 128:256] = dk.astype(bf16).reshape(8, TOK, 128)
    out[:, :, 256:384] = dv.astype(bf16).reshape(8, TOK, 128)


def fetch_forward(layer, core, src, wo, wu, wd, sems):
    fetch(layer, 0, core, src[0], wo, sems.at[0], 6, 8)
    fetch(layer, 1, core, src[1], wu, sems.at[1], 0, 8)
    fetch(layer, 2, core, src[2], wd, sems.at[2], 0, 8)


def forward(h_ref, back, vec, upb, o_ref, h1_ref, a2_ref, u_ref, next_ref, wo, wu, wd, sems):
    o = unwindow(lambda d: back[d].astype(f32)).astype(bf16)
    o_ref[...] = o
    arrived(wo, sems.at[0])
    got = jnp.concatenate([mul(o, units(wo, 2 * j, 2)) for j in range(3)], axis=1)
    h1 = h_ref[...].astype(f32) + got + vec[2:3]
    h1_ref[...] = h1
    xh, _ = norm_parts(h1)
    a2 = (xh * vec[0:1] + vec[1:2]).astype(bf16)
    a2_ref[...] = a2
    arrived(wu, sems.at[1])
    acts = []
    for j in range(12):
        u = mul(a2, units(wu, 2 * j, 2)) + upb[:, 256 * j : 256 * j + 256]
        u_ref[:, 256 * j : 256 * j + 256] = u
        acts.append(gelu_both(u)[0].astype(bf16))
    f = jnp.concatenate(acts, axis=1)
    arrived(wd, sems.at[2])
    for j in range(3):
        w = jnp.concatenate([tall_units(wd, 2 * j), tall_units(wd, 2 * j + 1)], axis=1)
        c = slice(256 * j, 256 * j + 256)
        next_ref[:, c] = (h1[:, c] + mul(f, w) + vec[3:4, c]).astype(next_ref.dtype)


def forward_kernel(core, h_ref, back, vec, upb, *refs):
    src, refs = sources_of(1, (0, 1, 2), refs)
    fetch_forward(1, core, src, *refs[5:])
    forward(h_ref, back, vec, upb, *refs)


def forward_project_kernel(core, h_ref, back, vec, upb, vec_next, *refs):
    src, refs = sources_of(0, (0, 1, 2), refs)
    src_next, refs = sources_of(1, (0,), refs)
    outs, (a1_ref, pay_ref), ws, (w, sem) = refs[:5], refs[5:7], refs[7:11], refs[11:]
    fetch_forward(0, core, src, *ws)
    fetch(1, 0, core, src_next[0], w, sem, 0, 6)
    forward(h_ref, back, vec, upb, *outs, *ws)
    project(outs[4], vec_next, a1_ref, pay_ref, w, sem)


def fetch_backward(layer, core, src, wo, wu, wd, sems):
    fetch(layer, 2, core, src[2], wd, sems.at[2], 0, 8)
    fetch(layer, 1, core, src[1], wu, sems.at[1], 0, 8)
    fetch(layer, 0, core, src[0], wo, sems.at[0], 6, 8)


def backward(e_ref, u_ref, h1_ref, vec, f_ref, du_ref, e1_ref, pay_ref, small_ref, upb_ref, wo, wu, wd, sems):
    e = e_ref[...].astype(f32)
    e2 = e.astype(bf16)
    arrived(wd, sems.at[2])
    df = jnp.zeros((TOK, 4 * D), f32)
    for j in range(3):
        w = jnp.concatenate([tall_units(wd, 2 * j), tall_units(wd, 2 * j + 1)], axis=1)
        df = df + mul_t(e2[:, 256 * j : 256 * j + 256], w)
    arrived(wu, sems.at[1])
    cot = jnp.zeros((TOK, D), f32)
    for j in range(12):
        c = slice(256 * j, 256 * j + 256)
        f, slope = gelu_both(u_ref[:, c])
        f_ref[:, c] = f.astype(bf16)
        du = (df[:, c] * slope).astype(bf16)
        du_ref[:, c] = du
        upb_ref[:, c] = rows_sum(du.astype(f32))
        cot = cot + mul_t(du, units(wu, 2 * j, 2))
    xh, r = norm_parts(h1_ref[...])
    e1 = e + norm_back(cot, vec[0:1], xh, r)
    e1_ref[...] = e1
    b1 = e1.astype(bf16)
    small_ref[0:1] = rows_sum(cot * xh)
    small_ref[1:2] = rows_sum(cot)
    small_ref[2:3] = rows_sum(b1.astype(f32))
    small_ref[3:4] = rows_sum(e2.astype(f32))
    arrived(wo, sems.at[0])
    do = jnp.zeros((TOK, D), f32)
    for j in range(3):
        do = do + mul_t(b1[:, 256 * j : 256 * j + 256], units(wo, 2 * j, 2))
    do = do.astype(bf16).astype(f32)
    for d, win in enumerate(windows(do)):
        pay_ref[d] = win.astype(bf16)


def backward_kernel(core, e_ref, u_ref, h1_ref, vec, *refs):
    src, refs = sources_of(1, (0, 1, 2), refs)
    fetch_backward(1, core, src, *refs[6:])
    backward(e_ref, u_ref, h1_ref, vec, *refs)


def back_project(back, e1_ref, h_ref, vec, g_ref, e_ref, small_ref, w, sem):
    for part in range(3):
        got = unwindow(lambda d: back[d, :, 128 * part : 128 * part + 128].astype(f32)).astype(bf16)
        g_ref[:, D * part : D * part + D] = got
        if part != 1:
            small_ref[2 + part // 2 : 3 + part // 2] = rows_sum(got.astype(f32))
    arrived(w, sem)
    cot = jnp.zeros((TOK, D), f32)
    for j in range(9):
        cot = cot + mul_t(g_ref[:, 256 * j : 256 * j + 256], units(w, 2 * j, 2))
    xh, r = norm_parts(h_ref[...].astype(f32))
    small_ref[0:1] = rows_sum(cot * xh)
    small_ref[1:2] = rows_sum(cot)
    e_ref[...] = e1_ref[...] + norm_back(cot, vec[0:1], xh, r)


def back_project_kernel(core, back, e1_ref, h_ref, vec, *refs):
    src, refs = sources_of(0, (0,), refs)
    fetch(0, 0, core, src[0], *refs[3:], 0, 6)
    back_project(back, e1_ref, h_ref, vec, *refs)


def back_both_kernel(core, back, e1_ref, h_ref, vec, u_ref, h1_ref, vec_next, *refs):
    src, refs = sources_of(1, (0,), refs)
    src_next, refs = sources_of(0, (0, 1, 2), refs)
    outs, outs_next, (w, sem), ws = refs[:3], refs[3:9], refs[9:11], refs[11:]
    fetch(1, 0, core, src[0], w, sem, 0, 6)
    fetch_backward(0, core, src_next, *ws)
    back_project(back, e1_ref, h_ref, vec, *outs, w, sem)
    backward(outs[1], u_ref, h1_ref, vec_next, *outs_next, *ws)


def cube_store(core, stage, first_tile, triple, k, rows):
    for row in range(16):
        target = row & 1
        tile = first_tile + 3 * k
        stage[core ^ target, SLOT_OF[(target, row, triple)], tile : tile + 3] = rows[row].reshape(3, 16, 128)


def plain_store(stage, unit, rows):
    stage[:, 3 * unit : 3 * unit + 3] = rows.reshape(16, 3, 16, 128)


def wide_grad(at, b, first, store):
    for j in range(b.shape[1] // D):
        wide = mul(at, b[:, D * j : D * j + D])
        for i in range(6):
            store(first + 6 * j + i, wide[:, 128 * i : 128 * i + 128].astype(bf16).reshape(16, 48, 128))


def tall_grad(ft, b, store):
    for j in range(3):
        wide = mul(ft, b[:, 256 * j : 256 * j + 256])
        for i in range(2):
            rows = wide[:, 128 * i : 128 * i + 128].astype(bf16).reshape(16, 4, 48, 128)
            for q in range(4):
                store(4 * (2 * j + i) + q, rows[:, q])


def low(ref):
    return ref[...].astype(f32).astype(bf16)


def ship(pairs, sem):
    copies = [pltpu.make_async_copy(src, dst, sem.at[k]) for k, (src, dst) in enumerate(pairs)]
    for copy in copies:
        copy.start()
    for copy in copies:
        copy.wait()


def grad_mlp_cube(core_ref, f_ref, e_ref, a2_ref, du_ref, keep, send, stage, sem):
    core = core_ref[0]
    tall_grad(f_ref[...].T, low(e_ref), lambda u, rows: cube_store(core, stage, 9, u // 3, u % 3, rows))
    wide_grad(a2_ref[...].T, du_ref[...], 0, lambda u, rows: cube_store(core, stage, 0, u // 3, u % 3, rows))
    ship(((stage.at[0], keep), (stage.at[1], send)), sem)


def grad_joint_cube(core_ref, a_ref, g_ref, o_ref, e1_ref, keep, send, stage, sem):
    core = core_ref[0]
    put = lambda u, rows: cube_store(core, stage, 0, u // 3, u % 3, rows)
    wide_grad(a_ref[...].T, g_ref[...], 0, put)
    wide_grad(o_ref[...].T, low(e1_ref), 18, put)
    ship(((stage.at[0], keep), (stage.at[1], send)), sem)


def grad_mlp_split(core_ref, f_ref, e_ref, a2_ref, du_ref, keep, send, plain, stage, wide, sem):
    core = core_ref[0]

    def put(u, rows):
        triple, k = divmod(u, 3)
        if k == 2:
            cube_store(core, stage, 0, triple, 0, rows)
        else:
            plain_store(wide, 2 * triple + k, rows)

    wide_grad(a2_ref[...].T, du_ref[...], 0, put)
    tall_grad(f_ref[...].T, low(e_ref), lambda u, rows: plain_store(wide, 16 + u, rows))
    ship(((stage.at[0], keep), (stage.at[1], send), (wide, plain)), sem)


def out_place(l, group, u):
    cube = ((0, 0), (1, 0), (0, 1), (0, 2))
    triple, k = divmod(u, 3)
    if (l, group) in cube:
        return triple, 3 * cube.index((l, group)) + k
    if group == 2:
        return None, 29 + u
    return (triple, 12) if k == 2 else (None, 13 + 2 * triple + k)


CUBE_IN, PLAIN_IN = ((0, 0), (0, 1), (1, 0)), ((0, 2), (1, 1), (1, 2))


def dense(pieces, tiles):
    left = 16 * tiles - 6 * len(pieces)
    rows = jnp.concatenate(pieces + ([jnp.zeros((left, 128), f32)] if left else []), axis=0)
    return rows.astype(bf16).reshape(tiles, 16, 128)


def pack_kernel(win, wout, wup, wdown, order, pay):
    ins = [win[...].astype(f32), wout[...].astype(f32)]
    wide = wup[...].astype(f32)
    stack = [wide[:, l, 384 * m : 384 * m + 384] for l in range(LAYERS) for m in range(8)]
    stack = mul(jnp.concatenate(stack, axis=0).astype(bf16), order[...])
    ups = [[stack[48 * l + 6 * m : 48 * l + 6 * m + 6] for m in range(8)] for l in range(LAYERS)]
    firsts = [[v[:, l] for v in ins] for l in range(LAYERS)]
    downs = [wdown[l].astype(f32) for l in range(LAYERS)]

    def get(l, group, u):
        if group == 0:
            wide, at = (firsts[l][0], u) if u < 18 else (firsts[l][1], u - 18)
            return wide[:, 128 * at : 128 * at + 128]
        if group == 1:
            return ups[l][u // 3][:, 128 * (u % 3) : 128 * (u % 3) + 128]
        cb, q = divmod(u, 4)
        return downs[l][6 * q : 6 * q + 6, 128 * cb : 128 * cb + 128]

    plain = dense([get(*key, u) for key in PLAIN_IN for u in range(24)], 27)
    for d in range(8):
        pay[d, 0:27] = plain
        pay[d, 27:31] = dense([get(*key, 3 * d + i) for key in CUBE_IN for i in range(3)], 4)


def regroup_kernel(got, smalls, first, third, fourth):
    plain = [got[d, 0:27].astype(f32).reshape(432, 128) for d in range(8)]
    cube = [got[d, 27:31].astype(f32).reshape(64, 128) for d in range(8)]

    def join(rows, u):
        return jnp.concatenate([v[6 * u : 6 * u + 6] for v in rows], axis=0).astype(bf16).reshape(3, 16, 128)

    first[9] = smalls[...]
    for u in range(9):
        tile = 3 * u if u < 3 else 3 * u + 1
        first[tile : tile + 3] = join(cube, u)
    for u in range(24):
        third[3 * u : 3 * u + 3] = join(plain, u)
    for u in range(48):
        fourth[3 * u : 3 * u + 3] = join(plain, 24 + u)


def first_project_kernel(core, h_ref, mine, theirs, *refs):
    outs, (w, sem, buf, small_sem) = refs[:7], refs[7:]
    vecs = outs[2:]
    fetch(0, 0, core, (mine, theirs), w, sem, 0, 6)
    small_parameters(core, mine, theirs, vecs[:4], vecs[4], buf, small_sem)
    project(h_ref, vecs[0], outs[0], outs[1], w, sem)


def small_parameters(core_ref, mine, theirs, vecs, few, buf, sem):
    core = core_ref[0]

    def step(n, carry):
        for src, own in ((mine, core), (theirs, 1 - core)):
            row, triple = place(n, own)
            pltpu.make_async_copy(src.at[n, 9], buf.at[row * 8 + triple], sem).start()
        return carry

    lax.fori_loop(0, 64, step, 0)
    pltpu.make_async_copy(buf, buf, sem).wait()
    rows = buf[...].astype(f32)
    low_part, high_part = rows[:, 0], rows[:, 1]
    few[:, 0:128] = low_part
    few[:, 128:256] = high_part
    low_part = low_part.astype(bf16)
    value = lax.broadcasted_iota(jnp.int32, (128, 16), 0) - 6 * lax.broadcasted_iota(jnp.int32, (128, 16), 1)
    place_in = lax.broadcasted_iota(jnp.int32, (128, D), 1) - 6 * lax.broadcasted_iota(jnp.int32, (128, D), 0)
    total = jnp.zeros((16, D), f32)
    for i in range(6):
        picked = mul(low_part, (value == i).astype(f32).astype(bf16)).astype(bf16)
        total = total + t_mul(picked, (place_in == i).astype(f32).astype(bf16))
    for l in range(LAYERS):
        for k, i in enumerate((2 * l, 4 + 2 * l, 8 + 2 * l, 9 + 2 * l)):
            vecs[2 * l][k : k + 1] = total[i : i + 1]
        for k, i in enumerate((2 * l + 1, 5 + 2 * l, 12 + 2 * l, 13 + 2 * l)):
            vecs[2 * l + 1][k : k + 1] = total[i : i + 1]


def finish_kernel(parts, total, out, few):
    small = jnp.zeros((2, 128), f32)
    for k in range(8):
        small = small + parts[k, 9].astype(f32)[0:2]
    few[...] = small
    units_of = []
    for u in range(13):
        tile = 3 * u if u < 3 else 3 * u + 1
        rows = jnp.zeros((48, 128), f32)
        for k in range(8):
            rows = rows + parts[k, tile : tile + 3].reshape(48, 128).astype(f32)
        units_of.append(rows)
    for u in range(40):
        units_of.append(total[3 * u : 3 * u + 3].reshape(48, 128).astype(f32))
    for d in range(8):
        out[d] = dense([rows[6 * d : 6 * d + 6] for rows in units_of], 20)


def unpack_kernel(got, order, g_in, g_out, g_up, g_down):
    cube = [got[d, 0:5].reshape(80, 128).astype(f32) for d in range(8)]
    plain = got[0].reshape(320, 128).astype(f32)
    for d in range(1, 8):
        plain = plain + got[d].reshape(320, 128).astype(f32)
    stack = []
    for l in range(LAYERS):
        for group in range(3):
            rows = []
            for u in range(24):
                triple, k = out_place(l, group, u)
                rows.append((plain if triple is None else cube[triple])[6 * k : 6 * k + 6])
            if group == 0:
                g_in[:, l] = jnp.concatenate(rows[:18], axis=1)
                g_out[:, l] = jnp.concatenate(rows[18:], axis=1)
            elif group == 1:
                stack += [jnp.concatenate(rows[3 * m : 3 * m + 3], axis=1) for m in range(8)]
            else:
                for u in range(24):
                    cb, q = divmod(u, 4)
                    g_down[l, 6 * q : 6 * q + 6, 128 * cb : 128 * cb + 128] = rows[u]
    left = jnp.concatenate(stack, axis=0)
    terms = []
    for _ in range(3):
        terms.append(left.astype(bf16))
        left = left - terms[-1].astype(f32)
    wide = mul_t(jnp.concatenate(terms, axis=0), order[...])
    wide = wide[0:96] + wide[96:192] + wide[192:288]
    for l in range(LAYERS):
        for m in range(8):
            g_up[:, l, 384 * m : 384 * m + 384] = wide[48 * l + 6 * m : 48 * l + 6 * m + 6]


def call(kernel, outs, ins, scratch=(), us=3, out_spaces=None, aliases=None):
    spaces = {"s": pltpu.SMEM, "v": pltpu.VMEM, "a": pl.ANY}
    return pl.pallas_call(
        kernel,
        out_shape=[jax.ShapeDtypeStruct(*o) for o in outs],
        in_specs=[pl.BlockSpec(memory_space=spaces[m]) for _, m in ins],
        out_specs=[pl.BlockSpec(memory_space=spaces[m]) for m in (out_spaces or "v" * len(outs))],
        scratch_shapes=list(scratch),
        input_output_aliases=aliases or {},
        compiler_params=pltpu.CompilerParams(vmem_limit_bytes=56 * 1024 * 1024),
        cost_estimate=pl.CostEstimate(flops=0, bytes_accessed=us * 3690000, transcendentals=0),
    )(*[a for a, _ in ins])


def w_scratch(count):
    return pltpu.VMEM((16, 3 * count, 16, 128), bf16)


DMA = pltpu.SemaphoreType.DMA


def after(values, *others):
    return lax.optimization_barrier((values,) + others)[0] if others else values


def copies(values, groups, *others):
    many = after(jnp.broadcast_to(values[None], (8,) + values.shape), *others)
    return lax.all_to_all(many, ALL, 0, 0, axis_index_groups=groups)


def sum_first(values):
    return jnp.sum(values.astype(f32), axis=0)


def swap_core(values):
    return lax.ppermute(values, "c", [(0, 1), (1, 0)])


def cube_copies(shards, *others):
    return copies(shards, GROUPS_B, *others).reshape((64,) + shards.shape[1:])


def spread(shards):
    mine = cube_copies(shards)
    return mine, swap_core(mine)


def add_kernel(*refs):
    out, first = refs[-1], 0
    for keep, got in zip(refs[0:-1:2], refs[1:-1:2]):
        n = keep.shape[1]
        out[:, first : first + n] = (keep[...].astype(f32) + got[...].astype(f32)).astype(bf16)
        first += n


def add_pairs(pairs):
    total = sum(a.shape[1] for a, _ in pairs)
    flat = [v for pair in pairs for v in pair]

    def spec(t):
        return pl.BlockSpec((8, t, 16, 128), lambda i: (i, 0, 0, 0))

    return pl.pallas_call(
        add_kernel,
        grid=(8,),
        out_shape=jax.ShapeDtypeStruct((64, total, 16, 128), bf16),
        in_specs=[spec(v.shape[1]) for v in flat],
        out_specs=spec(total),
        compiler_params=pltpu.CompilerParams(vmem_limit_bytes=56 * 1024 * 1024),
        cost_estimate=pl.CostEstimate(flops=2**22, bytes_accessed=3 * 64 * total * 4096, transcendentals=0),
    )(*flat)


def core_sums(pairs):
    return add_pairs([(keep, swap_core(send)) for keep, send in pairs])


def gather_sums(part):
    part = part.reshape((8, 8) + part.shape[1:])
    return sum_first(lax.all_to_all(part, ALL, 0, 0, axis_index_groups=GROUPS_B)).astype(bf16)


def token_ids(group_index, positions, sequence_group, sequence_start, sequence_length):
    member = (
        (sequence_group[None, :] == group_index)
        & (sequence_start[None, :] <= positions[:, None])
        & (positions[:, None] < (sequence_start + sequence_length)[None, :])
    )
    numbers = jnp.arange(sequence_group.shape[0], dtype=jnp.int32) + 1
    located = jnp.sum(jnp.where(member, numbers[None, :], 0), axis=1)
    return jnp.where(located > 0, located - 1, -1 - positions)


def body(hidden_in, out_grad, sequence_group, sequence_start, sequence_length, norm_gain, norm_bias,
         input_weight, input_bias, output_weight, branch_bias, up_weight, up_bias, down_weight):
    core = lax.axis_index("c").astype(jnp.int32).reshape(1)
    par = lax.axis_index("zl").astype(jnp.int32).reshape(1)
    positions = jnp.arange(SLOTS, dtype=jnp.int32)
    ids = token_ids(lax.axis_index(DATA), positions, sequence_group, sequence_start, sequence_length)
    idc, idr = ids.reshape(CTX_DEV, TOK, 1), ids.reshape(1, SLOTS)

    order = jnp.asarray(FF_ORDER, bf16)
    smalls = jnp.concatenate([v.reshape(-1) for v in (norm_gain, norm_bias, input_bias, branch_bias, up_bias)])
    smalls = jnp.pad(smalls, (0, 2048 - 144)).reshape(16, 128)
    (pay,) = call(pack_kernel, [((8, 31, 16, 128), bf16)],
                  [(jnp.swapaxes(v, 0, 1), "v") for v in (input_weight, output_weight, up_weight)]
                  + [(down_weight, "v"), (order, "v")])
    got = lax.all_to_all(pay, CTX, 0, 0)
    first, third, fourth = call(
        regroup_kernel,
        [((28, 16, 128), bf16), ((72, 16, 128), bf16), ((144, 16, 128), bf16)],
        [(got, "v"), (smalls, "v")])
    down_0 = lax.all_gather(third, DATA, axis=0, tiled=False)
    shards = copies(first, GROUPS_A)
    group_e, shards = spread(shards[:, :10]), shards[:, 10:]
    shards = jnp.broadcast_to(shards[None], (8,) + shards.shape)
    group_e = tuple(after(v, shards) for v in group_e)
    sources = {(0, 0): group_e, (0, 2): (down_0,)}

    a1, pay, *vecs, few = call(
        first_project_kernel,
        [((TOK, D), bf16), ((8, TOK, 384), bf16)] + [((4, D), f32)] * 4 + [((128, 256), f32)],
        [(core, "s"), (hidden_in[0], "v"), (group_e[0], "a"), (group_e[1], "a")],
        [w_scratch(18), DMA, pltpu.VMEM((128, 16, 128), bf16), DMA], us=7)
    ups = few[:, 96:144].reshape(16, 8, 2, 4, 6).transpose(2, 0, 3, 1, 4).reshape(2, 4 * D)

    def weights(l, all_groups):
        return [(w, "a") for group in range(3 if all_groups else 1) for w in sources[l, group]]

    def attend(heads):
        return call(attend_kernel, [((8, TOK, 128), bf16)],
                    [(par, "s"), (heads, "v"), (idc, "v"), (idr, "v")], us=6)[0]

    def attend_back(heads, cot):
        return call(attend_back_kernel, [((8, TOK, 384), bf16)],
                    [(par, "s"), (heads, "v"), (cot, "v"), (idc, "v"), (idr, "v")],
                    [pltpu.VMEM((2, SLOTS, 64), f32)] * 2, us=8)[0]

    def exchange(values):
        return lax.all_to_all(values, CTX, 0, 0)

    block_scratch = [w_scratch(6), w_scratch(24), w_scratch(24), DMA((3,))]
    project_scratch = [w_scratch(18), DMA]
    project_outs = [((TOK, D), bf16), ((8, TOK, 384), bf16)]
    forward_outs = [((TOK, D), bf16), ((TOK, D), f32), ((TOK, D), bf16), ((TOK, 4 * D), f32)]
    backward_outs = [((TOK, 4 * D), bf16), ((TOK, 4 * D), bf16), ((TOK, D), f32), ((8, TOK, 128), bf16),
                     ((4, D), f32), ((1, 4 * D), f32)]
    back_project_outs = [((TOK, 3 * D), bf16), ((TOK, D), f32), ((4, D), f32)]

    hidden_0 = hidden_in[0]
    both_1 = lax.all_gather(after(fourth, a1), DATA, axis=0, tiled=False)
    sources[1, 1] = sources[1, 2] = (both_1,)
    a1 = [a1, None]
    heads_0 = exchange(pay)
    mine = lax.all_to_all(after(shards, heads_0, down_0), ALL, 0, 0, axis_index_groups=GROUPS_B)
    mine = mine.reshape((64,) + mine.shape[2:])
    mix = attend(heads_0)
    theirs = swap_core(after(mine, mix))
    sources[0, 1] = sources[1, 0] = (mine, theirs)
    back = exchange(after(mix, mine))
    o_0, h1_0, a2_0, u_0, hidden_1, a1[1], pay = call(
        forward_project_kernel,
        forward_outs + [((TOK, D), f32)] + project_outs,
        [(core, "s"), (hidden_0, "v"), (back, "v"), (vecs[1], "v"), (ups[0:1], "v"), (vecs[2], "v")]
        + weights(0, True) + weights(1, False),
        block_scratch + project_scratch, us=12)
    heads_1 = exchange(pay)
    back = exchange(attend(heads_1))
    o_1, h1_1, a2_1, u_1, hidden = call(
        forward_kernel,
        forward_outs + [((TOK, D), bf16)],
        [(core, "s"), (hidden_1, "v"), (back, "v"), (vecs[3], "v"), (ups[1:2], "v")] + weights(1, True),
        block_scratch, us=8)

    def grad_joint(a1, g, o, e1):
        return call(
            grad_joint_cube, [((64, 9, 16, 128), bf16)] * 2,
            [(core, "s"), (a1, "v"), (g, "v"), (o, "v"), (e1, "v")],
            [pltpu.VMEM((2, 64, 9, 16, 128), bf16), DMA((2,))], us=5, out_spaces="aa")

    grad = out_grad[0]
    few_rows, few_up, joint = [None] * 2, [None] * 2, [None] * 2
    f, du, e1, pay, small_b, few_up[1] = call(
        backward_kernel, backward_outs,
        [(core, "s"), (grad, "v"), (u_1, "v"), (h1_1, "v"), (vecs[3], "v")] + weights(1, True),
        block_scratch, us=10)
    cot = exchange(pay)
    keep_u, send_u, mlp_1 = call(
        grad_mlp_split, [((64, 3, 16, 128), bf16)] * 2 + [((16, 120, 16, 128), bf16)],
        [(core, "s"), (f, "v"), (grad, "v"), (a2_1, "v"), (du, "v")],
        [pltpu.VMEM((2, 64, 3, 16, 128), bf16), w_scratch(40), DMA((3,))], us=9, out_spaces="aaa")
    scattered = lax.psum_scatter(after(mlp_1, cot), DATA, scatter_dimension=0, tiled=False)
    back = exchange(attend_back(heads_1, after(cot, mlp_1)))
    e1_1, small_b1 = e1, small_b
    g_1, grad, small_a1, f, du, e1, pay, small_b, few_up[0] = call(
        back_both_kernel, back_project_outs + backward_outs,
        [(core, "s"), (back, "v"), (e1_1, "v"), (hidden_1, "v"), (vecs[2], "v"), (u_0, "v"), (h1_0, "v"),
         (vecs[1], "v")] + weights(1, False) + weights(0, True),
        project_scratch + block_scratch, us=16)
    cot = exchange(pay)
    keep_ud, send_ud = call(
        grad_mlp_cube, [((64, 18, 16, 128), bf16)] * 2,
        [(core, "s"), (f, "v"), (grad, "v"), (a2_0, "v"), (du, "v")],
        [pltpu.VMEM((2, 64, 18, 16, 128), bf16), DMA((2,))], us=9, out_spaces="aa")
    send_ud = after(send_ud, cot)
    back = exchange(attend_back(heads_0, after(cot, keep_ud)))
    middle = core_sums([(keep_ud, send_ud), (keep_u, send_u)])
    g_0, grad, small_a0 = call(
        back_project_kernel, back_project_outs,
        [(core, "s"), (after(back, middle), "v"), (e1, "v"), (hidden_0, "v"), (vecs[0], "v")] + weights(0, False),
        project_scratch, us=6)
    joint = [grad_joint(a1[0], g_0, o_0, e1), grad_joint(a1[1], g_1, o_1, e1_1)]
    for l, (first, second) in enumerate(((small_a0, small_b), (small_a1, small_b1))):
        few_rows[l] = jnp.concatenate([first[0:1], second[0:1], first[1:2], second[1:2], first[2:4], second[2:4]], axis=0)

    few = jnp.concatenate([r.reshape(8, 128, 6).transpose(1, 0, 2).reshape(128, 48) for r in few_rows]
                          + [r.reshape(16, 4, 8, 6).transpose(0, 2, 1, 3).reshape(128, 24) for r in few_up], axis=1)
    few = jnp.pad(few, ((0, 0), (0, 256 - 144))).astype(bf16)
    few = jnp.dot(jnp.asarray(TAIL_ORDER.T, bf16), few, preferred_element_type=f32).astype(bf16)
    few = jnp.pad(few.reshape(2, 64, 1, 2, 128), ((0, 0),) * 3 + ((0, 14), (0, 0)))
    few = [jnp.where(core[0] == k, few[0], few[1]) for k in range(2)]

    middle = gather_sums(middle)
    last = gather_sums(after(core_sums([joint[0], few, joint[1]]), middle, scattered))
    sums = jnp.concatenate([last, middle], axis=1)
    sums = lax.all_to_all(sums, ALL, 0, 0, axis_index_groups=GROUPS_A)
    sums, few = call(finish_kernel, [((8, 20, 16, 128), bf16), ((2, 128), f32)],
                     [(sums, "v"), (scattered, "v")])
    got = lax.all_to_all(sums, CTX, 0, 0)
    grad_in, grad_out, grad_up, grad_down = call(
        unpack_kernel,
        [((6, 2, 3 * D), f32), ((6, 2, D), f32), ((6, 2, 4 * D), f32), ((2, 24, D), f32)],
        [(got, "v"), (order, "v")])
    few = few.reshape(256)
    few_l = [few[48 * l : 48 * l + 48].reshape(4, 2, 6) for l in range(2)]

    def pair(k):
        return jnp.stack([few_l[0][k], few_l[1][k]])

    return (
        hidden[None],
        grad[None],
        pair(0),
        pair(1),
        jnp.swapaxes(grad_in, 0, 1),
        pair(2),
        jnp.swapaxes(grad_out, 0, 1),
        pair(3),
        jnp.swapaxes(grad_up, 0, 1),
        few[96:144].reshape(2, 24),
        grad_down,
    )


def solution(mesh):
    mesh = Mesh(mesh.devices.reshape(4, 2, 2, 4, 2), ALL)
    token = P(DATA, CTX, None)
    one = P(None, ALL)
    two = P(None, None, ALL)
    mat = P(None, ALL, None)
    return jax.shard_map(
        body,
        mesh=mesh,
        in_specs=(token, token, P(), P(), P(), two, two, mat, two, mat, two, mat, one, mat),
        out_specs=(token, token, two, two, mat, two, mat, two, mat, one, mat),
        check_vma=False,
    )
```

```python
import functools

import jax
import jax.numpy as jnp
import numpy as np
from jax import lax
from jax.experimental import pallas as pl
from jax.experimental.pallas import tpu as pltpu
from jax.sharding import Mesh, PartitionSpec as P

LAYERS = 2
D = 768
TOK = 128
CTX_DEV = 8
SLOTS = TOK * CTX_DEV
DATA = ("y", "zh", "c")
CTX = ("x", "zl")
ALL = DATA + CTX
bf16 = jnp.bfloat16
f32 = jnp.float32
norm_eps = 1e-05
score_scale = 0.125
hidden_value = -1000000000.0


def coord(bit_b, bit_a, core):
    return core * (2 * bit_b + bit_a) + (1 - core) * (3 * bit_a + bit_b * (1 - 2 * bit_a))


def place(n, core):
    y = coord((n >> 5) & 1, (n >> 2) & 1, core)
    z = coord((n >> 4) & 1, (n >> 1) & 1, core)
    x = coord((n >> 3) & 1, n & 1, core)
    return (y * 2 + (z >> 1)) * 2 + core, x * 2 + (z & 1)


SLOT_OF = {(c,) + place(n, c): n for c in range(2) for n in range(64)}


def tail_order():
    table = np.zeros((128, 128), np.float32)
    for (c, row, triple), n in SLOT_OF.items():
        table[row * 8 + triple, 64 * c + n] = 1.0
    return table


TAIL_ORDER = tail_order()


def device_id(y, z, core, x):
    return y * 32 + (z >> 1) * 16 + core * 8 + x * 2 + (z & 1)


def cube_groups(level):
    found = {}
    for core in range(2):
        for n in range(64):
            bits = [(n >> s) & 1 for s in range(6)]
            y, z, x = (coord(bits[3 + s], bits[s], core) for s in (2, 1, 0))
            if level == 1:
                key = (core,) + tuple(coord(bits[3 + s], 0, core) for s in (2, 1, 0))
                slot = n & 7
            else:
                pair = [coord(bits[3 + s], bits[s], core) for s in (2, 1, 0)]
                pair = [(v // 2 if core == 0 else ((v + 1) // 2) % 2) for v in pair]
                key = (core,) + tuple(pair)
                slot = n >> 3
            found.setdefault(key, [None] * 8)[slot] = device_id(y, z, core, x)
    return [found[k] for k in sorted(found)]


GROUPS_A = cube_groups(1)
GROUPS_B = cube_groups(0)


def ff_order():
    used = np.arange(384)
    block, q, ctx, r = used // 192, used // 48 % 4, used // 6 % 8, used % 6
    table = np.zeros((384, 384), np.float32)
    table[block * 192 + ctx * 24 + q * 6 + r, used] = 1.0
    return table


FF_ORDER = ff_order()


def slot_at(y, z, x, core):
    n = 0
    for v, m in ((y, 4), (z, 2), (x, 1)):
        bit_a = core * (v & 1) + (1 - core) * (v >> 1)
        bit_b = core * (v >> 1) + (1 - core) * ((v ^ (v >> 1)) & 1)
        n = n + m * (8 * bit_b + bit_a)
    return n


def fetch_cube(core_ref, mine, theirs, offset, w, sem, low, high):
    core = core_ref[0]

    def step(k, carry):
        y, z, x = (k >> 2) & 3, k & 3, (low >> 1) + (k >> 4)
        for src, own in ((mine, core), (theirs, 1 - core)):
            row = (y * 2 + (z >> 1)) * 2 + own
            first = ((k >> 4) * 2 + (z & 1)) * 9
            pltpu.make_async_copy(
                src.at[slot_at(y, z, x, own), pl.ds(offset, 9)], w.at[row, pl.ds(first, 9)], sem).start()
        return carry

    lax.fori_loop(0, 8 * (high - low), step, 0, unroll=4)


COMES = {(0, 0): ("cube", 0), (0, 1): ("cube", 0), (0, 2): ("plain", 0),
         (1, 0): ("cube", 9), (1, 1): ("plain", 0), (1, 2): ("plain", 72)}


def fetch(layer, group, core_ref, sources, w, sem, low, high):
    kind, first = COMES[layer, group]
    if kind == "cube":
        fetch_cube(core_ref, sources[0], sources[1], first, w, sem, low, high)
    else:
        tiles = pl.ds(first + 9 * low, 9 * (high - low))
        pltpu.make_async_copy(sources[0].at[:, tiles], w, sem).start()


def sources_of(layer, groups, refs):
    out, at = {}, 0
    for group in groups:
        n = 2 if COMES[layer, group][0] == "cube" else 1
        out[group] = refs[at : at + n]
        at += n
    return out, refs[at:]


def arrived(w, sem):
    pltpu.make_async_copy(w, w, sem).wait()


def units(w, first, count):
    parts = [w[:, 3 * (first + i) : 3 * (first + i) + 3].reshape(D, 128) for i in range(count)]
    return parts[0] if count == 1 else jnp.concatenate(parts, axis=1)


def tall_units(w, cb):
    return w[:, 12 * cb : 12 * cb + 12].reshape(4 * D, 128)


def mul(a, b):
    return jnp.dot(a, b, preferred_element_type=f32)


def mul_t(a, b):
    return lax.dot_general(a, b, (((1,), (1,)), ((), ())), preferred_element_type=f32)


def t_mul(a, b):
    return lax.dot_general(a, b, (((0,), (0,)), ((), ())), preferred_element_type=f32)


def norm_parts(values):
    centre = values - jnp.mean(values, axis=-1, keepdims=True)
    var = jnp.mean(centre * centre, axis=-1, keepdims=True)
    r = lax.rsqrt(var + norm_eps)
    return centre * r, r


def norm_back(cot, gain, xh, r):
    cg = cot * gain
    return r * (cg - jnp.mean(cg, axis=-1, keepdims=True) - xh * jnp.mean(cg * xh, axis=-1, keepdims=True))


def rows_sum(values):
    return jnp.sum(values, axis=0, keepdims=True)


def windows(values):
    out = []
    for x in range(4):
        for zl in range(2):
            own, shared = 3 * x + 2 * zl, 3 * x + 1
            out.append(jnp.concatenate([values[:, 64 * own : 64 * own + 64],
                                        values[:, 64 * shared : 64 * shared + 64]], axis=1))
    return out


def unwindow(get):
    parts = []
    for x in range(4):
        lo, hi = get(2 * x), get(2 * x + 1)
        parts += [lo[:, :64], lo[:, 64:] + hi[:, 64:], hi[:, :64]]
    return jnp.concatenate(parts, axis=1)


def gelu_both(u):
    k = 0.7978845608028654
    t = jnp.tanh(k * (u + 0.044715 * u * u * u))
    half = 0.5 * (1.0 + t)
    return u * half, half + 0.5 * u * (1.0 - t * t) * (k * (1.0 + 3 * 0.044715 * u * u))


def project_kernel(layer, core, h_ref, vec, *refs):
    src, (a1_ref, pay_ref, w, sem) = sources_of(layer, (0,), refs)
    fetch(layer, 0, core, src[0], w, sem, 0, 6)
    project(h_ref, vec, a1_ref, pay_ref, w, sem)


def project(h_ref, vec, a1_ref, pay_ref, w, sem):
    xh, _ = norm_parts(h_ref[...].astype(f32))
    a1 = (xh * vec[0:1] + vec[1:2]).astype(bf16)
    a1_ref[...] = a1
    arrived(w, sem)
    for part in range(3):
        cols = [mul(a1, units(w, 6 * part + 2 * j, 2)) for j in range(3)]
        got = jnp.concatenate(cols, axis=1)
        if part != 1:
            got = got + vec[2 + part // 2 : 3 + part // 2]
        got = got.astype(bf16).astype(f32)
        for d, win in enumerate(windows(got)):
            pay_ref[d, :, 128 * part : 128 * part + 128] = win.astype(bf16)


def masked(scores, first_block, second_block, idc_ref, idr_ref):
    n = scores.shape[1]
    ids = jnp.concatenate([idc_ref[first_block], idc_ref[second_block]], axis=0)
    row = lax.broadcasted_iota(jnp.int32, (2 * TOK, n), 0)
    qpos = row + jnp.where(row < TOK, first_block * TOK, (second_block - 1) * TOK)
    seen = (ids == idr_ref[:, 0:n]) & (lax.broadcasted_iota(jnp.int32, (2 * TOK, n), 1) <= qpos)
    return jnp.where(seen, scores, hidden_value)


def head_pairs(par):
    return ([(0, 2 * i, 2 * i + 1, 2 * i + 2) for i in range(4)]
            + [(1, 4 * i + par, 4 * i + 2 + par, 4 * i + 4) for i in range(2)])


def half(values, head):
    return values[:, 64 * head : 64 * head + 64]


def two_blocks(ref, first, second, lanes, head):
    return jnp.concatenate([half(ref[first, :, lanes], head), half(ref[second, :, lanes], head)], axis=0)


def store_blocks(out, par, results):
    for b in range(8):
        own = results[b // 2][TOK * (b % 2) : TOK * (b % 2) + TOK]
        shared = results[4 + b // 4][TOK * (b // 2 % 2) : TOK * (b // 2 % 2) + TOK]
        shared = jnp.where(par == b % 2, shared, 0.0)
        out[b, :, 0:128] = jnp.concatenate([own, shared], axis=1).astype(bf16)


def weights_of(q, key, *where):
    s = masked(mul_t(q, key), *where)
    e = jnp.exp(s - jnp.max(s, axis=1, keepdims=True))
    return e * (1.0 / jnp.sum(e, axis=1, keepdims=True))


def attend_kernel(par_ref, heads, idc, idr, out):
    par = par_ref[0]
    key = heads[:, :, 128:256].reshape(SLOTS, 128)
    val = heads[:, :, 256:384].reshape(SLOTS, 128)
    keys, vals = [half(key, h) for h in range(2)], [half(val, h) for h in range(2)]
    results = []
    for head, first, second, count in head_pairs(par):
        n = count * TOK
        q = two_blocks(heads, first, second, slice(0, 128), head) * score_scale
        p = weights_of(q, keys[head][:n], first, second, idc, idr).astype(bf16)
        results.append(mul(p, vals[head][:n]))
    store_blocks(out, par, results)


def attend_back_kernel(par_ref, heads, cot, idc, idr, out, dk_acc, dv_acc):
    par = par_ref[0]
    key = heads[:, :, 128:256].reshape(SLOTS, 128)
    val = heads[:, :, 256:384].reshape(SLOTS, 128)
    keys, vals = [half(key, h) for h in range(2)], [half(val, h) for h in range(2)]
    dk_acc[...] = jnp.zeros_like(dk_acc)
    dv_acc[...] = jnp.zeros_like(dv_acc)
    results = []
    for head, first, second, count in head_pairs(par):
        n = count * TOK
        q = two_blocks(heads, first, second, slice(0, 128), head) * score_scale
        g = two_blocks(cot, first, second, slice(0, 128), head)
        p = weights_of(q, keys[head][:n], first, second, idc, idr)
        dp = mul_t(g, vals[head][:n])
        ds = (p * (dp - jnp.sum(p * dp, axis=1, keepdims=True))).astype(bf16)
        results.append(mul(ds, keys[head][:n]) * score_scale)
        dk_acc[head, 0:n] += t_mul(ds, q)
        dv_acc[head, 0:n] += t_mul(p.astype(bf16), g)
    store_blocks(out, par, results)
    dk = jnp.concatenate([dk_acc[0], dk_acc[1]], axis=1)
    dv = jnp.concatenate([dv_acc[0], dv_acc[1]], axis=1)
    out[:, :, 128:256] = dk.astype(bf16).reshape(8, TOK, 128)
    out[:, :, 256:384] = dv.astype(bf16).reshape(8, TOK, 128)


def fetch_forward(layer, core, src, wo, wu, wd, sems):
    fetch(layer, 0, core, src[0], wo, sems.at[0], 6, 8)
    fetch(layer, 1, core, src[1], wu, sems.at[1], 0, 8)
    fetch(layer, 2, core, src[2], wd, sems.at[2], 0, 8)


def forward(h_ref, back, vec, upb, o_ref, h1_ref, a2_ref, u_ref, f_ref, next_ref, wo, wu, wd, sems):
    o = unwindow(lambda d: back[d].astype(f32)).astype(bf16)
    o_ref[...] = o
    arrived(wo, sems.at[0])
    got = jnp.concatenate([mul(o, units(wo, 2 * j, 2)) for j in range(3)], axis=1)
    h1 = h_ref[...].astype(f32) + got + vec[2:3]
    h1_ref[...] = h1
    xh, _ = norm_parts(h1)
    a2 = (xh * vec[0:1] + vec[1:2]).astype(bf16)
    a2_ref[...] = a2
    arrived(wu, sems.at[1])
    acts = []
    for j in range(12):
        c = slice(256 * j, 256 * j + 256)
        u = mul(a2, units(wu, 2 * j, 2)) + upb[:, c]
        act, slope = gelu_both(u)
        acts.append(act.astype(bf16))
        if f_ref is None:
            u_ref[:, c] = u
        else:
            u_ref[:, c] = slope
            f_ref[:, c] = acts[-1]
    f = jnp.concatenate(acts, axis=1)
    arrived(wd, sems.at[2])
    for j in range(3):
        w = jnp.concatenate([tall_units(wd, 2 * j), tall_units(wd, 2 * j + 1)], axis=1)
        c = slice(256 * j, 256 * j + 256)
        next_ref[:, c] = (h1[:, c] + mul(f, w) + vec[3:4, c]).astype(next_ref.dtype)


def last_kernel(core, h_ref, back, vec, upb, e_ref, *refs):
    src, refs = sources_of(1, (0, 1, 2), refs)
    o_ref, a2_ref, next_ref, f_ref, outs, h1, slope, ws = refs[0], refs[1], refs[2], refs[3], refs[4:9], refs[9], refs[10], refs[11:]
    fetch_forward(1, core, src, *ws)
    forward(h_ref, back, vec, upb, o_ref, h1, a2_ref, slope, f_ref, next_ref, *ws)
    backward(e_ref, slope, h1, vec, None, *outs, *ws[:3], None)


def forward_project_kernel(core, h_ref, back, vec, upb, vec_next, *refs):
    src, refs = sources_of(0, (0, 1, 2), refs)
    src_next, refs = sources_of(1, (0,), refs)
    outs, (a1_ref, pay_ref), ws, (w, sem) = refs[:5], refs[5:7], refs[7:11], refs[11:]
    fetch_forward(0, core, src, *ws)
    fetch(1, 0, core, src_next[0], w, sem, 0, 6)
    forward(h_ref, back, vec, upb, *outs[:4], None, outs[4], *ws)
    project(outs[4], vec_next, a1_ref, pay_ref, w, sem)


def fetch_backward(layer, core, src, wo, wu, wd, sems):
    fetch(layer, 2, core, src[2], wd, sems.at[2], 0, 8)
    fetch(layer, 1, core, src[1], wu, sems.at[1], 0, 8)
    fetch(layer, 0, core, src[0], wo, sems.at[0], 6, 8)


def backward(e_ref, u_ref, h1_ref, vec, f_ref, du_ref, e1_ref, pay_ref, small_ref, upb_ref, wo, wu, wd, sems):
    def arrive(w, k):
        if sems is not None:
            arrived(w, sems.at[k])

    e = e_ref[...].astype(f32)
    e2 = e.astype(bf16)
    arrive(wd, 2)
    df = jnp.zeros((TOK, 4 * D), f32)
    for j in range(3):
        w = jnp.concatenate([tall_units(wd, 2 * j), tall_units(wd, 2 * j + 1)], axis=1)
        df = df + mul_t(e2[:, 256 * j : 256 * j + 256], w)
    arrive(wu, 1)
    cot = jnp.zeros((TOK, D), f32)
    for j in range(12):
        c = slice(256 * j, 256 * j + 256)
        slope = u_ref[:, c]
        if f_ref is not None:
            f, slope = gelu_both(slope)
            f_ref[:, c] = f.astype(bf16)
        du = (df[:, c] * slope).astype(bf16)
        du_ref[:, c] = du
        upb_ref[:, c] = rows_sum(du.astype(f32))
        cot = cot + mul_t(du, units(wu, 2 * j, 2))
    xh, r = norm_parts(h1_ref[...])
    e1 = e + norm_back(cot, vec[0:1], xh, r)
    e1_ref[...] = e1
    b1 = e1.astype(bf16)
    small_ref[0:1] = rows_sum(cot * xh)
    small_ref[1:2] = rows_sum(cot)
    small_ref[2:3] = rows_sum(b1.astype(f32))
    small_ref[3:4] = rows_sum(e2.astype(f32))
    arrive(wo, 0)
    do = jnp.zeros((TOK, D), f32)
    for j in range(3):
        do = do + mul_t(b1[:, 256 * j : 256 * j + 256], units(wo, 2 * j, 2))
    do = do.astype(bf16).astype(f32)
    for d, win in enumerate(windows(do)):
        pay_ref[d] = win.astype(bf16)


def back_project(back, e1_ref, h_ref, vec, g_ref, e_ref, small_ref, w, sem):
    for part in range(3):
        got = unwindow(lambda d: back[d, :, 128 * part : 128 * part + 128].astype(f32)).astype(bf16)
        g_ref[:, D * part : D * part + D] = got
        if part != 1:
            small_ref[2 + part // 2 : 3 + part // 2] = rows_sum(got.astype(f32))
    arrived(w, sem)
    cot = jnp.zeros((TOK, D), f32)
    for j in range(9):
        cot = cot + mul_t(g_ref[:, 256 * j : 256 * j + 256], units(w, 2 * j, 2))
    xh, r = norm_parts(h_ref[...].astype(f32))
    small_ref[0:1] = rows_sum(cot * xh)
    small_ref[1:2] = rows_sum(cot)
    e_ref[...] = e1_ref[...] + norm_back(cot, vec[0:1], xh, r)


def back_project_kernel(core, back, e1_ref, h_ref, vec, *refs):
    src, refs = sources_of(0, (0,), refs)
    fetch(0, 0, core, src[0], *refs[3:], 0, 6)
    back_project(back, e1_ref, h_ref, vec, *refs)


def back_both_kernel(core, back, e1_ref, h_ref, vec, u_ref, h1_ref, vec_next, *refs):
    src, refs = sources_of(1, (0,), refs)
    src_next, refs = sources_of(0, (0, 1, 2), refs)
    outs, outs_next, (w, sem), ws = refs[:3], refs[3:9], refs[9:11], refs[11:]
    fetch(1, 0, core, src[0], w, sem, 0, 6)
    fetch_backward(0, core, src_next, *ws)
    back_project(back, e1_ref, h_ref, vec, *outs, w, sem)
    backward(outs[1], u_ref, h1_ref, vec_next, *outs_next, *ws)


def cube_store(core, stage, first_tile, triple, k, rows):
    for row in range(16):
        target = row & 1
        tile = first_tile + 3 * k
        stage[core ^ target, SLOT_OF[(target, row, triple)], tile : tile + 3] = rows[row].reshape(3, 16, 128)


def plain_store(stage, unit, rows):
    stage[:, 3 * unit : 3 * unit + 3] = rows.reshape(16, 3, 16, 128)


def wide_grad(at, b, first, store):
    for j in range(b.shape[1] // D):
        wide = mul(at, b[:, D * j : D * j + D])
        for i in range(6):
            store(first + 6 * j + i, wide[:, 128 * i : 128 * i + 128].astype(bf16).reshape(16, 48, 128))


def tall_grad(ft, b, store):
    for j in range(3):
        wide = mul(ft, b[:, 256 * j : 256 * j + 256])
        for i in range(2):
            rows = wide[:, 128 * i : 128 * i + 128].astype(bf16).reshape(16, 4, 48, 128)
            for q in range(4):
                store(4 * (2 * j + i) + q, rows[:, q])


def low(ref):
    return ref[...].astype(f32).astype(bf16)


def ship(pairs, sem):
    copies = [pltpu.make_async_copy(src, dst, sem.at[k]) for k, (src, dst) in enumerate(pairs)]
    for copy in copies:
        copy.start()
    for copy in copies:
        copy.wait()


def grad_mlp_cube(core_ref, f_ref, e_ref, a2_ref, du_ref, keep, send, stage, sem):
    core = core_ref[0]
    tall_grad(f_ref[...].T, low(e_ref), lambda u, rows: cube_store(core, stage, 9, u // 3, u % 3, rows))
    wide_grad(a2_ref[...].T, du_ref[...], 0, lambda u, rows: cube_store(core, stage, 0, u // 3, u % 3, rows))
    ship(((stage.at[0], keep), (stage.at[1], send)), sem)


def grad_joint_cube(core_ref, a_ref, g_ref, o_ref, e1_ref, keep, send, stage, sem):
    core = core_ref[0]
    put = lambda u, rows: cube_store(core, stage, 0, u // 3, u % 3, rows)
    wide_grad(a_ref[...].T, g_ref[...], 0, put)
    wide_grad(o_ref[...].T, low(e1_ref), 18, put)
    ship(((stage.at[0], keep), (stage.at[1], send)), sem)


def grad_mlp_split(core_ref, f_ref, e_ref, a2_ref, du_ref, keep, send, plain, stage, wide, sem):
    core = core_ref[0]

    def put(u, rows):
        triple, k = divmod(u, 3)
        if k == 2:
            cube_store(core, stage, 0, triple, 0, rows)
        else:
            plain_store(wide, 2 * triple + k, rows)

    wide_grad(a2_ref[...].T, du_ref[...], 0, put)
    tall_grad(f_ref[...].T, low(e_ref), lambda u, rows: plain_store(wide, 16 + u, rows))
    ship(((stage.at[0], keep), (stage.at[1], send), (wide, plain)), sem)


def out_place(l, group, u):
    cube = ((0, 0), (1, 0), (0, 1), (0, 2))
    triple, k = divmod(u, 3)
    if (l, group) in cube:
        return triple, 3 * cube.index((l, group)) + k
    if group == 2:
        return None, 29 + u
    return (triple, 12) if k == 2 else (None, 13 + 2 * triple + k)


CUBE_IN, PLAIN_IN = ((0, 0), (0, 1), (1, 0)), ((0, 2), (1, 1), (1, 2))


def dense(pieces, tiles):
    left = 16 * tiles - 6 * len(pieces)
    rows = jnp.concatenate(pieces + ([jnp.zeros((left, 128), f32)] if left else []), axis=0)
    return rows.astype(bf16).reshape(tiles, 16, 128)


def pack_kernel(win, wout, wup, wdown, order, pay):
    ins = [win[...].astype(f32), wout[...].astype(f32)]
    wide = wup[...].astype(f32)
    stack = [wide[:, l, 384 * m : 384 * m + 384] for l in range(LAYERS) for m in range(8)]
    stack = mul(jnp.concatenate(stack, axis=0).astype(bf16), order[...])
    ups = [[stack[48 * l + 6 * m : 48 * l + 6 * m + 6] for m in range(8)] for l in range(LAYERS)]
    firsts = [[v[:, l] for v in ins] for l in range(LAYERS)]
    downs = [wdown[l].astype(f32) for l in range(LAYERS)]

    def get(l, group, u):
        if group == 0:
            wide, at = (firsts[l][0], u) if u < 18 else (firsts[l][1], u - 18)
            return wide[:, 128 * at : 128 * at + 128]
        if group == 1:
            return ups[l][u // 3][:, 128 * (u % 3) : 128 * (u % 3) + 128]
        cb, q = divmod(u, 4)
        return downs[l][6 * q : 6 * q + 6, 128 * cb : 128 * cb + 128]

    plain = dense([get(*key, u) for key in PLAIN_IN for u in range(24)], 27)
    for d in range(8):
        pay[d, 0:27] = plain
        pay[d, 27:31] = dense([get(*key, 3 * d + i) for key in CUBE_IN for i in range(3)], 4)


def regroup_kernel(got, smalls, first, third, fourth):
    plain = [got[d, 0:27].astype(f32).reshape(432, 128) for d in range(8)]
    cube = [got[d, 27:31].astype(f32).reshape(64, 128) for d in range(8)]

    def join(rows, u):
        return jnp.concatenate([v[6 * u : 6 * u + 6] for v in rows], axis=0).astype(bf16).reshape(3, 16, 128)

    first[9] = smalls[...]
    for u in range(9):
        tile = 3 * u if u < 3 else 3 * u + 1
        first[tile : tile + 3] = join(cube, u)
    for u in range(24):
        third[3 * u : 3 * u + 3] = join(plain, u)
    for u in range(48):
        fourth[3 * u : 3 * u + 3] = join(plain, 24 + u)


def first_project_kernel(core, h_ref, mine, theirs, *refs):
    outs, (w, sem, buf, small_sem) = refs[:7], refs[7:]
    vecs = outs[2:]
    fetch(0, 0, core, (mine, theirs), w, sem, 0, 6)
    small_parameters(core, mine, theirs, vecs[:4], vecs[4], buf, small_sem)
    project(h_ref, vecs[0], outs[0], outs[1], w, sem)


def small_parameters(core_ref, mine, theirs, vecs, few, buf, sem):
    core = core_ref[0]

    def step(n, carry):
        for src, own in ((mine, core), (theirs, 1 - core)):
            row, triple = place(n, own)
            pltpu.make_async_copy(src.at[n, 9], buf.at[row * 8 + triple], sem).start()
        return carry

    lax.fori_loop(0, 64, step, 0)
    pltpu.make_async_copy(buf, buf, sem).wait()
    rows = buf[...].astype(f32)
    low_part, high_part = rows[:, 0], rows[:, 1]
    few[:, 0:128] = low_part
    few[:, 128:256] = high_part
    low_part = low_part.astype(bf16)
    value = lax.broadcasted_iota(jnp.int32, (128, 16), 0) - 6 * lax.broadcasted_iota(jnp.int32, (128, 16), 1)
    place_in = lax.broadcasted_iota(jnp.int32, (128, D), 1) - 6 * lax.broadcasted_iota(jnp.int32, (128, D), 0)
    total = jnp.zeros((16, D), f32)
    for i in range(6):
        picked = mul(low_part, (value == i).astype(f32).astype(bf16)).astype(bf16)
        total = total + t_mul(picked, (place_in == i).astype(f32).astype(bf16))
    for l in range(LAYERS):
        for k, i in enumerate((2 * l, 4 + 2 * l, 8 + 2 * l, 9 + 2 * l)):
            vecs[2 * l][k : k + 1] = total[i : i + 1]
        for k, i in enumerate((2 * l + 1, 5 + 2 * l, 12 + 2 * l, 13 + 2 * l)):
            vecs[2 * l + 1][k : k + 1] = total[i : i + 1]


def finish_kernel(parts, total, out, few):
    small = jnp.zeros((2, 128), f32)
    for k in range(8):
        small = small + parts[k, 9].astype(f32)[0:2]
    few[...] = small
    units_of = []
    for u in range(13):
        tile = 3 * u if u < 3 else 3 * u + 1
        rows = jnp.zeros((48, 128), f32)
        for k in range(8):
            rows = rows + parts[k, tile : tile + 3].reshape(48, 128).astype(f32)
        units_of.append(rows)
    for u in range(40):
        units_of.append(total[3 * u : 3 * u + 3].reshape(48, 128).astype(f32))
    for d in range(8):
        out[d] = dense([rows[6 * d : 6 * d + 6] for rows in units_of], 20)


def unpack_kernel(got, order, g_in, g_out, g_up, g_down):
    cube = [got[d, 0:5].reshape(80, 128).astype(f32) for d in range(8)]
    plain = got[0].reshape(320, 128).astype(f32)
    for d in range(1, 8):
        plain = plain + got[d].reshape(320, 128).astype(f32)
    stack = []
    for l in range(LAYERS):
        for group in range(3):
            rows = []
            for u in range(24):
                triple, k = out_place(l, group, u)
                rows.append((plain if triple is None else cube[triple])[6 * k : 6 * k + 6])
            if group == 0:
                g_in[:, l] = jnp.concatenate(rows[:18], axis=1)
                g_out[:, l] = jnp.concatenate(rows[18:], axis=1)
            elif group == 1:
                stack += [jnp.concatenate(rows[3 * m : 3 * m + 3], axis=1) for m in range(8)]
            else:
                for u in range(24):
                    cb, q = divmod(u, 4)
                    g_down[l, 6 * q : 6 * q + 6, 128 * cb : 128 * cb + 128] = rows[u]
    left = jnp.concatenate(stack, axis=0)
    terms = []
    for _ in range(3):
        terms.append(left.astype(bf16))
        left = left - terms[-1].astype(f32)
    wide = mul_t(jnp.concatenate(terms, axis=0), order[...])
    wide = wide[0:96] + wide[96:192] + wide[192:288]
    for l in range(LAYERS):
        for m in range(8):
            g_up[:, l, 384 * m : 384 * m + 384] = wide[48 * l + 6 * m : 48 * l + 6 * m + 6]


def call(kernel, outs, ins, scratch=(), us=3, out_spaces=None, aliases=None):
    spaces = {"s": pltpu.SMEM, "v": pltpu.VMEM, "a": pl.ANY}
    return pl.pallas_call(
        kernel,
        out_shape=[jax.ShapeDtypeStruct(*o) for o in outs],
        in_specs=[pl.BlockSpec(memory_space=spaces[m]) for _, m in ins],
        out_specs=[pl.BlockSpec(memory_space=spaces[m]) for m in (out_spaces or "v" * len(outs))],
        scratch_shapes=list(scratch),
        input_output_aliases=aliases or {},
        compiler_params=pltpu.CompilerParams(vmem_limit_bytes=56 * 1024 * 1024),
        cost_estimate=pl.CostEstimate(flops=0, bytes_accessed=us * 3690000, transcendentals=0),
    )(*[a for a, _ in ins])


def w_scratch(count):
    return pltpu.VMEM((16, 3 * count, 16, 128), bf16)


DMA = pltpu.SemaphoreType.DMA


def after(values, *others):
    return lax.optimization_barrier((values,) + others)[0] if others else values


def copies(values, groups, *others):
    many = after(jnp.broadcast_to(values[None], (8,) + values.shape), *others)
    return lax.all_to_all(many, ALL, 0, 0, axis_index_groups=groups)


def sum_first(values):
    return jnp.sum(values.astype(f32), axis=0)


def swap_core(values):
    return lax.ppermute(values, "c", [(0, 1), (1, 0)])


def cube_copies(shards, *others):
    return copies(shards, GROUPS_B, *others).reshape((64,) + shards.shape[1:])


def spread(shards):
    mine = cube_copies(shards)
    return mine, swap_core(mine)


def add_kernel(*refs):
    out, first = refs[-1], 0
    for keep, got in zip(refs[0:-1:2], refs[1:-1:2]):
        n = keep.shape[1]
        out[:, first : first + n] = (keep[...].astype(f32) + got[...].astype(f32)).astype(bf16)
        first += n


def add_pairs(pairs):
    total = sum(a.shape[1] for a, _ in pairs)
    flat = [v for pair in pairs for v in pair]

    def spec(t):
        return pl.BlockSpec((8, t, 16, 128), lambda i: (i, 0, 0, 0))

    return pl.pallas_call(
        add_kernel,
        grid=(8,),
        out_shape=jax.ShapeDtypeStruct((64, total, 16, 128), bf16),
        in_specs=[spec(v.shape[1]) for v in flat],
        out_specs=spec(total),
        compiler_params=pltpu.CompilerParams(vmem_limit_bytes=56 * 1024 * 1024),
        cost_estimate=pl.CostEstimate(flops=2**22, bytes_accessed=3 * 64 * total * 4096, transcendentals=0),
    )(*flat)


def core_sums(pairs):
    return add_pairs([(keep, swap_core(send)) for keep, send in pairs])


def to_cube(part):
    return lax.all_to_all(part.reshape((8, 8) + part.shape[1:]), ALL, 0, 0, axis_index_groups=GROUPS_B)


def token_ids(group_index, positions, sequence_group, sequence_start, sequence_length):
    member = (
        (sequence_group[None, :] == group_index)
        & (sequence_start[None, :] <= positions[:, None])
        & (positions[:, None] < (sequence_start + sequence_length)[None, :])
    )
    numbers = jnp.arange(sequence_group.shape[0], dtype=jnp.int32) + 1
    located = jnp.sum(jnp.where(member, numbers[None, :], 0), axis=1)
    return jnp.where(located > 0, located - 1, -1 - positions)


def body(hidden_in, out_grad, sequence_group, sequence_start, sequence_length, norm_gain, norm_bias,
         input_weight, input_bias, output_weight, branch_bias, up_weight, up_bias, down_weight):
    core = lax.axis_index("c").astype(jnp.int32).reshape(1)
    par = lax.axis_index("zl").astype(jnp.int32).reshape(1)
    positions = jnp.arange(SLOTS, dtype=jnp.int32)
    ids = token_ids(lax.axis_index(DATA), positions, sequence_group, sequence_start, sequence_length)
    idc, idr = ids.reshape(CTX_DEV, TOK, 1), ids.reshape(1, SLOTS)

    order = jnp.asarray(FF_ORDER, bf16)
    smalls = jnp.concatenate([v.reshape(-1) for v in (norm_gain, norm_bias, input_bias, branch_bias, up_bias)])
    smalls = jnp.pad(smalls, (0, 2048 - 144)).reshape(16, 128)
    (pay,) = call(pack_kernel, [((8, 31, 16, 128), bf16)],
                  [(jnp.swapaxes(v, 0, 1), "v") for v in (input_weight, output_weight, up_weight)]
                  + [(down_weight, "v"), (order, "v")])
    got = lax.all_to_all(pay, CTX, 0, 0)
    first, third, fourth = call(
        regroup_kernel,
        [((28, 16, 128), bf16), ((72, 16, 128), bf16), ((144, 16, 128), bf16)],
        [(got, "v"), (smalls, "v")])
    down_0 = lax.all_gather(third, DATA, axis=0, tiled=False)
    shards = copies(first, GROUPS_A)
    group_e, shards = spread(shards[:, :10]), shards[:, 10:]
    shards = jnp.broadcast_to(shards[None], (8,) + shards.shape)
    group_e = tuple(after(v, shards) for v in group_e)
    sources = {(0, 0): group_e, (0, 2): (down_0,)}

    a1, pay, *vecs, few = call(
        first_project_kernel,
        [((TOK, D), bf16), ((8, TOK, 384), bf16)] + [((4, D), f32)] * 4 + [((128, 256), f32)],
        [(core, "s"), (hidden_in[0], "v"), (group_e[0], "a"), (group_e[1], "a")],
        [w_scratch(18), DMA, pltpu.VMEM((128, 16, 128), bf16), DMA], us=7)
    ups = few[:, 96:144].reshape(16, 8, 2, 4, 6).transpose(2, 0, 3, 1, 4).reshape(2, 4 * D)

    def weights(l, all_groups):
        return [(w, "a") for group in range(3 if all_groups else 1) for w in sources[l, group]]

    def attend(heads):
        return call(attend_kernel, [((8, TOK, 128), bf16)],
                    [(par, "s"), (heads, "v"), (idc, "v"), (idr, "v")], us=6)[0]

    def attend_back(heads, cot):
        return call(attend_back_kernel, [((8, TOK, 384), bf16)],
                    [(par, "s"), (heads, "v"), (cot, "v"), (idc, "v"), (idr, "v")],
                    [pltpu.VMEM((2, SLOTS, 64), f32)] * 2, us=8)[0]

    def exchange(values):
        return lax.all_to_all(values, CTX, 0, 0)

    block_scratch = [w_scratch(6), w_scratch(24), w_scratch(24), DMA((3,))]
    project_scratch = [w_scratch(18), DMA]
    project_outs = [((TOK, D), bf16), ((8, TOK, 384), bf16)]
    forward_outs = [((TOK, D), bf16), ((TOK, D), f32), ((TOK, D), bf16), ((TOK, 4 * D), f32)]
    backward_outs = [((TOK, 4 * D), bf16), ((TOK, D), f32), ((8, TOK, 128), bf16), ((4, D), f32), ((1, 4 * D), f32)]
    back_project_outs = [((TOK, 3 * D), bf16), ((TOK, D), f32), ((4, D), f32)]

    hidden_0 = hidden_in[0]
    both_1 = lax.all_gather(after(fourth, a1), DATA, axis=0, tiled=False)
    sources[1, 1] = sources[1, 2] = (both_1,)
    a1 = [a1, None]
    heads_0 = exchange(pay)
    mine = lax.all_to_all(after(shards, heads_0, down_0), ALL, 0, 0, axis_index_groups=GROUPS_B)
    mine = mine.reshape((64,) + mine.shape[2:])
    mix = attend(heads_0)
    theirs = swap_core(after(mine, mix))
    sources[0, 1] = sources[1, 0] = (mine, theirs)
    back = exchange(after(mix, mine))
    o_0, h1_0, a2_0, u_0, hidden_1, a1[1], pay = call(
        forward_project_kernel,
        forward_outs + [((TOK, D), f32)] + project_outs,
        [(core, "s"), (hidden_0, "v"), (back, "v"), (vecs[1], "v"), (ups[0:1], "v"), (vecs[2], "v")]
        + weights(0, True) + weights(1, False),
        block_scratch + project_scratch, us=12)
    heads_1 = exchange(pay)
    back = exchange(attend(heads_1))
    def grad_joint(a1, g, o, e1):
        return call(
            grad_joint_cube, [((64, 9, 16, 128), bf16)] * 2,
            [(core, "s"), (a1, "v"), (g, "v"), (o, "v"), (e1, "v")],
            [pltpu.VMEM((2, 64, 9, 16, 128), bf16), DMA((2,))], us=5, out_spaces="aa")

    grad = out_grad[0]
    few_rows, few_up, joint = [None] * 2, [None] * 2, [None] * 2
    o_1, a2_1, hidden, f, du, e1, pay, small_b, few_up[1] = call(
        last_kernel,
        [((TOK, D), bf16), ((TOK, D), bf16), ((TOK, D), bf16), ((TOK, 4 * D), bf16)] + backward_outs,
        [(core, "s"), (hidden_1, "v"), (back, "v"), (vecs[3], "v"), (ups[1:2], "v"), (grad, "v")] + weights(1, True),
        [pltpu.VMEM((TOK, D), f32), pltpu.VMEM((TOK, 4 * D), f32)] + block_scratch, us=16)
    cot = exchange(pay)
    keep_u, send_u, mlp_1 = call(
        grad_mlp_split, [((64, 3, 16, 128), bf16)] * 2 + [((16, 120, 16, 128), bf16)],
        [(core, "s"), (f, "v"), (grad, "v"), (a2_1, "v"), (du, "v")],
        [pltpu.VMEM((2, 64, 3, 16, 128), bf16), w_scratch(40), DMA((3,))], us=9, out_spaces="aaa")
    scattered = lax.psum_scatter(after(mlp_1, cot), DATA, scatter_dimension=0, tiled=False)
    back = exchange(attend_back(heads_1, after(cot, mlp_1)))
    e1_1, small_b1 = e1, small_b
    g_1, grad, small_a1, f_0, du, e1, pay, small_b, few_up[0] = call(
        back_both_kernel, back_project_outs + [((TOK, 4 * D), bf16)] + backward_outs,
        [(core, "s"), (back, "v"), (e1_1, "v"), (hidden_1, "v"), (vecs[2], "v"), (u_0, "v"), (h1_0, "v"),
         (vecs[1], "v")] + weights(1, False) + weights(0, True),
        project_scratch + block_scratch, us=16)
    cot = exchange(pay)
    keep_ud, send_ud = call(
        grad_mlp_cube, [((64, 18, 16, 128), bf16)] * 2,
        [(core, "s"), (f_0, "v"), (grad, "v"), (a2_0, "v"), (du, "v")],
        [pltpu.VMEM((2, 64, 18, 16, 128), bf16), DMA((2,))], us=9, out_spaces="aa")
    send_ud = after(send_ud, cot)
    back = exchange(attend_back(heads_0, after(cot, keep_ud)))
    middle = core_sums([(keep_ud, send_ud), (keep_u, send_u)])
    g_0, grad, small_a0 = call(
        back_project_kernel, back_project_outs,
        [(core, "s"), (after(back, middle), "v"), (e1, "v"), (hidden_0, "v"), (vecs[0], "v")] + weights(0, False),
        project_scratch, us=6)
    joint = [grad_joint(a1[0], g_0, o_0, e1), grad_joint(a1[1], g_1, o_1, e1_1)]
    for l, (first, second) in enumerate(((small_a0, small_b), (small_a1, small_b1))):
        few_rows[l] = jnp.concatenate([first[0:1], second[0:1], first[1:2], second[1:2], first[2:4], second[2:4]], axis=0)

    few = jnp.concatenate([r.reshape(8, 128, 6).transpose(1, 0, 2).reshape(128, 48) for r in few_rows]
                          + [r.reshape(16, 4, 8, 6).transpose(0, 2, 1, 3).reshape(128, 24) for r in few_up], axis=1)
    few = jnp.pad(few, ((0, 0), (0, 256 - 144))).astype(bf16)
    few = jnp.dot(jnp.asarray(TAIL_ORDER.T, bf16), few, preferred_element_type=f32).astype(bf16)
    few = jnp.pad(few.reshape(2, 64, 1, 2, 128), ((0, 0),) * 3 + ((0, 14), (0, 0)))
    few = [jnp.where(core[0] == k, few[0], few[1]) for k in range(2)]

    middle = to_cube(middle)
    last = to_cube(after(core_sums([joint[0], few, joint[1]]), middle, scattered))
    sums = jnp.concatenate([sum_first(last).astype(bf16), sum_first(middle).astype(bf16)], axis=1)
    sums = lax.all_to_all(sums, ALL, 0, 0, axis_index_groups=GROUPS_A)
    sums, few = call(finish_kernel, [((8, 20, 16, 128), bf16), ((2, 128), f32)],
                     [(sums, "v"), (scattered, "v")])
    got = lax.all_to_all(sums, CTX, 0, 0)
    grad_in, grad_out, grad_up, grad_down = call(
        unpack_kernel,
        [((6, 2, 3 * D), f32), ((6, 2, D), f32), ((6, 2, 4 * D), f32), ((2, 24, D), f32)],
        [(got, "v"), (order, "v")])
    few = few.reshape(256)
    few_l = [few[48 * l : 48 * l + 48].reshape(4, 2, 6) for l in range(2)]

    def pair(k):
        return jnp.stack([few_l[0][k], few_l[1][k]])

    return (
        hidden[None],
        grad[None],
        pair(0),
        pair(1),
        jnp.swapaxes(grad_in, 0, 1),
        pair(2),
        jnp.swapaxes(grad_out, 0, 1),
        pair(3),
        jnp.swapaxes(grad_up, 0, 1),
        few[96:144].reshape(2, 24),
        grad_down,
    )


def solution(mesh):
    mesh = Mesh(mesh.devices.reshape(4, 2, 2, 4, 2), ALL)
    token = P(DATA, CTX, None)
    one = P(None, ALL)
    two = P(None, None, ALL)
    mat = P(None, ALL, None)
    return jax.shard_map(
        body,
        mesh=mesh,
        in_specs=(token, token, P(), P(), P(), two, two, mat, two, mat, two, mat, one, mat),
        out_specs=(token, token, two, two, mat, two, mat, two, mat, one, mat),
        check_vma=False,
    )
```

```python
import functools

import jax
import jax.numpy as jnp
import numpy as np
from jax import lax
from jax.experimental import pallas as pl
from jax.experimental.pallas import tpu as pltpu
from jax.sharding import Mesh, PartitionSpec as P

LAYERS = 2
D = 768
TOK = 128
CTX_DEV = 8
SLOTS = TOK * CTX_DEV
DATA = ("y", "zh", "c")
CTX = ("x", "zl")
ALL = DATA + CTX
bf16 = jnp.bfloat16
f32 = jnp.float32
norm_eps = 1e-05
score_scale = 0.125
hidden_value = -1000000000.0


def coord(bit_b, bit_a, core):
    return core * (2 * bit_b + bit_a) + (1 - core) * (3 * bit_a + bit_b * (1 - 2 * bit_a))


def place(n, core):
    y = coord((n >> 5) & 1, (n >> 2) & 1, core)
    z = coord((n >> 4) & 1, (n >> 1) & 1, core)
    x = coord((n >> 3) & 1, n & 1, core)
    return (y * 2 + (z >> 1)) * 2 + core, x * 2 + (z & 1)


SLOT_OF = {(c,) + place(n, c): n for c in range(2) for n in range(64)}


def tail_order():
    table = np.zeros((128, 128), np.float32)
    for (c, row, triple), n in SLOT_OF.items():
        table[row * 8 + triple, 64 * c + n] = 1.0
    return table


TAIL_ORDER = tail_order()


def device_id(y, z, core, x):
    return y * 32 + (z >> 1) * 16 + core * 8 + x * 2 + (z & 1)


def cube_groups(level):
    found = {}
    for core in range(2):
        for n in range(64):
            bits = [(n >> s) & 1 for s in range(6)]
            y, z, x = (coord(bits[3 + s], bits[s], core) for s in (2, 1, 0))
            if level == 1:
                key = (core,) + tuple(coord(bits[3 + s], 0, core) for s in (2, 1, 0))
                slot = n & 7
            else:
                pair = [coord(bits[3 + s], bits[s], core) for s in (2, 1, 0)]
                pair = [(v // 2 if core == 0 else ((v + 1) // 2) % 2) for v in pair]
                key = (core,) + tuple(pair)
                slot = n >> 3
            found.setdefault(key, [None] * 8)[slot] = device_id(y, z, core, x)
    return [found[k] for k in sorted(found)]


GROUPS_A = cube_groups(1)
GROUPS_B = cube_groups(0)


def ff_order():
    used = np.arange(384)
    block, q, ctx, r = used // 192, used // 48 % 4, used // 6 % 8, used % 6
    table = np.zeros((384, 384), np.float32)
    table[block * 192 + ctx * 24 + q * 6 + r, used] = 1.0
    return table


FF_ORDER = ff_order()


def slot_at(y, z, x, core):
    n = 0
    for v, m in ((y, 4), (z, 2), (x, 1)):
        bit_a = core * (v & 1) + (1 - core) * (v >> 1)
        bit_b = core * (v >> 1) + (1 - core) * ((v ^ (v >> 1)) & 1)
        n = n + m * (8 * bit_b + bit_a)
    return n


def fetch_cube(core_ref, mine, theirs, offset, w, sem, low, high):
    core = core_ref[0]

    def step(k, carry):
        y, z, x = (k >> 2) & 3, k & 3, (low >> 1) + (k >> 4)
        for src, own in ((mine, core), (theirs, 1 - core)):
            row = (y * 2 + (z >> 1)) * 2 + own
            first = ((k >> 4) * 2 + (z & 1)) * 9
            pltpu.make_async_copy(
                src.at[slot_at(y, z, x, own), pl.ds(offset, 9)], w.at[row, pl.ds(first, 9)], sem).start()
        return carry

    lax.fori_loop(0, 8 * (high - low), step, 0, unroll=4)


COMES = {(0, 0): ("cube", 0), (0, 1): ("cube", 0), (0, 2): ("plain", 0),
         (1, 0): ("cube", 9), (1, 1): ("plain", 0), (1, 2): ("plain", 72)}


def fetch(layer, group, core_ref, sources, w, sem, low, high):
    kind, first = COMES[layer, group]
    if kind == "cube":
        fetch_cube(core_ref, sources[0], sources[1], first, w, sem, low, high)
    else:
        tiles = pl.ds(first + 9 * low, 9 * (high - low))
        pltpu.make_async_copy(sources[0].at[:, tiles], w, sem).start()


def sources_of(layer, groups, refs):
    out, at = {}, 0
    for group in groups:
        n = 2 if COMES[layer, group][0] == "cube" else 1
        out[group] = refs[at : at + n]
        at += n
    return out, refs[at:]


def arrived(w, sem):
    pltpu.make_async_copy(w, w, sem).wait()


def units(w, first, count):
    parts = [w[:, 3 * (first + i) : 3 * (first + i) + 3].reshape(D, 128) for i in range(count)]
    return parts[0] if count == 1 else jnp.concatenate(parts, axis=1)


def tall_units(w, cb):
    return w[:, 12 * cb : 12 * cb + 12].reshape(4 * D, 128)


def mul(a, b):
    return jnp.dot(a, b, preferred_element_type=f32)


def mul_t(a, b):
    return lax.dot_general(a, b, (((1,), (1,)), ((), ())), preferred_element_type=f32)


def t_mul(a, b):
    return lax.dot_general(a, b, (((0,), (0,)), ((), ())), preferred_element_type=f32)


def norm_parts(values):
    centre = values - jnp.mean(values, axis=-1, keepdims=True)
    var = jnp.mean(centre * centre, axis=-1, keepdims=True)
    r = lax.rsqrt(var + norm_eps)
    return centre * r, r


def norm_back(cot, gain, xh, r):
    cg = cot * gain
    return r * (cg - jnp.mean(cg, axis=-1, keepdims=True) - xh * jnp.mean(cg * xh, axis=-1, keepdims=True))


def rows_sum(values):
    return jnp.sum(values, axis=0, keepdims=True)


def windows(values):
    out = []
    for x in range(4):
        for zl in range(2):
            own, shared = 3 * x + 2 * zl, 3 * x + 1
            out.append(jnp.concatenate([values[:, 64 * own : 64 * own + 64],
                                        values[:, 64 * shared : 64 * shared + 64]], axis=1))
    return out


def unwindow(get):
    parts = []
    for x in range(4):
        lo, hi = get(2 * x), get(2 * x + 1)
        parts += [lo[:, :64], lo[:, 64:] + hi[:, 64:], hi[:, :64]]
    return jnp.concatenate(parts, axis=1)


def gelu_both(u):
    k = 0.7978845608028654
    t = jnp.tanh(k * (u + 0.044715 * u * u * u))
    half = 0.5 * (1.0 + t)
    return u * half, half + 0.5 * u * (1.0 - t * t) * (k * (1.0 + 3 * 0.044715 * u * u))


def project_kernel(layer, core, h_ref, vec, *refs):
    src, (a1_ref, pay_ref, w, sem) = sources_of(layer, (0,), refs)
    fetch(layer, 0, core, src[0], w, sem, 0, 6)
    project(h_ref, vec, a1_ref, pay_ref, w, sem)


def project(h_ref, vec, a1_ref, pay_ref, w, sem):
    xh, _ = norm_parts(h_ref[...].astype(f32))
    a1 = (xh * vec[0:1] + vec[1:2]).astype(bf16)
    a1_ref[...] = a1
    arrived(w, sem)
    for part in range(3):
        cols = [mul(a1, units(w, 6 * part + 2 * j, 2)) for j in range(3)]
        got = jnp.concatenate(cols, axis=1)
        if part != 1:
            got = got + vec[2 + part // 2 : 3 + part // 2]
        got = got.astype(bf16).astype(f32)
        for d, win in enumerate(windows(got)):
            pay_ref[d, :, 128 * part : 128 * part + 128] = win.astype(bf16)


def masked(scores, first_block, second_block, idc_ref, idr_ref):
    n = scores.shape[1]
    ids = jnp.concatenate([idc_ref[first_block], idc_ref[second_block]], axis=0)
    row = lax.broadcasted_iota(jnp.int32, (2 * TOK, n), 0)
    qpos = row + jnp.where(row < TOK, first_block * TOK, (second_block - 1) * TOK)
    seen = (ids == idr_ref[:, 0:n]) & (lax.broadcasted_iota(jnp.int32, (2 * TOK, n), 1) <= qpos)
    return jnp.where(seen, scores, hidden_value)


def head_pairs(par):
    return ([(0, 2 * i, 2 * i + 1, 2 * i + 2) for i in range(4)]
            + [(1, 4 * i + par, 4 * i + 2 + par, 4 * i + 4) for i in range(2)])


def half(values, head):
    return values[:, 64 * head : 64 * head + 64]


def two_blocks(ref, first, second, lanes, head):
    return jnp.concatenate([half(ref[first, :, lanes], head), half(ref[second, :, lanes], head)], axis=0)


def store_blocks(out, par, results):
    for b in range(8):
        own = results[b // 2][TOK * (b % 2) : TOK * (b % 2) + TOK]
        shared = results[4 + b // 4][TOK * (b // 2 % 2) : TOK * (b // 2 % 2) + TOK]
        shared = jnp.where(par == b % 2, shared, 0.0)
        out[b, :, 0:128] = jnp.concatenate([own, shared], axis=1).astype(bf16)


def weights_of(q, key, *where):
    s = masked(mul_t(q, key), *where)
    e = jnp.exp(s - jnp.max(s, axis=1, keepdims=True))
    return e * (1.0 / jnp.sum(e, axis=1, keepdims=True))


def attend_kernel(par_ref, heads, idc, idr, out):
    par = par_ref[0]
    key = heads[:, :, 128:256].reshape(SLOTS, 128)
    val = heads[:, :, 256:384].reshape(SLOTS, 128)
    keys, vals = [half(key, h) for h in range(2)], [half(val, h) for h in range(2)]
    results = []
    for head, first, second, count in head_pairs(par):
        n = count * TOK
        q = two_blocks(heads, first, second, slice(0, 128), head) * score_scale
        p = weights_of(q, keys[head][:n], first, second, idc, idr).astype(bf16)
        results.append(mul(p, vals[head][:n]))
    store_blocks(out, par, results)


def attend_back_kernel(par_ref, heads, cot, idc, idr, out, dk_acc, dv_acc):
    par = par_ref[0]
    key = heads[:, :, 128:256].reshape(SLOTS, 128)
    val = heads[:, :, 256:384].reshape(SLOTS, 128)
    keys, vals = [half(key, h) for h in range(2)], [half(val, h) for h in range(2)]
    dk_acc[...] = jnp.zeros_like(dk_acc)
    dv_acc[...] = jnp.zeros_like(dv_acc)
    results = []
    for head, first, second, count in head_pairs(par):
        n = count * TOK
        q = two_blocks(heads, first, second, slice(0, 128), head) * score_scale
        g = two_blocks(cot, first, second, slice(0, 128), head)
        p = weights_of(q, keys[head][:n], first, second, idc, idr)
        dp = mul_t(g, vals[head][:n])
        ds = (p * (dp - jnp.sum(p * dp, axis=1, keepdims=True))).astype(bf16)
        results.append(mul(ds, keys[head][:n]) * score_scale)
        dk_acc[head, 0:n] += t_mul(ds, q)
        dv_acc[head, 0:n] += t_mul(p.astype(bf16), g)
    store_blocks(out, par, results)
    dk = jnp.concatenate([dk_acc[0], dk_acc[1]], axis=1)
    dv = jnp.concatenate([dv_acc[0], dv_acc[1]], axis=1)
    out[:, :, 128:256] = dk.astype(bf16).reshape(8, TOK, 128)
    out[:, :, 256:384] = dv.astype(bf16).reshape(8, TOK, 128)


def fetch_forward(layer, core, src, wo, wu, wd, sems):
    fetch(layer, 0, core, src[0], wo, sems.at[0], 6, 8)
    fetch(layer, 1, core, src[1], wu, sems.at[1], 0, 8)
    fetch(layer, 2, core, src[2], wd, sems.at[2], 0, 8)


def forward(h_ref, back, vec, upb, o_ref, h1_ref, a2_ref, u_ref, f_ref, next_ref, wo, wu, wd, sems):
    o = unwindow(lambda d: back[d].astype(f32)).astype(bf16)
    o_ref[...] = o
    arrived(wo, sems.at[0])
    got = jnp.concatenate([mul(o, units(wo, 2 * j, 2)) for j in range(3)], axis=1)
    h1 = h_ref[...].astype(f32) + got + vec[2:3]
    h1_ref[...] = h1
    xh, _ = norm_parts(h1)
    a2 = (xh * vec[0:1] + vec[1:2]).astype(bf16)
    a2_ref[...] = a2
    arrived(wu, sems.at[1])
    acts = []
    for j in range(12):
        c = slice(256 * j, 256 * j + 256)
        u = mul(a2, units(wu, 2 * j, 2)) + upb[:, c]
        act, slope = gelu_both(u)
        acts.append(act.astype(bf16))
        if f_ref is None:
            u_ref[:, c] = u
        else:
            u_ref[:, c] = slope
            f_ref[:, c] = acts[-1]
    f = jnp.concatenate(acts, axis=1)
    arrived(wd, sems.at[2])
    for j in range(3):
        w = jnp.concatenate([tall_units(wd, 2 * j), tall_units(wd, 2 * j + 1)], axis=1)
        c = slice(256 * j, 256 * j + 256)
        next_ref[:, c] = (h1[:, c] + mul(f, w) + vec[3:4, c]).astype(next_ref.dtype)


def last_kernel(core, h_ref, back, vec, upb, e_ref, *refs):
    src, refs = sources_of(1, (0, 1, 2), refs)
    o_ref, a2_ref, next_ref, f_ref, outs, h1, slope, ws = refs[0], refs[1], refs[2], refs[3], refs[4:9], refs[9], refs[10], refs[11:]
    fetch_forward(1, core, src, *ws)
    forward(h_ref, back, vec, upb, o_ref, h1, a2_ref, slope, f_ref, next_ref, *ws)
    backward(e_ref, slope, h1, vec, None, *outs, *ws[:3], None)


def forward_project_kernel(core, h_ref, back, vec, upb, vec_next, *refs):
    src, refs = sources_of(0, (0, 1, 2), refs)
    src_next, refs = sources_of(1, (0,), refs)
    outs, (a1_ref, pay_ref), ws, (w, sem) = refs[:5], refs[5:7], refs[7:11], refs[11:]
    fetch_forward(0, core, src, *ws)
    fetch(1, 0, core, src_next[0], w, sem, 0, 6)
    forward(h_ref, back, vec, upb, *outs[:4], None, outs[4], *ws)
    project(outs[4], vec_next, a1_ref, pay_ref, w, sem)


def fetch_backward(layer, core, src, wo, wu, wd, sems):
    fetch(layer, 2, core, src[2], wd, sems.at[2], 0, 8)
    fetch(layer, 1, core, src[1], wu, sems.at[1], 0, 8)
    fetch(layer, 0, core, src[0], wo, sems.at[0], 6, 8)


def backward(e_ref, u_ref, h1_ref, vec, f_ref, du_ref, e1_ref, pay_ref, small_ref, upb_ref, wo, wu, wd, sems):
    def arrive(w, k):
        if sems is not None:
            arrived(w, sems.at[k])

    e = e_ref[...].astype(f32)
    e2 = e.astype(bf16)
    arrive(wd, 2)
    df = None
    for j in range(3):
        w = jnp.concatenate([tall_units(wd, 2 * j), tall_units(wd, 2 * j + 1)], axis=1)
        part = mul_t(e2[:, 256 * j : 256 * j + 256], w)
        df = part if df is None else df + part
    arrive(wu, 1)
    cot = jnp.zeros((TOK, D), f32)
    for j in range(12):
        c = slice(256 * j, 256 * j + 256)
        slope = u_ref[:, c]
        if f_ref is not None:
            f, slope = gelu_both(slope)
            f_ref[:, c] = f.astype(bf16)
        du = (df[:, c] * slope).astype(bf16)
        du_ref[:, c] = du
        upb_ref[:, c] = rows_sum(du.astype(f32))
        if j % 3 == 2:
            cot = cot + mul_t(du_ref[:, D * (j // 3) : D * (j // 3) + D], units(wu, 2 * j - 4, 6))
    xh, r = norm_parts(h1_ref[...])
    e1 = e + norm_back(cot, vec[0:1], xh, r)
    e1_ref[...] = e1
    b1 = e1.astype(bf16)
    small_ref[0:1] = rows_sum(cot * xh)
    small_ref[1:2] = rows_sum(cot)
    small_ref[2:3] = rows_sum(b1.astype(f32))
    small_ref[3:4] = rows_sum(e2.astype(f32))
    arrive(wo, 0)
    do = mul_t(b1, units(wo, 0, 6)).astype(bf16).astype(f32)
    for d, win in enumerate(windows(do)):
        pay_ref[d] = win.astype(bf16)


def back_project(back, e1_ref, h_ref, vec, g_ref, e_ref, small_ref, w, sem):
    for part in range(3):
        got = unwindow(lambda d: back[d, :, 128 * part : 128 * part + 128].astype(f32)).astype(bf16)
        g_ref[:, D * part : D * part + D] = got
        if part != 1:
            small_ref[2 + part // 2 : 3 + part // 2] = rows_sum(got.astype(f32))
    arrived(w, sem)
    cot = jnp.zeros((TOK, D), f32)
    for j in range(3):
        cot = cot + mul_t(g_ref[:, D * j : D * j + D], units(w, 6 * j, 6))
    xh, r = norm_parts(h_ref[...].astype(f32))
    small_ref[0:1] = rows_sum(cot * xh)
    small_ref[1:2] = rows_sum(cot)
    e_ref[...] = e1_ref[...] + norm_back(cot, vec[0:1], xh, r)


def back_project_kernel(core, back, e1_ref, h_ref, vec, *refs):
    src, refs = sources_of(0, (0,), refs)
    fetch(0, 0, core, src[0], *refs[3:], 0, 6)
    back_project(back, e1_ref, h_ref, vec, *refs)


def back_both_kernel(core, back, e1_ref, h_ref, vec, u_ref, h1_ref, vec_next, *refs):
    src, refs = sources_of(1, (0,), refs)
    src_next, refs = sources_of(0, (0, 1, 2), refs)
    outs, outs_next, (w, sem), ws = refs[:3], refs[3:9], refs[9:11], refs[11:]
    fetch(1, 0, core, src[0], w, sem, 0, 6)
    fetch_backward(0, core, src_next, *ws)
    back_project(back, e1_ref, h_ref, vec, *outs, w, sem)
    backward(outs[1], u_ref, h1_ref, vec_next, *outs_next, *ws)


def cube_store(core, stage, first_tile, triple, k, rows):
    for row in range(16):
        target = row & 1
        tile = first_tile + 3 * k
        stage[core ^ target, SLOT_OF[(target, row, triple)], tile : tile + 3] = rows[row].reshape(3, 16, 128)


def plain_store(stage, unit, rows):
    stage[:, 3 * unit : 3 * unit + 3] = rows.reshape(16, 3, 16, 128)


def wide_grad(at, b, first, store):
    for j in range(b.shape[1] // D):
        wide = mul(at, b[:, D * j : D * j + D])
        for i in range(6):
            store(first + 6 * j + i, wide[:, 128 * i : 128 * i + 128].astype(bf16).reshape(16, 48, 128))


def tall_grad(ft, b, store):
    for j in range(3):
        wide = mul(ft, b[:, 256 * j : 256 * j + 256])
        for i in range(2):
            rows = wide[:, 128 * i : 128 * i + 128].astype(bf16).reshape(16, 4, 48, 128)
            for q in range(4):
                store(4 * (2 * j + i) + q, rows[:, q])


def low(ref):
    return ref[...].astype(f32).astype(bf16)


def ship(pairs, sem):
    copies = [pltpu.make_async_copy(src, dst, sem.at[k]) for k, (src, dst) in enumerate(pairs)]
    for copy in copies:
        copy.start()
    for copy in copies:
        copy.wait()


def grad_mlp_cube(core_ref, f_ref, e_ref, a2_ref, du_ref, keep, send, stage, sem):
    core = core_ref[0]
    tall_grad(f_ref[...].T, low(e_ref), lambda u, rows: cube_store(core, stage, 9, u // 3, u % 3, rows))
    wide_grad(a2_ref[...].T, du_ref[...], 0, lambda u, rows: cube_store(core, stage, 0, u // 3, u % 3, rows))
    ship(((stage.at[0], keep), (stage.at[1], send)), sem)


def grad_joint_cube(core_ref, a_ref, g_ref, o_ref, e1_ref, keep, send, stage, sem):
    core = core_ref[0]
    put = lambda u, rows: cube_store(core, stage, 0, u // 3, u % 3, rows)
    wide_grad(a_ref[...].T, g_ref[...], 0, put)
    wide_grad(o_ref[...].T, low(e1_ref), 18, put)
    ship(((stage.at[0], keep), (stage.at[1], send)), sem)


def grad_mlp_split(core_ref, f_ref, e_ref, a2_ref, du_ref, keep, send, plain, stage, wide, sem):
    core = core_ref[0]

    def put(u, rows):
        triple, k = divmod(u, 3)
        if k == 2:
            cube_store(core, stage, 0, triple, 0, rows)
        else:
            plain_store(wide, 2 * triple + k, rows)

    wide_grad(a2_ref[...].T, du_ref[...], 0, put)
    tall_grad(f_ref[...].T, low(e_ref), lambda u, rows: plain_store(wide, 16 + u, rows))
    ship(((stage.at[0], keep), (stage.at[1], send), (wide, plain)), sem)


def out_place(l, group, u):
    cube = ((0, 0), (1, 0), (0, 1), (0, 2))
    triple, k = divmod(u, 3)
    if (l, group) in cube:
        return triple, 3 * cube.index((l, group)) + k
    if group == 2:
        return None, 29 + u
    return (triple, 12) if k == 2 else (None, 13 + 2 * triple + k)


CUBE_IN, PLAIN_IN = ((0, 0), (0, 1), (1, 0)), ((0, 2), (1, 1), (1, 2))


def dense(pieces, tiles):
    left = 16 * tiles - 6 * len(pieces)
    rows = jnp.concatenate(pieces + ([jnp.zeros((left, 128), f32)] if left else []), axis=0)
    return rows.astype(bf16).reshape(tiles, 16, 128)


def pack_kernel(win, wout, wup, wdown, order, pay):
    ins = [win[...].astype(f32), wout[...].astype(f32)]
    wide = wup[...].astype(f32)
    stack = [wide[:, l, 384 * m : 384 * m + 384] for l in range(LAYERS) for m in range(8)]
    stack = mul(jnp.concatenate(stack, axis=0).astype(bf16), order[...])
    ups = [[stack[48 * l + 6 * m : 48 * l + 6 * m + 6] for m in range(8)] for l in range(LAYERS)]
    firsts = [[v[:, l] for v in ins] for l in range(LAYERS)]
    downs = [wdown[l].astype(f32) for l in range(LAYERS)]

    def get(l, group, u):
        if group == 0:
            wide, at = (firsts[l][0], u) if u < 18 else (firsts[l][1], u - 18)
            return wide[:, 128 * at : 128 * at + 128]
        if group == 1:
            return ups[l][u // 3][:, 128 * (u % 3) : 128 * (u % 3) + 128]
        cb, q = divmod(u, 4)
        return downs[l][6 * q : 6 * q + 6, 128 * cb : 128 * cb + 128]

    plain = dense([get(*key, u) for key in PLAIN_IN for u in range(24)], 27)
    for d in range(8):
        pay[d, 0:27] = plain
        pay[d, 27:31] = dense([get(*key, 3 * d + i) for key in CUBE_IN for i in range(3)], 4)


def regroup_kernel(got, smalls, first, third, fourth):
    plain = [got[d, 0:27].astype(f32).reshape(432, 128) for d in range(8)]
    cube = [got[d, 27:31].astype(f32).reshape(64, 128) for d in range(8)]

    def join(rows, u):
        return jnp.concatenate([v[6 * u : 6 * u + 6] for v in rows], axis=0).astype(bf16).reshape(3, 16, 128)

    first[9] = smalls[...]
    for u in range(9):
        tile = 3 * u if u < 3 else 3 * u + 1
        first[tile : tile + 3] = join(cube, u)
    for u in range(24):
        third[3 * u : 3 * u + 3] = join(plain, u)
    for u in range(48):
        fourth[3 * u : 3 * u + 3] = join(plain, 24 + u)


def first_project_kernel(core, h_ref, mine, theirs, *refs):
    outs, (w, sem, buf, small_sem) = refs[:7], refs[7:]
    vecs = outs[2:]
    fetch(0, 0, core, (mine, theirs), w, sem, 0, 6)
    small_parameters(core, mine, theirs, vecs[:4], vecs[4], buf, small_sem)
    project(h_ref, vecs[0], outs[0], outs[1], w, sem)


def small_parameters(core_ref, mine, theirs, vecs, few, buf, sem):
    core = core_ref[0]

    def step(n, carry):
        for src, own in ((mine, core), (theirs, 1 - core)):
            row, triple = place(n, own)
            pltpu.make_async_copy(src.at[n, 9], buf.at[row * 8 + triple], sem).start()
        return carry

    lax.fori_loop(0, 64, step, 0)
    pltpu.make_async_copy(buf, buf, sem).wait()
    rows = buf[...].astype(f32)
    low_part, high_part = rows[:, 0], rows[:, 1]
    few[:, 0:128] = low_part
    few[:, 128:256] = high_part
    low_part = low_part.astype(bf16)
    value = lax.broadcasted_iota(jnp.int32, (128, 16), 0) - 6 * lax.broadcasted_iota(jnp.int32, (128, 16), 1)
    place_in = lax.broadcasted_iota(jnp.int32, (128, D), 1) - 6 * lax.broadcasted_iota(jnp.int32, (128, D), 0)
    total = jnp.zeros((16, D), f32)
    for i in range(6):
        picked = mul(low_part, (value == i).astype(f32).astype(bf16)).astype(bf16)
        total = total + t_mul(picked, (place_in == i).astype(f32).astype(bf16))
    for l in range(LAYERS):
        for k, i in enumerate((2 * l, 4 + 2 * l, 8 + 2 * l, 9 + 2 * l)):
            vecs[2 * l][k : k + 1] = total[i : i + 1]
        for k, i in enumerate((2 * l + 1, 5 + 2 * l, 12 + 2 * l, 13 + 2 * l)):
            vecs[2 * l + 1][k : k + 1] = total[i : i + 1]


def finish_kernel(parts, total, out, few):
    small = jnp.zeros((2, 128), f32)
    for k in range(8):
        small = small + parts[k, 9].astype(f32)[0:2]
    few[...] = small
    units_of = []
    for u in range(13):
        tile = 3 * u if u < 3 else 3 * u + 1
        rows = jnp.zeros((48, 128), f32)
        for k in range(8):
            rows = rows + parts[k, tile : tile + 3].reshape(48, 128).astype(f32)
        units_of.append(rows)
    for u in range(40):
        units_of.append(total[3 * u : 3 * u + 3].reshape(48, 128).astype(f32))
    for d in range(8):
        out[d] = dense([rows[6 * d : 6 * d + 6] for rows in units_of], 20)


def unpack_kernel(got, order, g_in, g_out, g_up, g_down):
    cube = [got[d, 0:5].reshape(80, 128).astype(f32) for d in range(8)]
    plain = got[0].reshape(320, 128).astype(f32)
    for d in range(1, 8):
        plain = plain + got[d].reshape(320, 128).astype(f32)
    stack = []
    for l in range(LAYERS):
        for group in range(3):
            rows = []
            for u in range(24):
                triple, k = out_place(l, group, u)
                rows.append((plain if triple is None else cube[triple])[6 * k : 6 * k + 6])
            if group == 0:
                g_in[:, l] = jnp.concatenate(rows[:18], axis=1)
                g_out[:, l] = jnp.concatenate(rows[18:], axis=1)
            elif group == 1:
                stack += [jnp.concatenate(rows[3 * m : 3 * m + 3], axis=1) for m in range(8)]
            else:
                for u in range(24):
                    cb, q = divmod(u, 4)
                    g_down[l, 6 * q : 6 * q + 6, 128 * cb : 128 * cb + 128] = rows[u]
    left = jnp.concatenate(stack, axis=0)
    terms = []
    for _ in range(3):
        terms.append(left.astype(bf16))
        left = left - terms[-1].astype(f32)
    wide = mul_t(jnp.concatenate(terms, axis=0), order[...])
    wide = wide[0:96] + wide[96:192] + wide[192:288]
    for l in range(LAYERS):
        for m in range(8):
            g_up[:, l, 384 * m : 384 * m + 384] = wide[48 * l + 6 * m : 48 * l + 6 * m + 6]


def call(kernel, outs, ins, scratch=(), us=3, out_spaces=None, aliases=None):
    spaces = {"s": pltpu.SMEM, "v": pltpu.VMEM, "a": pl.ANY}
    return pl.pallas_call(
        kernel,
        out_shape=[jax.ShapeDtypeStruct(*o) for o in outs],
        in_specs=[pl.BlockSpec(memory_space=spaces[m]) for _, m in ins],
        out_specs=[pl.BlockSpec(memory_space=spaces[m]) for m in (out_spaces or "v" * len(outs))],
        scratch_shapes=list(scratch),
        input_output_aliases=aliases or {},
        compiler_params=pltpu.CompilerParams(vmem_limit_bytes=56 * 1024 * 1024),
        cost_estimate=pl.CostEstimate(flops=0, bytes_accessed=us * 3690000, transcendentals=0),
    )(*[a for a, _ in ins])


def w_scratch(count):
    return pltpu.VMEM((16, 3 * count, 16, 128), bf16)


DMA = pltpu.SemaphoreType.DMA


def after(values, *others):
    return lax.optimization_barrier((values,) + others)[0] if others else values


def copies(values, groups, *others):
    many = after(jnp.broadcast_to(values[None], (8,) + values.shape), *others)
    return lax.all_to_all(many, ALL, 0, 0, axis_index_groups=groups)


def sum_first(values):
    return jnp.sum(values.astype(f32), axis=0)


def swap_core(values):
    return lax.ppermute(values, "c", [(0, 1), (1, 0)])


def cube_copies(shards, *others):
    return copies(shards, GROUPS_B, *others).reshape((64,) + shards.shape[1:])


def spread(shards):
    mine = cube_copies(shards)
    return mine, swap_core(mine)


def add_kernel(*refs):
    out, first = refs[-1], 0
    for keep, got in zip(refs[0:-1:2], refs[1:-1:2]):
        n = keep.shape[1]
        out[:, first : first + n] = (keep[...].astype(f32) + got[...].astype(f32)).astype(bf16)
        first += n


def add_pairs(pairs):
    total = sum(a.shape[1] for a, _ in pairs)
    flat = [v for pair in pairs for v in pair]

    def spec(t):
        return pl.BlockSpec((8, t, 16, 128), lambda i: (i, 0, 0, 0))

    return pl.pallas_call(
        add_kernel,
        grid=(8,),
        out_shape=jax.ShapeDtypeStruct((64, total, 16, 128), bf16),
        in_specs=[spec(v.shape[1]) for v in flat],
        out_specs=spec(total),
        compiler_params=pltpu.CompilerParams(vmem_limit_bytes=56 * 1024 * 1024),
        cost_estimate=pl.CostEstimate(flops=2**22, bytes_accessed=3 * 64 * total * 4096, transcendentals=0),
    )(*flat)


def core_sums(pairs):
    return add_pairs([(keep, swap_core(send)) for keep, send in pairs])


def to_cube(part):
    return lax.all_to_all(part.reshape((8, 8) + part.shape[1:]), ALL, 0, 0, axis_index_groups=GROUPS_B)


def token_ids(group_index, positions, sequence_group, sequence_start, sequence_length):
    member = (
        (sequence_group[None, :] == group_index)
        & (sequence_start[None, :] <= positions[:, None])
        & (positions[:, None] < (sequence_start + sequence_length)[None, :])
    )
    numbers = jnp.arange(sequence_group.shape[0], dtype=jnp.int32) + 1
    located = jnp.sum(jnp.where(member, numbers[None, :], 0), axis=1)
    return jnp.where(located > 0, located - 1, -1 - positions)


def body(hidden_in, out_grad, sequence_group, sequence_start, sequence_length, norm_gain, norm_bias,
         input_weight, input_bias, output_weight, branch_bias, up_weight, up_bias, down_weight):
    core = lax.axis_index("c").astype(jnp.int32).reshape(1)
    par = lax.axis_index("zl").astype(jnp.int32).reshape(1)
    positions = jnp.arange(SLOTS, dtype=jnp.int32)
    ids = token_ids(lax.axis_index(DATA), positions, sequence_group, sequence_start, sequence_length)
    idc, idr = ids.reshape(CTX_DEV, TOK, 1), ids.reshape(1, SLOTS)

    order = jnp.asarray(FF_ORDER, bf16)
    smalls = jnp.concatenate([v.reshape(-1) for v in (norm_gain, norm_bias, input_bias, branch_bias, up_bias)])
    smalls = jnp.pad(smalls, (0, 2048 - 144)).reshape(16, 128)
    (pay,) = call(pack_kernel, [((8, 31, 16, 128), bf16)],
                  [(jnp.swapaxes(v, 0, 1), "v") for v in (input_weight, output_weight, up_weight)]
                  + [(down_weight, "v"), (order, "v")])
    got = lax.all_to_all(pay, CTX, 0, 0)
    first, third, fourth = call(
        regroup_kernel,
        [((28, 16, 128), bf16), ((72, 16, 128), bf16), ((144, 16, 128), bf16)],
        [(got, "v"), (smalls, "v")])
    down_0 = lax.all_gather(third, DATA, axis=0, tiled=False)
    shards = copies(first, GROUPS_A)
    group_e, shards = spread(shards[:, :10]), shards[:, 10:]
    shards = jnp.broadcast_to(shards[None], (8,) + shards.shape)
    group_e = tuple(after(v, shards) for v in group_e)
    sources = {(0, 0): group_e, (0, 2): (down_0,)}

    a1, pay, *vecs, few = call(
        first_project_kernel,
        [((TOK, D), bf16), ((8, TOK, 384), bf16)] + [((4, D), f32)] * 4 + [((128, 256), f32)],
        [(core, "s"), (hidden_in[0], "v"), (group_e[0], "a"), (group_e[1], "a")],
        [w_scratch(18), DMA, pltpu.VMEM((128, 16, 128), bf16), DMA], us=7)
    ups = few[:, 96:144].reshape(16, 8, 2, 4, 6).transpose(2, 0, 3, 1, 4).reshape(2, 4 * D)

    def weights(l, all_groups):
        return [(w, "a") for group in range(3 if all_groups else 1) for w in sources[l, group]]

    def attend(heads):
        return call(attend_kernel, [((8, TOK, 128), bf16)],
                    [(par, "s"), (heads, "v"), (idc, "v"), (idr, "v")], us=6)[0]

    def attend_back(heads, cot):
        return call(attend_back_kernel, [((8, TOK, 384), bf16)],
                    [(par, "s"), (heads, "v"), (cot, "v"), (idc, "v"), (idr, "v")],
                    [pltpu.VMEM((2, SLOTS, 64), f32)] * 2, us=8)[0]

    def exchange(values):
        return lax.all_to_all(values, CTX, 0, 0)

    block_scratch = [w_scratch(6), w_scratch(24), w_scratch(24), DMA((3,))]
    project_scratch = [w_scratch(18), DMA]
    project_outs = [((TOK, D), bf16), ((8, TOK, 384), bf16)]
    forward_outs = [((TOK, D), bf16), ((TOK, D), f32), ((TOK, D), bf16), ((TOK, 4 * D), f32)]
    backward_outs = [((TOK, 4 * D), bf16), ((TOK, D), f32), ((8, TOK, 128), bf16), ((4, D), f32), ((1, 4 * D), f32)]
    back_project_outs = [((TOK, 3 * D), bf16), ((TOK, D), f32), ((4, D), f32)]

    hidden_0 = hidden_in[0]
    both_1 = lax.all_gather(after(fourth, a1), DATA, axis=0, tiled=False)
    sources[1, 1] = sources[1, 2] = (both_1,)
    a1 = [a1, None]
    heads_0 = exchange(pay)
    mine = lax.all_to_all(after(shards, heads_0, down_0), ALL, 0, 0, axis_index_groups=GROUPS_B)
    mine = mine.reshape((64,) + mine.shape[2:])
    mix = attend(heads_0)
    theirs = swap_core(after(mine, mix))
    sources[0, 1] = sources[1, 0] = (mine, theirs)
    back = exchange(after(mix, mine))
    o_0, h1_0, a2_0, u_0, hidden_1, a1[1], pay = call(
        forward_project_kernel,
        forward_outs + [((TOK, D), f32)] + project_outs,
        [(core, "s"), (hidden_0, "v"), (back, "v"), (vecs[1], "v"), (ups[0:1], "v"), (vecs[2], "v")]
        + weights(0, True) + weights(1, False),
        block_scratch + project_scratch, us=12)
    heads_1 = exchange(pay)
    back = exchange(attend(heads_1))
    def grad_joint(a1, g, o, e1):
        return call(
            grad_joint_cube, [((64, 9, 16, 128), bf16)] * 2,
            [(core, "s"), (a1, "v"), (g, "v"), (o, "v"), (e1, "v")],
            [pltpu.VMEM((2, 64, 9, 16, 128), bf16), DMA((2,))], us=5, out_spaces="aa")

    grad = out_grad[0]
    few_rows, few_up, joint = [None] * 2, [None] * 2, [None] * 2
    o_1, a2_1, hidden, f, du, e1, pay, small_b, few_up[1] = call(
        last_kernel,
        [((TOK, D), bf16), ((TOK, D), bf16), ((TOK, D), bf16), ((TOK, 4 * D), bf16)] + backward_outs,
        [(core, "s"), (hidden_1, "v"), (back, "v"), (vecs[3], "v"), (ups[1:2], "v"), (grad, "v")] + weights(1, True),
        [pltpu.VMEM((TOK, D), f32), pltpu.VMEM((TOK, 4 * D), f32)] + block_scratch, us=16)
    cot = exchange(pay)
    keep_u, send_u, mlp_1 = call(
        grad_mlp_split, [((64, 3, 16, 128), bf16)] * 2 + [((16, 120, 16, 128), bf16)],
        [(core, "s"), (f, "v"), (grad, "v"), (a2_1, "v"), (du, "v")],
        [pltpu.VMEM((2, 64, 3, 16, 128), bf16), w_scratch(40), DMA((3,))], us=9, out_spaces="aaa")
    scattered = lax.psum_scatter(after(mlp_1, cot), DATA, scatter_dimension=0, tiled=False)
    back = exchange(attend_back(heads_1, after(cot, mlp_1)))
    e1_1, small_b1 = e1, small_b
    g_1, grad, small_a1, f_0, du, e1, pay, small_b, few_up[0] = call(
        back_both_kernel, back_project_outs + [((TOK, 4 * D), bf16)] + backward_outs,
        [(core, "s"), (back, "v"), (e1_1, "v"), (hidden_1, "v"), (vecs[2], "v"), (u_0, "v"), (h1_0, "v"),
         (vecs[1], "v")] + weights(1, False) + weights(0, True),
        project_scratch + block_scratch, us=16)
    cot = exchange(pay)
    keep_ud, send_ud = call(
        grad_mlp_cube, [((64, 18, 16, 128), bf16)] * 2,
        [(core, "s"), (f_0, "v"), (grad, "v"), (a2_0, "v"), (du, "v")],
        [pltpu.VMEM((2, 64, 18, 16, 128), bf16), DMA((2,))], us=9, out_spaces="aa")
    send_ud = after(send_ud, cot)
    back = exchange(attend_back(heads_0, after(cot, keep_ud)))
    middle = core_sums([(keep_ud, send_ud), (keep_u, send_u)])
    g_0, grad, small_a0 = call(
        back_project_kernel, back_project_outs,
        [(core, "s"), (after(back, middle), "v"), (e1, "v"), (hidden_0, "v"), (vecs[0], "v")] + weights(0, False),
        project_scratch, us=6)
    joint = [grad_joint(a1[0], g_0, o_0, e1), grad_joint(a1[1], g_1, o_1, e1_1)]
    for l, (first, second) in enumerate(((small_a0, small_b), (small_a1, small_b1))):
        few_rows[l] = jnp.concatenate([first[0:1], second[0:1], first[1:2], second[1:2], first[2:4], second[2:4]], axis=0)

    few = jnp.concatenate([r.reshape(8, 128, 6).transpose(1, 0, 2).reshape(128, 48) for r in few_rows]
                          + [r.reshape(16, 4, 8, 6).transpose(0, 2, 1, 3).reshape(128, 24) for r in few_up], axis=1)
    few = jnp.pad(few, ((0, 0), (0, 256 - 144))).astype(bf16)
    few = jnp.dot(jnp.asarray(TAIL_ORDER.T, bf16), few, preferred_element_type=f32).astype(bf16)
    few = jnp.pad(few.reshape(2, 64, 1, 2, 128), ((0, 0),) * 3 + ((0, 14), (0, 0)))
    few = [jnp.where(core[0] == k, few[0], few[1]) for k in range(2)]

    middle = to_cube(middle)
    last = to_cube(after(core_sums([joint[0], few, joint[1]]), middle, scattered))
    sums = jnp.concatenate([sum_first(last).astype(bf16), sum_first(middle).astype(bf16)], axis=1)
    sums = lax.all_to_all(sums, ALL, 0, 0, axis_index_groups=GROUPS_A)
    sums, few = call(finish_kernel, [((8, 20, 16, 128), bf16), ((2, 128), f32)],
                     [(sums, "v"), (scattered, "v")])
    got = lax.all_to_all(sums, CTX, 0, 0)
    grad_in, grad_out, grad_up, grad_down = call(
        unpack_kernel,
        [((6, 2, 3 * D), f32), ((6, 2, D), f32), ((6, 2, 4 * D), f32), ((2, 24, D), f32)],
        [(got, "v"), (order, "v")])
    few = few.reshape(256)
    few_l = [few[48 * l : 48 * l + 48].reshape(4, 2, 6) for l in range(2)]

    def pair(k):
        return jnp.stack([few_l[0][k], few_l[1][k]])

    return (
        hidden[None],
        grad[None],
        pair(0),
        pair(1),
        jnp.swapaxes(grad_in, 0, 1),
        pair(2),
        jnp.swapaxes(grad_out, 0, 1),
        pair(3),
        jnp.swapaxes(grad_up, 0, 1),
        few[96:144].reshape(2, 24),
        grad_down,
    )


def solution(mesh):
    mesh = Mesh(mesh.devices.reshape(4, 2, 2, 4, 2), ALL)
    token = P(DATA, CTX, None)
    one = P(None, ALL)
    two = P(None, None, ALL)
    mat = P(None, ALL, None)
    return jax.shard_map(
        body,
        mesh=mesh,
        in_specs=(token, token, P(), P(), P(), two, two, mat, two, mat, two, mat, one, mat),
        out_specs=(token, token, two, two, mat, two, mat, two, mat, one, mat),
        check_vma=False,
    )
```
